32 devices in a mesh: fsdp: 2 (over core), ctx: 8 (over z, x), tp: 2 (over y).
Axes of the slice: x: 2, y: 2, z: 4, core: 2. Of those that a mesh axis runs over, the one named last changes fastest.
Arguments:
- tokens: bfloat16 [4096, 2048], P(('fsdp', 'ctx')), may hold values from -6 to 6
- cotangent: bfloat16 [4096, 2048], P(('fsdp', 'ctx')), may hold values from -6 to 6
- token_order: int32 [2, 2048], P('fsdp'), may hold values from 0 to 2047, each once within a row
- seq_lengths: int32 [2, 3], P('fsdp'), may hold values from 1 to 1024, 2048 in all within a row
- rel_buckets: int32 [2047], replicated, may hold values from 0 to 31, as said below
- gain_attn: bfloat16 [2048], P('fsdp'), may hold values from 0.5 to 1.5
- w_query: bfloat16 [2048, 2048], P('fsdp', 'tp'), may hold values from -1 to 1
- w_key: bfloat16 [2048, 2048], P('fsdp', 'tp'), may hold values from -0.125 to 0.125
- w_value: bfloat16 [2048, 2048], P('fsdp', 'tp'), may hold values from -0.125 to 0.125
- w_out: bfloat16 [2048, 2048], P('tp', 'fsdp'), may hold values from -0.75 to 0.75
- rel_bias: bfloat16 [32, 32], P('fsdp', 'tp'), may hold values from -4 to 4
- gain_ffn: bfloat16 [2048], P('fsdp'), may hold values from 0.5 to 1.5
- w_gate: bfloat16 [2048, 5120], P('fsdp', 'tp'), may hold values from -0.125 to 0.125
- w_up: bfloat16 [2048, 5120], P('fsdp', 'tp'), may hold values from -0.125 to 0.125
- w_down: bfloat16 [5120, 2048], P('tp', 'fsdp'), may hold values from -0.125 to 0.125
Outputs:
- output: bfloat16 [4096, 2048], P(('fsdp', 'ctx'))
- grad_tokens: float32 [4096, 2048], P(('fsdp', 'ctx'))
- grad_gain_attn: float32 [2048], P('fsdp')
- grad_query: float32 [2048, 2048], P('fsdp', 'tp')
- grad_key: float32 [2048, 2048], P('fsdp', 'tp')
- grad_value: float32 [2048, 2048], P('fsdp', 'tp')
- grad_out: float32 [2048, 2048], P('tp', 'fsdp')
- grad_bias: float32 [32, 32], P('fsdp', 'tp')
- grad_gain_ffn: float32 [2048], P('fsdp')
- grad_gate: float32 [2048, 5120], P('fsdp', 'tp')
- grad_up: float32 [2048, 5120], P('fsdp', 'tp')
- grad_down: float32 [5120, 2048], P('tp', 'fsdp')
- head_maxima: float32 [32], P('tp')
- query_clipped: bfloat16 [2048, 2048], P('fsdp', 'tp')
- key_clipped: bfloat16 [2048, 2048], P('fsdp', 'tp')
The draws below stay inside these ranges and needn't reach their ends.
Inputs may be any that keep to these rules, and one draw needn't show every extreme that they name: `token_order`: each row names every position 0 to 2047 once. `seq_lengths`: each row holds 3 lengths that sum to 2048; the largest is 1024. `rel_buckets`: for relative position r: |r| for |r| < 8, else 8 to 15 and non-decreasing in |r|; plus 16 when r > 0.
All inputs are finite; a program needn't handle non-finite values.
Results may differ from the reference program's by a relative error of at most 0.025.
Values may be sent and summed in bfloat16 or wider, within the bound.
A program may use at most 256 MiB of HBM per device.

```python
import math
import jax
import jax.numpy as jnp
import numpy as np
from jax import lax

D = 2048
H = 32
DH = 64
FF = 5120
NB = 32
SEQS = 3
TOK_DEV = 256
GROUP = 2048
TOKENS = 4096
LONGEST = 1024
N_FSDP = 2
N_CTX = 8
N_TP = 2


def draw_w_query(key, part):
    scale_key, entry_key = jax.random.split(key)
    head_scale = jnp.exp(jax.random.uniform(scale_key, (H,), jnp.float32, math.log(0.5), math.log(2.5)))
    entries = jax.random.normal(entry_key, (D, H, DH), jnp.float32)
    values = entries * head_scale[None, :, None] / math.sqrt(D * DH)
    return values.reshape(D, H * DH).astype(jnp.bfloat16)


def draw_rel_buckets(key, part):
    level_keys = jax.random.split(key, 7)
    gap_sizes = jnp.stack([jax.random.randint(level_keys[level_idx], (), 1 << level_idx, (2 << level_idx) + 1, jnp.int32) for level_idx in range(7)])
    bounds = (8 + jnp.cumsum(gap_sizes)).astype(jnp.int32)
    offsets = jnp.arange(2 * LONGEST - 1, dtype=jnp.int32) - (LONGEST - 1)
    distance = jnp.abs(offsets)
    far_bucket = 8 + jnp.sum((distance[:, None] >= bounds[None, :]).astype(jnp.int32), axis=1)
    bucket = jnp.where(distance < 8, distance, far_bucket)
    return (bucket + 16 * (offsets > 0).astype(jnp.int32)).astype(jnp.int32)


def block_scale(stream_key, dims, cuts, least, top_value):
    factor_of, own = 1.0, jax.random.fold_in(stream_key, 6)
    for dim, parts in cuts:
        steps = jnp.exp(jax.random.uniform(jax.random.fold_in(own, dim), (parts,), jnp.float32, least / len(cuts), top_value / len(cuts)))
        factor_of = factor_of * jnp.repeat(steps, dims[dim] // parts).reshape([-1 if axis == dim else 1 for axis in range(len(dims))])
    return factor_of


def profile(count, total, bound, skew):
    loads = [(1 << 20) // math.isqrt(grade ** skew) + 1 for grade in range(2, count + 1)]
    rest, counts = total - bound - (count - 1), [1] * (count - 1)
    while rest > 0:
        free = [i for i in range(count - 1) if counts[i] < bound]
        whole, remaining = sum([loads[i] for i in free]), rest
        for i in free:
            extra = min(bound - counts[i], max(1, remaining * loads[i] // whole), rest)
            counts[i] = counts[i] + extra
            rest = rest - extra
    return np.array([bound] + counts)


def ragged_sizes(key, amount, total, limit, slope):
    if amount == 2:
        one = jax.random.randint(key, (), max(1, total - limit), min(limit, total - 1) + 1)
        return jnp.stack([one, total - one])
    tallies = jnp.asarray(profile(amount, total, limit, slope), jnp.int32)
    pairs = (amount - 1) // 2
    source_of, receiver = tallies[1:1 + 2 * pairs:2], tallies[2:2 + 2 * pairs:2]
    margin = jnp.minimum(source_of - 1, limit - receiver)
    moved = jax.random.randint(jax.random.fold_in(key, 1), (pairs,), 0, 1 << 20) % (margin + 1)
    tallies = tallies.at[1:1 + 2 * pairs:2].set(source_of - moved).at[2:2 + 2 * pairs:2].set(receiver + moved)
    return tallies[jax.random.permutation(jax.random.fold_in(key, 2), amount)]


def noise(stream_key, shape, width, limit, cuts=(), held_as=jnp.bfloat16):
    values = width * jax.random.normal(stream_key, shape, jnp.float32)
    if cuts:
        values = values * block_scale(stream_key, shape, cuts, -0.22, 0.18)
    return jnp.clip(values, -limit, limit).astype(held_as)


def setup_inputs(seed: int = 0) -> dict:
    streams_of = jax.random.split(jax.random.key(seed), 16)
    return {
        "tokens": noise(streams_of[0], (TOKENS, D), 1.0, 6.0, ((0, 16),)),
        "cotangent": noise(streams_of[1], (TOKENS, D), 1.0, 6.0, ((0, 16),)),
        "token_order": jax.vmap(lambda own: jax.random.permutation(own, GROUP))(jax.random.split(streams_of[2], N_FSDP)).reshape((N_FSDP, GROUP)).astype(jnp.int32),
        "seq_lengths": jax.vmap(lambda own: ragged_sizes(own, SEQS, GROUP, LONGEST, 2))(jax.random.split(streams_of[3], N_FSDP)).reshape((N_FSDP, SEQS)).astype(jnp.int32),
        "rel_buckets": draw_rel_buckets(jax.random.fold_in(streams_of[15], 71), 0),
        "gain_attn": jnp.clip(1.0 + 0.1 * jax.random.normal(streams_of[5], (D,), jnp.float32), 0.5, 1.5).astype(jnp.bfloat16),
        "w_query": draw_w_query(jax.random.fold_in(streams_of[15], 71), 0),
        "w_key": noise(streams_of[7], (D, H * DH), D ** -0.5, 0.125, ((0, 2), (1, 2))),
        "w_value": noise(streams_of[8], (D, H * DH), D ** -0.5, 0.125, ((0, 2), (1, 2))),
        "w_out": noise(streams_of[9], (H * DH, D), (D // 32) ** -0.5, 0.75, ((0, 2), (1, 2))),
        "rel_bias": noise(streams_of[10], (NB, H), 1.0, 4.0, ((0, 2), (1, 2))),
        "gain_ffn": jnp.clip(1.0 + 0.1 * jax.random.normal(streams_of[11], (D,), jnp.float32), 0.5, 1.5).astype(jnp.bfloat16),
        "w_gate": noise(streams_of[12], (D, FF), D ** -0.5, 0.125, ((0, 2), (1, 2))),
        "w_up": noise(streams_of[13], (D, FF), D ** -0.5, 0.125, ((0, 2), (1, 2))),
        "w_down": noise(streams_of[14], (FF, D), (FF // 2) ** -0.5, 0.125, ((0, 2), (1, 2))),
    }


EPS = 1e-06
TAU_CLIP = 6.0
HIGH = lax.Precision.HIGHEST

@jax.custom_vjp
def low(v):
    return lax.optimization_barrier(v.astype(jnp.bfloat16)).astype(jnp.float32)

@jax.custom_vjp
def low_back(v):
    return v

def low_keep(v):
    return (low(v), None)

def low_pass(kept, grad):
    return (grad,)

def back_keep(v):
    return (v, None)

def back_low(kept, grad):
    return (low(grad),)
low.defvjp(low_keep, low_pass)
low_back.defvjp(back_keep, back_low)

def rms_norm(values, gain):
    return values * lax.rsqrt(lax.optimization_barrier(jnp.mean(values * values, axis=-1, keepdims=True)) + EPS) * gain

def segment_of(positions, lengths_row):
    offsets = (jnp.cumsum(lengths_row) - lengths_row).astype(jnp.int32)
    counted = lax.optimization_barrier(jnp.sum((positions[:, None] >= offsets[None, :]).astype(jnp.int32), axis=1))
    return (counted - 1).astype(jnp.int32)

def attend_block(query_blk, query_pos, query_seg, key_group, value_group, key_pos, key_seg, bias_table, rel_buckets):
    raw_scores = jnp.einsum('qhd,khd->hqk', query_blk, key_group, precision=HIGH)
    offset = jnp.clip(key_pos[None, :] - query_pos[:, None] + LONGEST - 1, 0, 2 * LONGEST - 2).astype(jnp.int32)
    pair_bucket = jnp.take(rel_buckets, offset)
    pair_bias = jnp.transpose(jnp.take(bias_table, pair_bucket, axis=0), (2, 0, 1))
    same_seq = (query_seg[:, None] == key_seg[None, :])[None]
    scores = low_back(raw_scores + pair_bias)
    weights = jnp.where(same_seq, jnp.exp(scores), jnp.float32(0.0))
    totals = lax.optimization_barrier(jnp.sum(weights, axis=2))
    summed = low_back(jnp.einsum('hqk,khd->qhd', low(weights), value_group, precision=HIGH))
    context = summed / jnp.transpose(totals)[:, :, None]
    head_top = lax.optimization_barrier(jnp.max(jnp.where(same_seq, raw_scores, jnp.float32(-1e+30)), axis=(1, 2)))
    return (context, head_top)

def reference(tokens, cotangent, token_order, seq_lengths, rel_buckets, gain_attn, w_query, w_key, w_value, w_out, rel_bias, gain_ffn, w_gate, w_up, w_down):
    group_rows = TOK_DEV * N_CTX
    query_rows = min(256, group_rows)
    head_cols = H * DH // N_TP
    hidden_cols = FF // N_TP
    segments = [segment_of(token_order[group_idx], seq_lengths[group_idx]) for group_idx in range(N_FSDP)]

    def forward(f_tokens, f_gain_a, f_query, f_key, f_value, f_out, f_bias, f_gain_f, f_gate, f_up, f_down):
        normed = low(rms_norm(f_tokens, f_gain_a))
        queries = low_back(low(jnp.dot(normed, f_query, precision=HIGH)))
        keys_all = low_back(low(jnp.dot(normed, f_key, precision=HIGH)))
        values_all = low_back(low(jnp.dot(normed, f_value, precision=HIGH)))
        contexts = []
        head_tops = []
        for group_idx in range(N_FSDP):
            start_row = group_idx * group_rows
            group_q = queries[start_row:start_row + group_rows].reshape(group_rows // query_rows, query_rows, H, DH)
            group_k = keys_all[start_row:start_row + group_rows].reshape(group_rows, H, DH)
            group_v = values_all[start_row:start_row + group_rows].reshape(group_rows, H, DH)
            positions = token_order[group_idx]
            seq_ids = segments[group_idx]

            def one_block(block_items, group_k=group_k, group_v=group_v, positions=positions, seq_ids=seq_ids):
                return attend_block(block_items[0], block_items[1], block_items[2], group_k, group_v, positions, seq_ids, f_bias, rel_buckets)
            block_ctx, block_top = lax.map(jax.checkpoint(one_block), (group_q, positions.reshape(-1, query_rows), seq_ids.reshape(-1, query_rows)))
            contexts.append(block_ctx.reshape(group_rows, H * DH))
            head_tops.append(lax.optimization_barrier(jnp.max(block_top, axis=0)))
        context = low(jnp.concatenate(contexts, axis=0))
        attn_out = jnp.zeros_like(f_tokens)
        for part_idx in range(N_TP):
            columns = slice(part_idx * head_cols, (part_idx + 1) * head_cols)
            attn_out = attn_out + low(jnp.dot(context[:, columns], f_out[columns], precision=HIGH))
        attn_out = low_back(attn_out)
        hidden_state = f_tokens + attn_out
        normed_ffn = low(rms_norm(hidden_state, f_gain_f))
        gate_pre = low_back(jnp.dot(normed_ffn, f_gate, precision=HIGH))
        up_pre = low_back(jnp.dot(normed_ffn, f_up, precision=HIGH))
        inner_act = low(jax.nn.gelu(gate_pre, approximate=True) * up_pre)
        ffn_out = jnp.zeros_like(f_tokens)
        for part_idx in range(N_TP):
            columns = slice(part_idx * hidden_cols, (part_idx + 1) * hidden_cols)
            ffn_out = ffn_out + low(jnp.dot(inner_act[:, columns], f_down[columns], precision=HIGH))
        return (hidden_state + ffn_out, lax.optimization_barrier(jnp.max(jnp.stack(head_tops), axis=0)))
    floats = tuple((array_in.astype(jnp.float32) for array_in in (tokens, gain_attn, w_query, w_key, w_value, w_out, rel_bias, gain_ffn, w_gate, w_up, w_down)))
    result, pullback, head_maxima = jax.vjp(forward, *floats, has_aux=True)
    gradients = pullback(cotangent.astype(jnp.float32))
    clip_scale = TAU_CLIP / jnp.maximum(head_maxima, TAU_CLIP)
    column_scale = jnp.repeat(jnp.sqrt(clip_scale), DH)
    query_clipped = (floats[2] * column_scale[None, :]).astype(jnp.bfloat16)
    key_clipped = (floats[3] * column_scale[None, :]).astype(jnp.bfloat16)
    return (result.astype(jnp.bfloat16), gradients[0], gradients[1], gradients[2], gradients[3], gradients[4], gradients[5], gradients[6], gradients[7], gradients[8], gradients[9], gradients[10], head_maxima, query_clipped, key_clipped)
```

```python
import jax
import jax.numpy as jnp
from jax import lax
from jax.sharding import PartitionSpec as P

DH = 64
NB = 32


EPS = 1e-06
TAU_CLIP = 6.0


def rms_norm(values, gain):
    return values * lax.rsqrt(jnp.mean(values * values, axis=-1, keepdims=True) + EPS) * gain


def geglu(gate_pre, up_pre):
    return jax.nn.gelu(gate_pre, approximate=True) * up_pre


def segment_of(positions, lengths_row):
    offsets = jnp.cumsum(lengths_row) - lengths_row
    return jnp.sum((positions[:, None] >= offsets[None, :]).astype(jnp.int32), axis=1) - 1


def bucket_ranges(rel_buckets):
    table_len = rel_buckets.shape[0]
    index_all = jnp.arange(table_len, dtype=jnp.int32)
    bucket_ids = jnp.arange(NB, dtype=jnp.int32)
    matched = rel_buckets[:, None] == bucket_ids[None, :]
    range_first = jnp.min(jnp.where(matched, index_all[:, None], table_len), axis=0)
    range_last = jnp.max(jnp.where(matched, index_all[:, None], -1), axis=0)
    return (range_first, range_last, table_len)


def pair_terms(query_pos, query_seg, key_pos, key_seg, ranges, bias_table):
    range_first, range_last, table_len = ranges
    longest = (table_len + 1) // 2
    offset = jnp.clip(key_pos[None, :] - query_pos[:, None] + longest - 1, 0, 2 * longest - 2)
    inside = (offset[None, :, :] >= range_first[:, None, None]) & (
        offset[None, :, :] <= range_last[:, None, None]
    )
    bucket_hot = inside.astype(jnp.bfloat16)
    pair_bias = jnp.einsum(
        "btk,bh->htk", bucket_hot, bias_table, preferred_element_type=jnp.float32
    )
    same_seq = (query_seg[:, None] == key_seg[None, :])[None]
    return (bucket_hot, pair_bias, same_seq)


def per_device_generic(
    tokens,
    cotangent,
    token_order,
    seq_lengths,
    rel_buckets,
    gain_attn,
    w_query,
    w_key,
    w_value,
    w_out,
    rel_bias,
    gain_ffn,
    w_gate,
    w_up,
    w_down,
):
    local_rows = tokens.shape[0]
    head_count = w_query.shape[1] // DH
    group_rows = local_rows * lax.axis_size("ctx")
    key_block = min(512, group_rows)
    block_count = group_rows // key_block
    ranges = bucket_ranges(rel_buckets)
    gain_a, full_query, full_key, full_value, full_out, bias_local = (
        lax.all_gather(gain_attn, "fsdp", axis=0, tiled=True),
        lax.all_gather(w_query, "fsdp", axis=0, tiled=True),
        lax.all_gather(w_key, "fsdp", axis=0, tiled=True),
        lax.all_gather(w_value, "fsdp", axis=0, tiled=True),
        lax.all_gather(w_out, "fsdp", axis=1, tiled=True),
        lax.all_gather(rel_bias, "fsdp", axis=0, tiled=True),
    )
    tokens_f = tokens.astype(jnp.float32)
    gain_a32 = gain_a.astype(jnp.float32)
    normed = rms_norm(tokens_f, gain_a32).astype(jnp.bfloat16)
    queries = jnp.dot(normed, full_query, preferred_element_type=jnp.float32).astype(jnp.bfloat16)
    keys_here = jnp.dot(normed, full_key, preferred_element_type=jnp.float32).astype(jnp.bfloat16)
    values_here = jnp.dot(normed, full_value, preferred_element_type=jnp.float32).astype(
        jnp.bfloat16
    )
    order_row = token_order[0]
    seq_ids = segment_of(order_row, seq_lengths[0])
    row_start = lax.axis_index("ctx") * local_rows
    query_pos = lax.dynamic_slice_in_dim(order_row, row_start, local_rows)
    query_seg = lax.dynamic_slice_in_dim(seq_ids, row_start, local_rows)
    pos_blocks = order_row.reshape(block_count, key_block)
    seg_blocks = seq_ids.reshape(block_count, key_block)
    query_heads = queries.reshape(local_rows, head_count, DH)
    key_all, value_all = (
        lax.all_gather(keys_here, "ctx", axis=0, tiled=True),
        lax.all_gather(values_here, "ctx", axis=0, tiled=True),
    )

    def blocked(array_in):
        return array_in.reshape(block_count, key_block, head_count, DH)

    def forward_block(running, inputs):
        summed, totals, head_top = running
        key_blk, value_blk, pos_blk, seg_blk = inputs
        raw_scores = jnp.einsum(
            "thd,khd->htk", query_heads, key_blk, preferred_element_type=jnp.float32
        )
        bucket_hot, pair_bias, same_seq = pair_terms(
            query_pos, query_seg, pos_blk, seg_blk, ranges, bias_local
        )
        weights = jnp.where(same_seq, jnp.exp(raw_scores + pair_bias), 0.0)
        totals = totals + jnp.sum(weights, axis=2)
        summed = summed + jnp.einsum(
            "htk,khd->thd",
            weights.astype(jnp.bfloat16),
            value_blk,
            preferred_element_type=jnp.float32,
        )
        head_top = jnp.maximum(
            head_top, jnp.max(jnp.where(same_seq, raw_scores, -1e30), axis=(1, 2))
        )
        return ((summed, totals, head_top), None)

    start_state = (
        jnp.zeros((local_rows, head_count, DH), jnp.float32),
        jnp.zeros((head_count, local_rows), jnp.float32),
        jnp.full((head_count,), -1e30, jnp.float32),
    )
    (summed, totals, head_top), unused = lax.scan(
        forward_block, start_state, (blocked(key_all), blocked(value_all), pos_blocks, seg_blocks)
    )
    row_totals = jnp.transpose(totals)[:, :, None]
    context_exact = summed / row_totals
    context = context_exact.reshape(local_rows, head_count * DH).astype(jnp.bfloat16)
    head_maxima = lax.pmax(head_top, ("fsdp", "ctx"))
    attn_out = lax.psum(
        jnp.dot(context, full_out, preferred_element_type=jnp.float32).astype(jnp.bfloat16), "tp"
    ).astype(jnp.float32)
    hidden_state = tokens_f + attn_out
    gain_f, full_gate, full_up, full_down = (
        lax.all_gather(gain_ffn, "fsdp", axis=0, tiled=True),
        lax.all_gather(w_gate, "fsdp", axis=0, tiled=True),
        lax.all_gather(w_up, "fsdp", axis=0, tiled=True),
        lax.all_gather(w_down, "fsdp", axis=1, tiled=True),
    )
    gain_f32 = gain_f.astype(jnp.float32)
    normed_ffn = rms_norm(hidden_state, gain_f32).astype(jnp.bfloat16)
    gate_pre = jnp.dot(normed_ffn, full_gate, preferred_element_type=jnp.float32)
    up_pre = jnp.dot(normed_ffn, full_up, preferred_element_type=jnp.float32)
    inner_act = geglu(gate_pre, up_pre).astype(jnp.bfloat16)
    ffn_out = lax.psum(
        jnp.dot(inner_act, full_down, preferred_element_type=jnp.float32).astype(jnp.bfloat16), "tp"
    ).astype(jnp.float32)
    output = (hidden_state + ffn_out).astype(jnp.bfloat16)
    grad_down = jnp.einsum("tf,td->fd", inner_act, cotangent, preferred_element_type=jnp.float32)
    inner_grad = jnp.einsum("td,fd->tf", cotangent, full_down, preferred_element_type=jnp.float32)
    unused, geglu_back = jax.vjp(geglu, gate_pre, up_pre)
    gate_grad, up_grad = geglu_back(inner_grad)
    gate_grad = gate_grad.astype(jnp.bfloat16)
    up_grad = up_grad.astype(jnp.bfloat16)
    grad_gate = jnp.einsum("tc,tf->cf", normed_ffn, gate_grad, preferred_element_type=jnp.float32)
    grad_up = jnp.einsum("tc,tf->cf", normed_ffn, up_grad, preferred_element_type=jnp.float32)
    ffn_term = jnp.einsum(
        "tf,cf->tc", gate_grad, full_gate, preferred_element_type=jnp.float32
    ) + jnp.einsum("tf,cf->tc", up_grad, full_up, preferred_element_type=jnp.float32)
    normed_ffn_grad = lax.psum(ffn_term.astype(jnp.bfloat16), "tp").astype(jnp.float32)
    unused, norm_ffn_back = jax.vjp(rms_norm, hidden_state, gain_f32)
    hidden_norm_grad, grad_gain_ffn = norm_ffn_back(normed_ffn_grad)
    hidden_grad = cotangent.astype(jnp.float32) + hidden_norm_grad
    attn_grad = hidden_grad.astype(jnp.bfloat16)
    grad_out = jnp.einsum("tc,td->cd", context, attn_grad, preferred_element_type=jnp.float32)
    context_grad = jnp.einsum(
        "td,cd->tc", attn_grad, full_out, preferred_element_type=jnp.float32
    ).reshape(local_rows, head_count, DH)
    summed_grad = (context_grad / row_totals).astype(jnp.bfloat16)
    total_grad = jnp.transpose(-jnp.sum(context_grad * context_exact, axis=2) / row_totals[:, :, 0])
    key_back, value_back = (key_all, value_all)

    def backward_block(running, inputs):
        query_acc, bias_acc = running
        key_blk, value_blk, pos_blk, seg_blk = inputs
        raw_scores = jnp.einsum(
            "thd,khd->htk", query_heads, key_blk, preferred_element_type=jnp.float32
        )
        bucket_hot, pair_bias, same_seq = pair_terms(
            query_pos, query_seg, pos_blk, seg_blk, ranges, bias_local
        )
        weights = jnp.where(same_seq, jnp.exp(raw_scores + pair_bias), 0.0)
        prob_grad = (
            jnp.einsum("thd,khd->htk", summed_grad, value_blk, preferred_element_type=jnp.float32)
            + total_grad[:, :, None]
        )
        score_grad = (weights * prob_grad).astype(jnp.bfloat16)
        query_acc = query_acc + jnp.einsum(
            "htk,khd->thd", score_grad, key_blk, preferred_element_type=jnp.float32
        )
        key_grad = jnp.einsum(
            "htk,thd->khd", score_grad, query_heads, preferred_element_type=jnp.float32
        )
        value_grad = jnp.einsum(
            "htk,thd->khd",
            weights.astype(jnp.bfloat16),
            summed_grad,
            preferred_element_type=jnp.float32,
        )
        bucket_sums = jnp.einsum(
            "htk,btk->hb", score_grad, bucket_hot, preferred_element_type=jnp.float32
        )
        return ((query_acc, bias_acc + bucket_sums), (key_grad, value_grad))

    zero_state = (
        jnp.zeros((local_rows, head_count, DH), jnp.float32),
        jnp.zeros((head_count, NB), jnp.float32),
    )
    (query_acc, bias_acc), (key_grads, value_grads) = lax.scan(
        backward_block, zero_state, (blocked(key_back), blocked(value_back), pos_blocks, seg_blocks)
    )
    key_grad_all, value_grad_all = (
        lax.psum_scatter(
            key_grads.reshape(group_rows, head_count * DH).astype(jnp.bfloat16),
            "ctx",
            scatter_dimension=0,
            tiled=True,
        ).astype(jnp.float32),
        lax.psum_scatter(
            value_grads.reshape(group_rows, head_count * DH).astype(jnp.bfloat16),
            "ctx",
            scatter_dimension=0,
            tiled=True,
        ).astype(jnp.float32),
    )
    query_grad = query_acc.reshape(local_rows, head_count * DH).astype(jnp.bfloat16)
    key_grad = key_grad_all.astype(jnp.bfloat16)
    value_grad = value_grad_all.astype(jnp.bfloat16)
    attn_term = jnp.einsum("tc,dc->td", query_grad, full_query, preferred_element_type=jnp.float32)
    attn_term = attn_term + jnp.einsum(
        "tc,dc->td", key_grad, full_key, preferred_element_type=jnp.float32
    )
    attn_term = attn_term + jnp.einsum(
        "tc,dc->td", value_grad, full_value, preferred_element_type=jnp.float32
    )
    normed_grad = lax.psum(attn_term.astype(jnp.bfloat16), "tp").astype(jnp.float32)
    unused, norm_attn_back = jax.vjp(rms_norm, tokens_f, gain_a32)
    token_norm_grad, grad_gain_attn = norm_attn_back(normed_grad)
    grad_tokens = hidden_grad + token_norm_grad
    grad_query = jnp.einsum("td,tc->dc", normed, query_grad, preferred_element_type=jnp.float32)
    grad_key = jnp.einsum("td,tc->dc", normed, key_grad, preferred_element_type=jnp.float32)
    grad_value = jnp.einsum("td,tc->dc", normed, value_grad, preferred_element_type=jnp.float32)
    grad_bias = jnp.transpose(bias_acc)
    (
        share_gain_a,
        share_query,
        share_key,
        share_value,
        share_out,
        share_bias,
        share_gain_f,
        share_gate,
        share_up,
        share_down,
    ) = (
        lax.psum_scatter(
            grad_gain_attn.astype(jnp.bfloat16), "fsdp", scatter_dimension=0, tiled=True
        ).astype(jnp.float32),
        lax.psum_scatter(
            grad_query.astype(jnp.bfloat16), "fsdp", scatter_dimension=0, tiled=True
        ).astype(jnp.float32),
        lax.psum_scatter(
            grad_key.astype(jnp.bfloat16), "fsdp", scatter_dimension=0, tiled=True
        ).astype(jnp.float32),
        lax.psum_scatter(
            grad_value.astype(jnp.bfloat16), "fsdp", scatter_dimension=0, tiled=True
        ).astype(jnp.float32),
        lax.psum_scatter(
            grad_out.astype(jnp.bfloat16), "fsdp", scatter_dimension=1, tiled=True
        ).astype(jnp.float32),
        lax.psum_scatter(
            grad_bias.astype(jnp.bfloat16), "fsdp", scatter_dimension=0, tiled=True
        ).astype(jnp.float32),
        lax.psum_scatter(
            grad_gain_ffn.astype(jnp.bfloat16), "fsdp", scatter_dimension=0, tiled=True
        ).astype(jnp.float32),
        lax.psum_scatter(
            grad_gate.astype(jnp.bfloat16), "fsdp", scatter_dimension=0, tiled=True
        ).astype(jnp.float32),
        lax.psum_scatter(
            grad_up.astype(jnp.bfloat16), "fsdp", scatter_dimension=0, tiled=True
        ).astype(jnp.float32),
        lax.psum_scatter(
            grad_down.astype(jnp.bfloat16), "fsdp", scatter_dimension=1, tiled=True
        ).astype(jnp.float32),
    )
    (
        final_gain_a,
        final_query,
        final_key,
        final_value,
        final_out,
        final_bias,
        final_gain_f,
        final_gate,
        final_up,
        final_down,
    ) = (
        lax.psum(share_gain_a.astype(jnp.bfloat16), "ctx").astype(jnp.float32),
        lax.psum(share_query.astype(jnp.bfloat16), "ctx").astype(jnp.float32),
        lax.psum(share_key.astype(jnp.bfloat16), "ctx").astype(jnp.float32),
        lax.psum(share_value.astype(jnp.bfloat16), "ctx").astype(jnp.float32),
        lax.psum(share_out.astype(jnp.bfloat16), "ctx").astype(jnp.float32),
        lax.psum(share_bias.astype(jnp.bfloat16), "ctx").astype(jnp.float32),
        lax.psum(share_gain_f.astype(jnp.bfloat16), "ctx").astype(jnp.float32),
        lax.psum(share_gate.astype(jnp.bfloat16), "ctx").astype(jnp.float32),
        lax.psum(share_up.astype(jnp.bfloat16), "ctx").astype(jnp.float32),
        lax.psum(share_down.astype(jnp.bfloat16), "ctx").astype(jnp.float32),
    )
    clip_scale = TAU_CLIP / jnp.maximum(head_maxima, TAU_CLIP)
    column_scale = jnp.repeat(jnp.sqrt(clip_scale), DH)
    query_clipped = (w_query.astype(jnp.float32) * column_scale[None, :]).astype(jnp.bfloat16)
    key_clipped = (w_key.astype(jnp.float32) * column_scale[None, :]).astype(jnp.bfloat16)
    return (
        output,
        grad_tokens,
        final_gain_a,
        final_query,
        final_key,
        final_value,
        final_out,
        final_bias,
        final_gain_f,
        final_gate,
        final_up,
        final_down,
        head_maxima,
        query_clipped,
        key_clipped,
    )


RING = (0, 2, 4, 6, 7, 5, 3, 1)
F32 = jnp.float32
BF16 = jnp.bfloat16


def look_up(table, index):
    found = jnp.int32(table[0])
    for place in range(1, len(table)):
        found = jnp.where(index == place, table[place], found)
    return found


def swap(array_in, axis_name):
    return lax.ppermute(array_in, axis_name, [(0, 1), (1, 0)])


def dot_f32(left, right):
    return jnp.dot(left, right, preferred_element_type=F32)


def dot_nt(left, right):
    return lax.dot_general(left, right, (((1,), (1,)), ((), ())), preferred_element_type=F32)


def dot_tn(left, right):
    return lax.dot_general(left, right, (((0,), (0,)), ((), ())), preferred_element_type=F32)


def ring_sum(forward_parts, backward_parts):
    count = len(RING)
    up_pairs = [(RING[i], RING[(i + 1) % count]) for i in range(count)]
    down_pairs = [(after, before) for before, after in up_pairs]
    me = look_up([RING.index(c) for c in range(count)], lax.axis_index("ctx"))
    flows = [(array_in, 1, up_pairs) for array_in in forward_parts]
    flows += [(array_in, -1, down_pairs) for array_in in backward_parts]

    def piece(array_in, chunk):
        rows = array_in.shape[0] // count
        return lax.dynamic_slice_in_dim(array_in, jnp.mod(chunk, count) * rows, rows)

    current = [piece(array_in, me) for array_in, way, pairs in flows]
    for step in range(count - 1):
        arrived = [
            lax.ppermute(held, "ctx", pairs) for held, (array_in, way, pairs) in zip(current, flows)
        ]
        current = [
            (got.astype(F32) + piece(array_in, me - way * (step + 1)).astype(F32)).astype(BF16)
            for got, (array_in, way, pairs) in zip(arrived, flows)
        ]
    results = [jnp.zeros(array_in.shape, F32) for array_in, way, pairs in flows]

    def place(result, chunk, held):
        rows = held.shape[0]
        return lax.dynamic_update_slice_in_dim(
            result, held.astype(F32), jnp.mod(chunk, count) * rows, 0
        )

    for step in range(count):
        results = [
            place(result, me - way * (count - 1 + step), held)
            for result, held, (array_in, way, pairs) in zip(results, current, flows)
        ]
        if step < count - 1:
            current = [
                lax.ppermute(held, "ctx", pairs)
                for held, (array_in, way, pairs) in zip(current, flows)
            ]
    forward_count = len(forward_parts)
    return (results[:forward_count], results[forward_count:])


def per_device_ring(
    tokens,
    cotangent,
    token_order,
    seq_lengths,
    rel_buckets,
    gain_attn,
    w_query,
    w_key,
    w_value,
    w_out,
    rel_bias,
    gain_ffn,
    w_gate,
    w_up,
    w_down,
):
    core = lax.axis_index("fsdp")
    ctx = lax.axis_index("ctx")
    tp = lax.axis_index("tp")
    local_rows = tokens.shape[0]
    half = w_query.shape[0]
    head_count = w_query.shape[1] // DH
    group_rows = local_rows * lax.axis_size("ctx")
    first = core == 0

    def halves(array_in):
        left, right = (array_in[:, :half], array_in[:, half:])
        return (jnp.where(first, left, right), jnp.where(first, right, left))

    def whole(own, other):
        return jnp.concatenate(
            [jnp.where(first, own, other), jnp.where(first, other, own)], axis=1
        )

    small = jnp.concatenate([gain_attn, gain_ffn, rel_bias.reshape(-1)])
    small_far = swap(small, "fsdp")
    wq_far, wk_far, wv_far = (swap(w_query, "fsdp"), swap(w_key, "fsdp"), swap(w_value, "fsdp"))
    wo_far = swap(w_out, "fsdp")
    wg_far, wu_far, wd_far = (swap(w_gate, "fsdp"), swap(w_up, "fsdp"), swap(w_down, "fsdp"))
    ga_own, ga_far = (gain_attn.astype(F32), small_far[:half].astype(F32))
    gf_own, gf_far = (gain_ffn.astype(F32), small_far[half : 2 * half].astype(F32))
    bias_far = small_far[2 * half :].reshape(rel_bias.shape)
    bias_local = jnp.where(
        first,
        jnp.concatenate([rel_bias, bias_far]),
        jnp.concatenate([bias_far, rel_bias]),
    )
    tok_own, tok_far = halves(tokens)
    cot_own, cot_far = halves(cotangent)
    tok_own, tok_far = (tok_own.astype(F32), tok_far.astype(F32))

    def norm_scale(own, far):
        total = jnp.sum(own * own, axis=1, keepdims=True) + jnp.sum(far * far, axis=1, keepdims=True)
        return lax.rsqrt(total / (2 * half) + EPS)

    scale_a = norm_scale(tok_own, tok_far)
    normed_own = (tok_own * scale_a * ga_own).astype(BF16)
    normed_far = (tok_far * scale_a * ga_far).astype(BF16)
    queries = (dot_f32(normed_own, w_query) + dot_f32(normed_far, wq_far)).astype(BF16)
    keys_here = (dot_f32(normed_own, w_key) + dot_f32(normed_far, wk_far)).astype(BF16)
    values_here = (dot_f32(normed_own, w_value) + dot_f32(normed_far, wv_far)).astype(BF16)
    key_block = min(512, group_rows)
    block_count = group_rows // key_block
    ranges = bucket_ranges(rel_buckets)
    order_row = token_order[0]
    seq_ids = segment_of(order_row, seq_lengths[0])
    row_start = lax.axis_index("ctx") * local_rows
    query_pos = lax.dynamic_slice_in_dim(order_row, row_start, local_rows)
    query_seg = lax.dynamic_slice_in_dim(seq_ids, row_start, local_rows)
    pos_blocks = order_row.reshape(block_count, key_block)
    seg_blocks = seq_ids.reshape(block_count, key_block)
    query_heads = queries.reshape(local_rows, head_count, DH)
    key_all, value_all = (
        lax.all_gather(keys_here, "ctx", axis=0, tiled=True),
        lax.all_gather(values_here, "ctx", axis=0, tiled=True),
    )

    def blocked(array_in):
        return array_in.reshape(block_count, key_block, head_count, DH)

    def forward_block(running, inputs):
        summed, totals, head_top = running
        key_blk, value_blk, pos_blk, seg_blk = inputs
        raw_scores = jnp.einsum(
            "thd,khd->htk", query_heads, key_blk, preferred_element_type=jnp.float32
        )
        bucket_hot, pair_bias, same_seq = pair_terms(
            query_pos, query_seg, pos_blk, seg_blk, ranges, bias_local
        )
        weights = jnp.where(same_seq, jnp.exp(raw_scores + pair_bias), 0.0)
        totals = totals + jnp.sum(weights, axis=2)
        summed = summed + jnp.einsum(
            "htk,khd->thd",
            weights.astype(jnp.bfloat16),
            value_blk,
            preferred_element_type=jnp.float32,
        )
        head_top = jnp.maximum(
            head_top, jnp.max(jnp.where(same_seq, raw_scores, -1e30), axis=(1, 2))
        )
        return ((summed, totals, head_top), None)

    start_state = (
        jnp.zeros((local_rows, head_count, DH), jnp.float32),
        jnp.zeros((head_count, local_rows), jnp.float32),
        jnp.full((head_count,), -1e30, jnp.float32),
    )
    (summed, totals, head_top), unused = lax.scan(
        forward_block, start_state, (blocked(key_all), blocked(value_all), pos_blocks, seg_blocks)
    )
    row_totals = jnp.transpose(totals)[:, :, None]
    context_exact = summed / row_totals
    context = context_exact.reshape(local_rows, head_count * DH).astype(jnp.bfloat16)
    head_maxima = lax.pmax(head_top, ("fsdp", "ctx"))

    def tp_sum(own, far):
        own, far = (own.astype(BF16), far.astype(BF16))
        return (
            own.astype(F32) + swap(own, "tp").astype(F32),
            far.astype(F32) + swap(far, "tp").astype(F32),
        )

    attn_own, attn_far = tp_sum(dot_f32(context, w_out), dot_f32(context, wo_far))
    hid_own, hid_far = (tok_own + attn_own, tok_far + attn_far)
    inner_grad = dot_nt(cot_own, w_down) + dot_nt(cot_far, wd_far)
    scale_f = norm_scale(hid_own, hid_far)
    nffn_own = (hid_own * scale_f * gf_own).astype(BF16)
    nffn_far = (hid_far * scale_f * gf_far).astype(BF16)
    gate_pre = dot_f32(nffn_own, w_gate) + dot_f32(nffn_far, wg_far)
    up_pre = dot_f32(nffn_own, w_up) + dot_f32(nffn_far, wu_far)
    inner_act = geglu(gate_pre, up_pre).astype(BF16)
    unused, geglu_back = jax.vjp(geglu, gate_pre, up_pre)
    gate_grad, up_grad = geglu_back(inner_grad)
    gate_grad = gate_grad.astype(BF16)
    up_grad = up_grad.astype(BF16)
    dnf_own, dnf_far = tp_sum(
        dot_nt(gate_grad, w_gate) + dot_nt(up_grad, w_up),
        dot_nt(gate_grad, wg_far) + dot_nt(up_grad, wu_far),
    )
    ffn_own, ffn_far = tp_sum(dot_f32(inner_act, w_down), dot_f32(inner_act, wd_far))
    output = whole(hid_own + ffn_own, hid_far + ffn_far).astype(BF16)

    def pair_rows(own):
        return jnp.concatenate([own, swap(own, "fsdp")])

    def pair_half(own, far):
        return jnp.concatenate([own, swap(far, "fsdp")])

    nffn_pair = pair_half(nffn_own, nffn_far)
    grad_gate = dot_tn(nffn_pair, pair_rows(gate_grad)).astype(BF16)
    grad_up = dot_tn(nffn_pair, pair_rows(up_grad)).astype(BF16)
    grad_down = dot_tn(pair_rows(inner_act), pair_half(cot_own, cot_far)).astype(BF16)
    down_rows = grad_down.shape[0] // 2

    def norm_back(own, far, scale, gain_own, gain_far, dy_own, dy_far):
        mean_term = (
            jnp.sum(gain_own * dy_own * own, axis=1, keepdims=True)
            + jnp.sum(gain_far * dy_far * far, axis=1, keepdims=True)
        ) / (2 * half)
        cubed = scale * scale * scale * mean_term
        return (
            scale * (gain_own * dy_own) - own * cubed,
            scale * (gain_far * dy_far) - far * cubed,
            jnp.sum(dy_own * own * scale, axis=0),
            jnp.sum(dy_far * far * scale, axis=0),
        )

    back_own, back_far, dgf_own, dgf_far = norm_back(
        hid_own, hid_far, scale_f, gf_own, gf_far, dnf_own, dnf_far
    )
    hgrad_own = cot_own.astype(F32) + back_own
    hgrad_far = cot_far.astype(F32) + back_far
    ag_own, ag_far = (hgrad_own.astype(BF16), hgrad_far.astype(BF16))
    grad_out = dot_tn(pair_rows(context), pair_half(ag_own, ag_far)).astype(BF16)
    context_grad = dot_nt(ag_own, w_out) + dot_nt(ag_far, wo_far)
    context_grad = context_grad.reshape(local_rows, head_count, DH)
    summed_grad = (context_grad / row_totals).astype(jnp.bfloat16)
    total_grad = jnp.transpose(-jnp.sum(context_grad * context_exact, axis=2) / row_totals[:, :, 0])
    key_back, value_back = (key_all, value_all)

    def backward_block(running, inputs):
        query_acc, bias_acc = running
        key_blk, value_blk, pos_blk, seg_blk = inputs
        raw_scores = jnp.einsum(
            "thd,khd->htk", query_heads, key_blk, preferred_element_type=jnp.float32
        )
        bucket_hot, pair_bias, same_seq = pair_terms(
            query_pos, query_seg, pos_blk, seg_blk, ranges, bias_local
        )
        weights = jnp.where(same_seq, jnp.exp(raw_scores + pair_bias), 0.0)
        prob_grad = (
            jnp.einsum("thd,khd->htk", summed_grad, value_blk, preferred_element_type=jnp.float32)
            + total_grad[:, :, None]
        )
        score_grad = (weights * prob_grad).astype(jnp.bfloat16)
        query_acc = query_acc + jnp.einsum(
            "htk,khd->thd", score_grad, key_blk, preferred_element_type=jnp.float32
        )
        key_grad = jnp.einsum(
            "htk,thd->khd", score_grad, query_heads, preferred_element_type=jnp.float32
        )
        value_grad = jnp.einsum(
            "htk,thd->khd",
            weights.astype(jnp.bfloat16),
            summed_grad,
            preferred_element_type=jnp.float32,
        )
        bucket_sums = jnp.einsum(
            "htk,btk->hb", score_grad, bucket_hot, preferred_element_type=jnp.float32
        )
        return ((query_acc, bias_acc + bucket_sums), (key_grad, value_grad))

    zero_state = (
        jnp.zeros((local_rows, head_count, DH), jnp.float32),
        jnp.zeros((head_count, NB), jnp.float32),
    )
    (query_acc, bias_acc), (key_grads, value_grads) = lax.scan(
        backward_block, zero_state, (blocked(key_back), blocked(value_back), pos_blocks, seg_blocks)
    )
    key_grad_all, value_grad_all = (
        lax.psum_scatter(
            key_grads.reshape(group_rows, head_count * DH).astype(jnp.bfloat16),
            "ctx",
            scatter_dimension=0,
            tiled=True,
        ).astype(jnp.float32),
        lax.psum_scatter(
            value_grads.reshape(group_rows, head_count * DH).astype(jnp.bfloat16),
            "ctx",
            scatter_dimension=0,
            tiled=True,
        ).astype(jnp.float32),
    )
    query_grad = query_acc.reshape(local_rows, head_count * DH).astype(jnp.bfloat16)
    key_grad = key_grad_all.astype(jnp.bfloat16)
    value_grad = value_grad_all.astype(jnp.bfloat16)
    grad_bias = jnp.transpose(bias_acc)
    (final_gate, down_low), (final_up, down_high) = ring_sum(
        [grad_gate, grad_down[:down_rows]], [grad_up, grad_down[down_rows:]]
    )
    final_down = jnp.concatenate([down_low, down_high])
    dn_own, dn_far = tp_sum(
        dot_nt(query_grad, w_query) + dot_nt(key_grad, w_key) + dot_nt(value_grad, w_value),
        dot_nt(query_grad, wq_far) + dot_nt(key_grad, wk_far) + dot_nt(value_grad, wv_far),
    )
    tback_own, tback_far, dga_own, dga_far = norm_back(
        tok_own, tok_far, scale_a, ga_own, ga_far, dn_own, dn_far
    )
    grad_tokens = whole(hgrad_own + tback_own, hgrad_far + tback_far)
    normed_pair = pair_half(normed_own, normed_far)
    grad_query = dot_tn(normed_pair, pair_rows(query_grad)).astype(BF16)
    grad_key = dot_tn(normed_pair, pair_rows(key_grad)).astype(BF16)
    grad_value = dot_tn(normed_pair, pair_rows(value_grad)).astype(BF16)
    (final_query, final_key), (final_value, final_out) = ring_sum(
        [grad_query, grad_key], [grad_value, grad_out]
    )
    bias_rows = rel_bias.shape[0]
    small_own = jnp.concatenate([dga_own, dgf_own])
    small_sent = jnp.concatenate([dga_far, dgf_far])
    bias_flat = grad_bias.reshape(2, -1)
    small_own = jnp.concatenate([small_own, jnp.where(first, bias_flat[0], bias_flat[1])])
    small_sent = jnp.concatenate([small_sent, jnp.where(first, bias_flat[1], bias_flat[0])])
    small_sum = lax.psum(small_own + swap(small_sent, "fsdp"), "ctx")
    final_gain_a, final_gain_f = (small_sum[:half], small_sum[half : 2 * half])
    final_bias = small_sum[2 * half :].reshape(rel_bias.shape)
    clip_scale = TAU_CLIP / jnp.maximum(head_maxima, TAU_CLIP)
    column_scale = jnp.repeat(jnp.sqrt(clip_scale), DH)
    query_clipped = (w_query.astype(F32) * column_scale[None, :]).astype(BF16)
    key_clipped = (w_key.astype(F32) * column_scale[None, :]).astype(BF16)
    return (
        output,
        grad_tokens,
        final_gain_a,
        final_query,
        final_key,
        final_value,
        final_out,
        final_bias,
        final_gain_f,
        final_gate,
        final_up,
        final_down,
        head_maxima,
        query_clipped,
        key_clipped,
    )


def pick_program(mesh):
    sizes = dict(mesh.shape)
    if sizes["fsdp"] == 2 and sizes["ctx"] == len(RING) and sizes["tp"] == 2:
        return per_device_ring
    return per_device_generic


def solution(mesh):
    in_specs = (
        P(("fsdp", "ctx"), None),
        P(("fsdp", "ctx"), None),
        P("fsdp", None),
        P("fsdp", None),
        P(),
        P("fsdp"),
        P("fsdp", "tp"),
        P("fsdp", "tp"),
        P("fsdp", "tp"),
        P("tp", "fsdp"),
        P("fsdp", "tp"),
        P("fsdp"),
        P("fsdp", "tp"),
        P("fsdp", "tp"),
        P("tp", "fsdp"),
    )
    out_specs = (
        P(("fsdp", "ctx"), None),
        P(("fsdp", "ctx"), None),
        P("fsdp"),
        P("fsdp", "tp"),
        P("fsdp", "tp"),
        P("fsdp", "tp"),
        P("tp", "fsdp"),
        P("fsdp", "tp"),
        P("fsdp"),
        P("fsdp", "tp"),
        P("fsdp", "tp"),
        P("tp", "fsdp"),
        P("tp"),
        P("fsdp", "tp"),
        P("fsdp", "tp"),
    )
    per_device = pick_program(mesh)
    return jax.shard_map(
        per_device, mesh=mesh, in_specs=in_specs, out_specs=out_specs, check_vma=False
    )
```

```python
import jax
import jax.numpy as jnp
from jax import lax
from jax.experimental import pallas as pl
from jax.experimental.pallas import tpu as pltpu
from jax.sharding import PartitionSpec as P

DH = 64
NB = 32


EPS = 1e-06
TAU_CLIP = 6.0


def rms_norm(values, gain):
    return values * lax.rsqrt(jnp.mean(values * values, axis=-1, keepdims=True) + EPS) * gain


def geglu(gate_pre, up_pre):
    return jax.nn.gelu(gate_pre, approximate=True) * up_pre


def segment_of(positions, lengths_row):
    offsets = jnp.cumsum(lengths_row) - lengths_row
    return jnp.sum((positions[:, None] >= offsets[None, :]).astype(jnp.int32), axis=1) - 1


def bucket_ranges(rel_buckets):
    table_len = rel_buckets.shape[0]
    index_all = jnp.arange(table_len, dtype=jnp.int32)
    bucket_ids = jnp.arange(NB, dtype=jnp.int32)
    matched = rel_buckets[:, None] == bucket_ids[None, :]
    range_first = jnp.min(jnp.where(matched, index_all[:, None], table_len), axis=0)
    range_last = jnp.max(jnp.where(matched, index_all[:, None], -1), axis=0)
    return (range_first, range_last, table_len)


def pair_terms(query_pos, query_seg, key_pos, key_seg, ranges, bias_table):
    range_first, range_last, table_len = ranges
    longest = (table_len + 1) // 2
    offset = jnp.clip(key_pos[None, :] - query_pos[:, None] + longest - 1, 0, 2 * longest - 2)
    inside = (offset[None, :, :] >= range_first[:, None, None]) & (
        offset[None, :, :] <= range_last[:, None, None]
    )
    bucket_hot = inside.astype(jnp.bfloat16)
    pair_bias = jnp.einsum(
        "btk,bh->htk", bucket_hot, bias_table, preferred_element_type=jnp.float32
    )
    same_seq = (query_seg[:, None] == key_seg[None, :])[None]
    return (bucket_hot, pair_bias, same_seq)


def per_device_generic(
    tokens,
    cotangent,
    token_order,
    seq_lengths,
    rel_buckets,
    gain_attn,
    w_query,
    w_key,
    w_value,
    w_out,
    rel_bias,
    gain_ffn,
    w_gate,
    w_up,
    w_down,
):
    local_rows = tokens.shape[0]
    head_count = w_query.shape[1] // DH
    group_rows = local_rows * lax.axis_size("ctx")
    key_block = min(512, group_rows)
    block_count = group_rows // key_block
    ranges = bucket_ranges(rel_buckets)
    gain_a, full_query, full_key, full_value, full_out, bias_local = (
        lax.all_gather(gain_attn, "fsdp", axis=0, tiled=True),
        lax.all_gather(w_query, "fsdp", axis=0, tiled=True),
        lax.all_gather(w_key, "fsdp", axis=0, tiled=True),
        lax.all_gather(w_value, "fsdp", axis=0, tiled=True),
        lax.all_gather(w_out, "fsdp", axis=1, tiled=True),
        lax.all_gather(rel_bias, "fsdp", axis=0, tiled=True),
    )
    tokens_f = tokens.astype(jnp.float32)
    gain_a32 = gain_a.astype(jnp.float32)
    normed = rms_norm(tokens_f, gain_a32).astype(jnp.bfloat16)
    queries = jnp.dot(normed, full_query, preferred_element_type=jnp.float32).astype(jnp.bfloat16)
    keys_here = jnp.dot(normed, full_key, preferred_element_type=jnp.float32).astype(jnp.bfloat16)
    values_here = jnp.dot(normed, full_value, preferred_element_type=jnp.float32).astype(
        jnp.bfloat16
    )
    order_row = token_order[0]
    seq_ids = segment_of(order_row, seq_lengths[0])
    row_start = lax.axis_index("ctx") * local_rows
    query_pos = lax.dynamic_slice_in_dim(order_row, row_start, local_rows)
    query_seg = lax.dynamic_slice_in_dim(seq_ids, row_start, local_rows)
    pos_blocks = order_row.reshape(block_count, key_block)
    seg_blocks = seq_ids.reshape(block_count, key_block)
    query_heads = queries.reshape(local_rows, head_count, DH)
    key_all, value_all = (
        lax.all_gather(keys_here, "ctx", axis=0, tiled=True),
        lax.all_gather(values_here, "ctx", axis=0, tiled=True),
    )

    def blocked(array_in):
        return array_in.reshape(block_count, key_block, head_count, DH)

    def forward_block(running, inputs):
        summed, totals, head_top = running
        key_blk, value_blk, pos_blk, seg_blk = inputs
        raw_scores = jnp.einsum(
            "thd,khd->htk", query_heads, key_blk, preferred_element_type=jnp.float32
        )
        bucket_hot, pair_bias, same_seq = pair_terms(
            query_pos, query_seg, pos_blk, seg_blk, ranges, bias_local
        )
        weights = jnp.where(same_seq, jnp.exp(raw_scores + pair_bias), 0.0)
        totals = totals + jnp.sum(weights, axis=2)
        summed = summed + jnp.einsum(
            "htk,khd->thd",
            weights.astype(jnp.bfloat16),
            value_blk,
            preferred_element_type=jnp.float32,
        )
        head_top = jnp.maximum(
            head_top, jnp.max(jnp.where(same_seq, raw_scores, -1e30), axis=(1, 2))
        )
        return ((summed, totals, head_top), None)

    start_state = (
        jnp.zeros((local_rows, head_count, DH), jnp.float32),
        jnp.zeros((head_count, local_rows), jnp.float32),
        jnp.full((head_count,), -1e30, jnp.float32),
    )
    (summed, totals, head_top), unused = lax.scan(
        forward_block, start_state, (blocked(key_all), blocked(value_all), pos_blocks, seg_blocks)
    )
    row_totals = jnp.transpose(totals)[:, :, None]
    context_exact = summed / row_totals
    context = context_exact.reshape(local_rows, head_count * DH).astype(jnp.bfloat16)
    head_maxima = lax.pmax(head_top, ("fsdp", "ctx"))
    attn_out = lax.psum(
        jnp.dot(context, full_out, preferred_element_type=jnp.float32).astype(jnp.bfloat16), "tp"
    ).astype(jnp.float32)
    hidden_state = tokens_f + attn_out
    gain_f, full_gate, full_up, full_down = (
        lax.all_gather(gain_ffn, "fsdp", axis=0, tiled=True),
        lax.all_gather(w_gate, "fsdp", axis=0, tiled=True),
        lax.all_gather(w_up, "fsdp", axis=0, tiled=True),
        lax.all_gather(w_down, "fsdp", axis=1, tiled=True),
    )
    gain_f32 = gain_f.astype(jnp.float32)
    normed_ffn = rms_norm(hidden_state, gain_f32).astype(jnp.bfloat16)
    gate_pre = jnp.dot(normed_ffn, full_gate, preferred_element_type=jnp.float32)
    up_pre = jnp.dot(normed_ffn, full_up, preferred_element_type=jnp.float32)
    inner_act = geglu(gate_pre, up_pre).astype(jnp.bfloat16)
    ffn_out = lax.psum(
        jnp.dot(inner_act, full_down, preferred_element_type=jnp.float32).astype(jnp.bfloat16), "tp"
    ).astype(jnp.float32)
    output = (hidden_state + ffn_out).astype(jnp.bfloat16)
    grad_down = jnp.einsum("tf,td->fd", inner_act, cotangent, preferred_element_type=jnp.float32)
    inner_grad = jnp.einsum("td,fd->tf", cotangent, full_down, preferred_element_type=jnp.float32)
    unused, geglu_back = jax.vjp(geglu, gate_pre, up_pre)
    gate_grad, up_grad = geglu_back(inner_grad)
    gate_grad = gate_grad.astype(jnp.bfloat16)
    up_grad = up_grad.astype(jnp.bfloat16)
    grad_gate = jnp.einsum("tc,tf->cf", normed_ffn, gate_grad, preferred_element_type=jnp.float32)
    grad_up = jnp.einsum("tc,tf->cf", normed_ffn, up_grad, preferred_element_type=jnp.float32)
    ffn_term = jnp.einsum(
        "tf,cf->tc", gate_grad, full_gate, preferred_element_type=jnp.float32
    ) + jnp.einsum("tf,cf->tc", up_grad, full_up, preferred_element_type=jnp.float32)
    normed_ffn_grad = lax.psum(ffn_term.astype(jnp.bfloat16), "tp").astype(jnp.float32)
    unused, norm_ffn_back = jax.vjp(rms_norm, hidden_state, gain_f32)
    hidden_norm_grad, grad_gain_ffn = norm_ffn_back(normed_ffn_grad)
    hidden_grad = cotangent.astype(jnp.float32) + hidden_norm_grad
    attn_grad = hidden_grad.astype(jnp.bfloat16)
    grad_out = jnp.einsum("tc,td->cd", context, attn_grad, preferred_element_type=jnp.float32)
    context_grad = jnp.einsum(
        "td,cd->tc", attn_grad, full_out, preferred_element_type=jnp.float32
    ).reshape(local_rows, head_count, DH)
    summed_grad = (context_grad / row_totals).astype(jnp.bfloat16)
    total_grad = jnp.transpose(-jnp.sum(context_grad * context_exact, axis=2) / row_totals[:, :, 0])
    key_back, value_back = (key_all, value_all)

    def backward_block(running, inputs):
        query_acc, bias_acc = running
        key_blk, value_blk, pos_blk, seg_blk = inputs
        raw_scores = jnp.einsum(
            "thd,khd->htk", query_heads, key_blk, preferred_element_type=jnp.float32
        )
        bucket_hot, pair_bias, same_seq = pair_terms(
            query_pos, query_seg, pos_blk, seg_blk, ranges, bias_local
        )
        weights = jnp.where(same_seq, jnp.exp(raw_scores + pair_bias), 0.0)
        prob_grad = (
            jnp.einsum("thd,khd->htk", summed_grad, value_blk, preferred_element_type=jnp.float32)
            + total_grad[:, :, None]
        )
        score_grad = (weights * prob_grad).astype(jnp.bfloat16)
        query_acc = query_acc + jnp.einsum(
            "htk,khd->thd", score_grad, key_blk, preferred_element_type=jnp.float32
        )
        key_grad = jnp.einsum(
            "htk,thd->khd", score_grad, query_heads, preferred_element_type=jnp.float32
        )
        value_grad = jnp.einsum(
            "htk,thd->khd",
            weights.astype(jnp.bfloat16),
            summed_grad,
            preferred_element_type=jnp.float32,
        )
        bucket_sums = jnp.einsum(
            "htk,btk->hb", score_grad, bucket_hot, preferred_element_type=jnp.float32
        )
        return ((query_acc, bias_acc + bucket_sums), (key_grad, value_grad))

    zero_state = (
        jnp.zeros((local_rows, head_count, DH), jnp.float32),
        jnp.zeros((head_count, NB), jnp.float32),
    )
    (query_acc, bias_acc), (key_grads, value_grads) = lax.scan(
        backward_block, zero_state, (blocked(key_back), blocked(value_back), pos_blocks, seg_blocks)
    )
    key_grad_all, value_grad_all = (
        lax.psum_scatter(
            key_grads.reshape(group_rows, head_count * DH).astype(jnp.bfloat16),
            "ctx",
            scatter_dimension=0,
            tiled=True,
        ).astype(jnp.float32),
        lax.psum_scatter(
            value_grads.reshape(group_rows, head_count * DH).astype(jnp.bfloat16),
            "ctx",
            scatter_dimension=0,
            tiled=True,
        ).astype(jnp.float32),
    )
    query_grad = query_acc.reshape(local_rows, head_count * DH).astype(jnp.bfloat16)
    key_grad = key_grad_all.astype(jnp.bfloat16)
    value_grad = value_grad_all.astype(jnp.bfloat16)
    attn_term = jnp.einsum("tc,dc->td", query_grad, full_query, preferred_element_type=jnp.float32)
    attn_term = attn_term + jnp.einsum(
        "tc,dc->td", key_grad, full_key, preferred_element_type=jnp.float32
    )
    attn_term = attn_term + jnp.einsum(
        "tc,dc->td", value_grad, full_value, preferred_element_type=jnp.float32
    )
    normed_grad = lax.psum(attn_term.astype(jnp.bfloat16), "tp").astype(jnp.float32)
    unused, norm_attn_back = jax.vjp(rms_norm, tokens_f, gain_a32)
    token_norm_grad, grad_gain_attn = norm_attn_back(normed_grad)
    grad_tokens = hidden_grad + token_norm_grad
    grad_query = jnp.einsum("td,tc->dc", normed, query_grad, preferred_element_type=jnp.float32)
    grad_key = jnp.einsum("td,tc->dc", normed, key_grad, preferred_element_type=jnp.float32)
    grad_value = jnp.einsum("td,tc->dc", normed, value_grad, preferred_element_type=jnp.float32)
    grad_bias = jnp.transpose(bias_acc)
    (
        share_gain_a,
        share_query,
        share_key,
        share_value,
        share_out,
        share_bias,
        share_gain_f,
        share_gate,
        share_up,
        share_down,
    ) = (
        lax.psum_scatter(
            grad_gain_attn.astype(jnp.bfloat16), "fsdp", scatter_dimension=0, tiled=True
        ).astype(jnp.float32),
        lax.psum_scatter(
            grad_query.astype(jnp.bfloat16), "fsdp", scatter_dimension=0, tiled=True
        ).astype(jnp.float32),
        lax.psum_scatter(
            grad_key.astype(jnp.bfloat16), "fsdp", scatter_dimension=0, tiled=True
        ).astype(jnp.float32),
        lax.psum_scatter(
            grad_value.astype(jnp.bfloat16), "fsdp", scatter_dimension=0, tiled=True
        ).astype(jnp.float32),
        lax.psum_scatter(
            grad_out.astype(jnp.bfloat16), "fsdp", scatter_dimension=1, tiled=True
        ).astype(jnp.float32),
        lax.psum_scatter(
            grad_bias.astype(jnp.bfloat16), "fsdp", scatter_dimension=0, tiled=True
        ).astype(jnp.float32),
        lax.psum_scatter(
            grad_gain_ffn.astype(jnp.bfloat16), "fsdp", scatter_dimension=0, tiled=True
        ).astype(jnp.float32),
        lax.psum_scatter(
            grad_gate.astype(jnp.bfloat16), "fsdp", scatter_dimension=0, tiled=True
        ).astype(jnp.float32),
        lax.psum_scatter(
            grad_up.astype(jnp.bfloat16), "fsdp", scatter_dimension=0, tiled=True
        ).astype(jnp.float32),
        lax.psum_scatter(
            grad_down.astype(jnp.bfloat16), "fsdp", scatter_dimension=1, tiled=True
        ).astype(jnp.float32),
    )
    (
        final_gain_a,
        final_query,
        final_key,
        final_value,
        final_out,
        final_bias,
        final_gain_f,
        final_gate,
        final_up,
        final_down,
    ) = (
        lax.psum(share_gain_a.astype(jnp.bfloat16), "ctx").astype(jnp.float32),
        lax.psum(share_query.astype(jnp.bfloat16), "ctx").astype(jnp.float32),
        lax.psum(share_key.astype(jnp.bfloat16), "ctx").astype(jnp.float32),
        lax.psum(share_value.astype(jnp.bfloat16), "ctx").astype(jnp.float32),
        lax.psum(share_out.astype(jnp.bfloat16), "ctx").astype(jnp.float32),
        lax.psum(share_bias.astype(jnp.bfloat16), "ctx").astype(jnp.float32),
        lax.psum(share_gain_f.astype(jnp.bfloat16), "ctx").astype(jnp.float32),
        lax.psum(share_gate.astype(jnp.bfloat16), "ctx").astype(jnp.float32),
        lax.psum(share_up.astype(jnp.bfloat16), "ctx").astype(jnp.float32),
        lax.psum(share_down.astype(jnp.bfloat16), "ctx").astype(jnp.float32),
    )
    clip_scale = TAU_CLIP / jnp.maximum(head_maxima, TAU_CLIP)
    column_scale = jnp.repeat(jnp.sqrt(clip_scale), DH)
    query_clipped = (w_query.astype(jnp.float32) * column_scale[None, :]).astype(jnp.bfloat16)
    key_clipped = (w_key.astype(jnp.float32) * column_scale[None, :]).astype(jnp.bfloat16)
    return (
        output,
        grad_tokens,
        final_gain_a,
        final_query,
        final_key,
        final_value,
        final_out,
        final_bias,
        final_gain_f,
        final_gate,
        final_up,
        final_down,
        head_maxima,
        query_clipped,
        key_clipped,
    )


RING = (0, 2, 4, 6, 7, 5, 3, 1)
F32 = jnp.float32
BF16 = jnp.bfloat16


def look_up(table, index):
    found = jnp.int32(table[0])
    for place in range(1, len(table)):
        found = jnp.where(index == place, table[place], found)
    return found


def swap(array_in, axis_name):
    return lax.ppermute(array_in, axis_name, [(0, 1), (1, 0)])


def dot_f32(left, right):
    return jnp.dot(left, right, preferred_element_type=F32)


def dot_nt(left, right):
    return lax.dot_general(left, right, (((1,), (1,)), ((), ())), preferred_element_type=F32)


def dot_tn(left, right):
    return lax.dot_general(left, right, (((0,), (0,)), ((), ())), preferred_element_type=F32)


BAND = 512


TILE = 256
PAIR = 2 * DH
FAR_OFF = 1e30


def lane_of(rows):
    return lax.broadcasted_iota(jnp.int32, (rows, PAIR), 1)


def head_lanes(lane, head):
    own = lane < DH if head == 0 else lane >= DH
    spare = lane - DH if head == 0 else lane
    return (own, spare)


def sequence_of(offsets, start):
    position = start + lax.broadcasted_iota(jnp.int32, (TILE, PAIR), 0)
    sequence = jnp.zeros((TILE, PAIR), jnp.int32)
    for item in range(1, offsets.shape[0]):
        sequence = sequence + (position >= offsets[item]).astype(jnp.int32)
    return sequence


def tile_rows(index):
    return pl.ds(pl.multiple_of(index * TILE, TILE), TILE)


def put_in_order(order_row, source, index):
    position = index * TILE + lax.broadcasted_iota(jnp.int32, (TILE, source.shape[0]), 0)
    hot = (order_row[...] == position).astype(F32).astype(BF16)
    return dot_f32(hot, source[...])


def put_back(order_col, source, index):
    position = lax.broadcasted_iota(jnp.int32, (TILE, source.shape[0]), 1)
    hot = (order_col[tile_rows(index), :] == position).astype(F32).astype(BF16)
    return dot_f32(hot, source[...]).astype(BF16)


def fill_strip(strip, table):
    width = table.shape[1]
    for head in range(2):
        row = jnp.broadcast_to(table[pl.ds(head, 1), :], (TILE, width))
        strip[head] = pltpu.roll(row, 1, 1, stride=1, stride_axis=0)


def score_operands(query, key, sequence, head):
    own, spare = head_lanes(lane_of(TILE), head)
    differs = jnp.where((spare < 8) & (sequence != spare), 1.0, 0.0)
    blocked = jnp.where(sequence == spare, -FAR_OFF, 0.0)
    return (
        jnp.where(own, query, differs).astype(BF16),
        jnp.where(own, key, blocked).astype(BF16),
    )


def attend_kernel(
    low, high, offsets, order_row, order_col, table, mixed,
    ordered, context, exact, inverse, tops,
    query_aug, key_aug, value_aug, strip, total, held,
):
    tiles = mixed.shape[0] // TILE
    reach = strip.shape[2] // TILE // 2
    lane = lane_of(TILE)
    fill_strip(strip, table)
    tops[...] = jnp.full(tops.shape, -FAR_OFF, F32)

    @pl.loop(0, tiles)
    def arrange(index):
        rows = tile_rows(index)
        block = put_in_order(order_row, mixed, index)
        ordered[rows, :] = block.astype(BF16)
        sequence = sequence_of(offsets, index * TILE)
        for head in range(2):
            own, spare = head_lanes(lane, head)
            query, key = score_operands(
                block[:, :PAIR], block[:, PAIR : 2 * PAIR], sequence, head
            )
            query_aug[head, rows, :] = query
            key_aug[head, rows, :] = key
            value_aug[head, rows, :] = jnp.where(
                own, block[:, 2 * PAIR :], jnp.where(spare == 0, 1.0, 0.0)
            ).astype(BF16)

    @pl.loop(0, tiles)
    def attend(index):
        rows = tile_rows(index)
        total[...] = jnp.zeros(total.shape, F32)

        @pl.loop(low[index], high[index])
        def keys(other):
            columns = tile_rows(other)
            place = tile_rows(other - index + reach)
            for head in range(2):
                raw = dot_nt(query_aug[head, rows, :], key_aug[head, columns, :])
                tops[head] = jnp.maximum(
                    tops[head], jnp.max(raw.reshape(TILE // 8, 8, TILE), axis=0)
                )
                weight = jnp.exp(raw + strip[head, :, place]).astype(BF16)
                total[head] += dot_f32(weight, value_aug[head, columns, :])

        parts = []
        for head in range(2):
            summed = total[head]
            spot = DH if head == 0 else 0
            row_total = summed[:, spot : spot + 1]
            parts.append((summed / row_total, jnp.broadcast_to(1.0 / row_total, summed.shape)))
        first = lane < DH
        result = jnp.where(first, parts[0][0], parts[1][0])
        exact[rows, :] = result
        inverse[rows, :] = jnp.where(first, parts[0][1], parts[1][1])
        held[rows, :] = result.astype(BF16)

    @pl.loop(0, tiles)
    def restore(index):
        context[tile_rows(index), :] = put_back(order_col, held, index)


def attend_back_kernel(
    low, high, offsets, order_row, order_col, table, ordered, exact, inverse, incoming,
    outgoing, slanted,
    query_aug, key_aug, value_aug, grad_aug, grad_plain, key_turned,
    strip, gathered, query_turned, key_sum, value_sum, held,
):
    rows_all = ordered.shape[0]
    tiles = rows_all // TILE
    reach = strip.shape[2] // TILE // 2
    lane = lane_of(TILE)
    fill_strip(strip, table)
    gathered[...] = jnp.zeros(gathered.shape, F32)
    key_sum[...] = jnp.zeros(key_sum.shape, F32)
    value_sum[...] = jnp.zeros(value_sum.shape, F32)

    @pl.loop(0, tiles)
    def arrange(index):
        rows = tile_rows(index)
        block = ordered[rows, :].astype(F32)
        sequence = sequence_of(offsets, index * TILE)
        arrived = put_in_order(order_row, incoming, index)
        scaled = arrived * inverse[rows, :]
        grad_plain[rows, :] = scaled.astype(BF16)
        product = scaled * exact[rows, :]
        key_turned[:, rows] = block[:, PAIR : 2 * PAIR].T.astype(BF16)
        for head in range(2):
            own, spare = head_lanes(lane, head)
            query, key = score_operands(
                block[:, :PAIR], block[:, PAIR : 2 * PAIR], sequence, head
            )
            query_aug[head, rows, :] = query
            key_aug[head, rows, :] = key
            value_aug[head, rows, :] = jnp.where(
                own, block[:, 2 * PAIR :], jnp.where(spare < 2, 1.0, 0.0)
            ).astype(BF16)
            shift = -jnp.sum(jnp.where(own, product, 0.0), axis=1, keepdims=True)
            coarse = shift.astype(BF16).astype(F32)
            fine = shift - coarse
            extra = jnp.where(spare == 0, coarse, jnp.where(spare == 1, fine, 0.0))
            grad_aug[head, rows, :] = jnp.where(own, scaled, extra).astype(BF16)

    @pl.loop(0, tiles)
    def attend(index):
        rows = tile_rows(index)
        query_turned[...] = jnp.zeros(query_turned.shape, F32)

        @pl.loop(low[index], high[index])
        def keys(other):
            columns = tile_rows(other)
            place = tile_rows(index - other + reach)
            query_plain = ordered[rows, pl.ds(0, PAIR)]
            key_parts, value_parts = ([], [])
            for head in range(2):
                raw = dot_nt(key_aug[head, columns, :], query_aug[head, rows, :])
                weight = jnp.exp(raw + strip[head, :, place])
                slope = dot_nt(value_aug[head, columns, :], grad_aug[head, rows, :])
                score = weight * slope
                gathered[head, :, place] += score
                score = score.astype(BF16)
                key_parts.append(dot_f32(score, query_plain))
                value_parts.append(dot_f32(weight.astype(BF16), grad_plain[rows, :]))
                query_turned[pl.ds(head * DH, DH), :] += dot_f32(
                    key_turned[pl.ds(head * DH, DH), columns], score
                )
            first = lane < DH
            key_sum[columns, :] += jnp.where(first, key_parts[0], key_parts[1])
            value_sum[columns, :] += jnp.where(first, value_parts[0], value_parts[1])

        held[rows, pl.ds(0, PAIR)] = query_turned[...].T.astype(BF16)

    held[:, pl.ds(PAIR, PAIR)] = key_sum[...].astype(BF16)
    held[:, pl.ds(2 * PAIR, PAIR)] = value_sum[...].astype(BF16)

    @pl.loop(0, tiles)
    def restore(index):
        outgoing[tile_rows(index), :] = put_back(order_col, held, index)

    width = gathered.shape[2]
    for head in range(2):
        folded = gathered[head]
        size = TILE // 2
        while size >= 8:
            folded = folded[:size] + pltpu.roll(folded[size:], width - size, 1)
            size //= 2
        slanted[head] = folded


def group_attention(low, high, offsets, order_row, order_col, table, mixed):
    rows = mixed.shape[0]
    smem = pl.BlockSpec(memory_space=pltpu.SMEM)
    vmem = pl.BlockSpec(memory_space=pltpu.VMEM)
    width = table.shape[1]
    return pl.pallas_call(
        attend_kernel,
        out_shape=(
            jax.ShapeDtypeStruct((rows, 3 * PAIR), BF16),
            jax.ShapeDtypeStruct((rows, PAIR), BF16),
            jax.ShapeDtypeStruct((rows, PAIR), F32),
            jax.ShapeDtypeStruct((rows, PAIR), F32),
            jax.ShapeDtypeStruct((2, 8, TILE), F32),
        ),
        in_specs=[smem] * 3 + [vmem] * 4,
        out_specs=(vmem,) * 5,
        scratch_shapes=[
            pltpu.VMEM((2, rows, PAIR), BF16),
            pltpu.VMEM((2, rows, PAIR), BF16),
            pltpu.VMEM((2, rows, PAIR), BF16),
            pltpu.VMEM((2, TILE, width), F32),
            pltpu.VMEM((2, TILE, PAIR), F32),
            pltpu.VMEM((rows, PAIR), BF16),
        ],
        name="attend",
        compiler_params=pltpu.CompilerParams(vmem_limit_bytes=40 << 20),
        cost_estimate=pl.CostEstimate(
            flops=37_000_000_000, bytes_accessed=8_000_000, transcendentals=5_000_000
        ),
    )(low, high, offsets, order_row, order_col, table, mixed)


def group_attention_back(
    low, high, offsets, order_row, order_col, table, ordered, exact, inverse, incoming
):
    rows = ordered.shape[0]
    smem = pl.BlockSpec(memory_space=pltpu.SMEM)
    vmem = pl.BlockSpec(memory_space=pltpu.VMEM)
    width = table.shape[1]
    return pl.pallas_call(
        attend_back_kernel,
        out_shape=(
            jax.ShapeDtypeStruct((rows, 3 * PAIR), BF16),
            jax.ShapeDtypeStruct((2, 8, width), F32),
        ),
        in_specs=[smem] * 3 + [vmem] * 7,
        out_specs=(vmem,) * 2,
        scratch_shapes=[
            pltpu.VMEM((2, rows, PAIR), BF16),
            pltpu.VMEM((2, rows, PAIR), BF16),
            pltpu.VMEM((2, rows, PAIR), BF16),
            pltpu.VMEM((2, rows, PAIR), BF16),
            pltpu.VMEM((rows, PAIR), BF16),
            pltpu.VMEM((PAIR, rows), BF16),
            pltpu.VMEM((2, TILE, width), F32),
            pltpu.VMEM((2, TILE, width), F32),
            pltpu.VMEM((PAIR, TILE), F32),
            pltpu.VMEM((rows, PAIR), F32),
            pltpu.VMEM((rows, PAIR), F32),
            pltpu.VMEM((rows, 3 * PAIR), BF16),
        ],
        name="attend_back",
        compiler_params=pltpu.CompilerParams(vmem_limit_bytes=50 << 20),
        cost_estimate=pl.CostEstimate(
            flops=45_000_000_000, bytes_accessed=12_000_000, transcendentals=5_000_000
        ),
    )(low, high, offsets, order_row, order_col, table, ordered, exact, inverse, incoming)


def sequence_plan(lengths, rows):
    offsets = jnp.cumsum(lengths) - lengths
    ends = offsets + lengths
    starts_at = jnp.arange(rows // TILE, dtype=jnp.int32) * TILE
    seq_first = jnp.sum((starts_at[:, None] >= offsets[None, :]).astype(jnp.int32), axis=1) - 1
    seq_last = (
        jnp.sum((starts_at[:, None] + TILE - 1 >= offsets[None, :]).astype(jnp.int32), axis=1) - 1
    )
    picks = jnp.arange(lengths.shape[0], dtype=jnp.int32)[None, :]
    low = jnp.sum(jnp.where(seq_first[:, None] == picks, offsets[None, :], 0), axis=1) // TILE
    high = jnp.sum(jnp.where(seq_last[:, None] == picks, ends[None, :], 0), axis=1)
    return (low, (high + TILE - 1) // TILE, offsets)


def bias_tables(rel_buckets, bias_pair):
    table_len = rel_buckets.shape[0]
    reach = (table_len + 1) // 2 // TILE
    width = (2 * reach + 1) * TILE
    hot = (rel_buckets[None, :] == jnp.arange(NB, dtype=jnp.int32)[:, None]).astype(BF16)
    table = dot_tn(bias_pair, hot)
    pad = ((0, 0), (0, width - table_len))
    return (jnp.pad(table, pad), jnp.pad(table[:, ::-1], pad))


def bucket_sums(rel_buckets, slanted):
    table_len = rel_buckets.shape[0]
    width = slanted.shape[2]
    total = jnp.zeros((2, table_len), F32)
    for row in range(8):
        total = total + slanted[:, row, row + 1 : row + 1 + table_len]
    hot = (rel_buckets[::-1][:, None] == jnp.arange(NB, dtype=jnp.int32)[None, :]).astype(F32)
    return jnp.dot(total, hot, precision=lax.Precision.HIGHEST, preferred_element_type=F32)


def blank_arrays(shapes):
    def leave(*refs):
        pass

    return pl.pallas_call(
        leave,
        out_shape=tuple(jax.ShapeDtypeStruct(shape, F32) for shape in shapes),
        out_specs=tuple(pl.BlockSpec(memory_space=pl.ANY) for shape in shapes),
        name="blank",
    )()


def fold_kernel(chunk, *refs):
    *sources, sent = refs
    got = sources.pop(0) if len(sources) == 4 else None
    start = 0
    for source in sources:
        rows = source.shape[0]
        for band in range(source.shape[1] // BAND):
            value = source[:, band * BAND : (band + 1) * BAND]
            place = pl.ds(start, rows)
            if got is not None:
                value = (value.astype(F32) + got[place, :].astype(F32)).astype(BF16)
            sent[place, :] = value
            start += rows


def spread_kernel(chunk, message, *refs):
    start = 0
    for result in refs[-3:]:
        rows = result.shape[0]
        for band in range(result.shape[1] // BAND):
            result[:, band * BAND : (band + 1) * BAND] = message[pl.ds(start, rows), :].astype(F32)
            start += rows


def whole_spec(shape):
    return pl.BlockSpec(shape, lambda step, chunk: (0,) * len(shape))


def row_spec(rows, width, first):
    return pl.BlockSpec((rows, width), lambda step, chunk: (chunk[0] + first, 0))


def fold_chunk(chunk, parts, got):
    rows = sum(count * array_in.shape[1] // BAND for array_in, count, first, item in parts)
    return pl.pallas_call(
        fold_kernel,
        grid_spec=pltpu.PrefetchScalarGridSpec(
            num_scalar_prefetch=1,
            grid=(1,),
            in_specs=[whole_spec((rows, BAND))] * len(got)
            + [row_spec(count, array_in.shape[1], first) for array_in, count, first, item in parts],
            out_specs=whole_spec((rows, BAND)),
        ),
        out_shape=jax.ShapeDtypeStruct((rows, BAND), BF16),
        name="fold",
        cost_estimate=pl.CostEstimate(flops=0, bytes_accessed=6 * rows * BAND, transcendentals=0),
    )(chunk.reshape(1), *got, *[array_in for array_in, count, first, item in parts])


def spread_chunk(chunk, message, parts, results):
    rows = message.shape[0]
    kept = [pl.BlockSpec(memory_space=pl.ANY)] * len(results)
    return pl.pallas_call(
        spread_kernel,
        grid_spec=pltpu.PrefetchScalarGridSpec(
            num_scalar_prefetch=1,
            grid=(1,),
            in_specs=[whole_spec((rows, BAND))] + kept,
            out_specs=tuple(
                row_spec(count, array_in.shape[1], first) for array_in, count, first, item in parts
            ),
        ),
        out_shape=tuple(jax.ShapeDtypeStruct(array_in.shape, F32) for array_in, count, first, item in parts),
        input_output_aliases={2 + item: item for item in range(len(results))},
        name="spread",
        cost_estimate=pl.CostEstimate(flops=0, bytes_accessed=6 * rows * BAND, transcendentals=0),
    )(chunk.reshape(1), message, *results)


def heads_kernel(chunk, message, *refs):
    for item, result in enumerate(refs[-3:]):
        result[...] = message[:, item * PAIR : (item + 1) * PAIR].astype(F32)


def spread_heads(chip, message, results):
    rows, parts = message.shape[0], len(RING)
    shape = jax.ShapeDtypeStruct((rows, parts * PAIR), F32)
    spec = pl.BlockSpec((rows, PAIR), lambda step, chunk: (0, chunk[0]))
    return pl.pallas_call(
        heads_kernel,
        grid_spec=pltpu.PrefetchScalarGridSpec(
            num_scalar_prefetch=1,
            grid=(1,),
            in_specs=[whole_spec(message.shape)]
            + [pl.BlockSpec(memory_space=pl.ANY)] * len(results),
            out_specs=(spec,) * 3,
        ),
        out_shape=(shape,) * 3,
        input_output_aliases={2 + item: item for item in range(len(results))},
        name="spread_heads",
        cost_estimate=pl.CostEstimate(flops=0, bytes_accessed=6 * message.size, transcendentals=0),
    )(chip.reshape(1), message, *results)


def tie(*values):
    return lax.optimization_barrier(values)


def ring_pairs(way):
    count = len(RING)
    return [(RING[i], RING[(i + way) % count]) for i in range(count)]


def ring_place():
    return look_up([RING.index(c) for c in range(len(RING))], lax.axis_index("ctx"))


def ring_chip(place):
    return look_up(RING, jnp.mod(place, len(RING)))


def tiny_gather(values):
    sent = jnp.broadcast_to(values[None], (len(RING),) + values.shape)
    return lax.all_to_all(sent, "ctx", 0, 0, tiled=True)


class RingSum:
    def __init__(self, ahead, back, results):
        self.flows = [(ahead, 1), (back, -1)]
        self.me = ring_place()
        self.step = 0
        self.results = list(results)
        self.arrived = None
        self.ready = [fold_chunk(self.me, parts, []) for parts, way in self.flows]

    @property
    def done(self):
        return self.step == 2 * (len(RING) - 1)

    def send(self):
        if self.done:
            return
        self.arrived = [
            lax.ppermute(held, "ctx", ring_pairs(way))
            for held, (parts, way) in zip(self.ready, self.flows)
        ]

    def absorb(self):
        if self.done:
            return
        self.step += 1
        for index, (parts, way) in enumerate(self.flows):
            chunk = jnp.mod(self.me - way * self.step, len(RING))
            got = self.arrived[index]
            self.ready[index] = (
                fold_chunk(chunk, parts, [got]) if self.step < len(RING) else got
            )

    def place(self):
        if self.step < len(RING) - 1:
            return
        for index, (parts, way) in enumerate(self.flows):
            chunk = jnp.mod(self.me - way * self.step, len(RING))
            ids = [part[3] for part in parts]
            written = spread_chunk(
                chunk, self.ready[index], parts, [self.results[item] for item in ids]
            )
            for item, result in zip(ids, written):
                self.results[item] = result


class RingGather:
    def __init__(self, block):
        self.me = ring_place()
        self.step = 0
        self.ready = (block, block)
        self.arrived = None
        self.results = ()
        self.found = [(lax.axis_index("ctx"), block)]

    def send(self):
        if self.step == len(RING) // 2:
            return
        self.step += 1
        ahead, back = self.ready
        ahead = lax.ppermute(ahead, "ctx", ring_pairs(1))
        if self.step < len(RING) // 2:
            back = lax.ppermute(back, "ctx", ring_pairs(-1))
        self.arrived = (ahead, back)

    def absorb(self):
        if len(self.found) == len(RING):
            return
        self.ready = self.arrived
        self.found.append((ring_chip(self.me - self.step), self.arrived[0]))
        if self.step < len(RING) // 2:
            self.found.append((ring_chip(self.me + self.step), self.arrived[1]))

    def place(self):
        pass


class HeadRing(RingGather):
    def __init__(self, block, results):
        super().__init__(block)
        self.results = results
        self.placed = 0

    def place(self):
        for chip, block in self.found[self.placed :]:
            self.results = spread_heads(chip, block, self.results)
        self.placed = len(self.found)


def stage(values, *rings):
    values, arrived = tie(values, [(ring.arrived, ring.results) for ring in rings])
    for ring, blocks in zip(rings, arrived):
        ring.arrived, ring.results = blocks
        ring.absorb()
    values, ready = tie(values, [ring.ready for ring in rings])
    for ring, blocks in zip(rings, ready):
        ring.ready = blocks
        ring.send()
        ring.place()
    return values


def per_device_ring(
    tokens,
    cotangent,
    token_order,
    seq_lengths,
    rel_buckets,
    gain_attn,
    w_query,
    w_key,
    w_value,
    w_out,
    rel_bias,
    gain_ffn,
    w_gate,
    w_up,
    w_down,
):
    core = lax.axis_index("fsdp")
    ctx = lax.axis_index("ctx")
    tp = lax.axis_index("tp")
    local_rows = tokens.shape[0]
    half = w_query.shape[0]
    head_count = w_query.shape[1] // DH
    group_rows = local_rows * lax.axis_size("ctx")
    first = core == 0

    def halves(array_in):
        left, right = (array_in[:, :half], array_in[:, half:])
        return (jnp.where(first, left, right), jnp.where(first, right, left))

    def whole(own, other):
        return jnp.concatenate(
            [jnp.where(first, own, other), jnp.where(first, other, own)], axis=1
        )

    small = jnp.concatenate([gain_attn, gain_ffn, rel_bias.reshape(-1)])
    small_far = swap(small, "fsdp")
    wq_far, wk_far, wv_far = (swap(w_query, "fsdp"), swap(w_key, "fsdp"), swap(w_value, "fsdp"))
    wo_far = swap(w_out, "fsdp")
    wg_far, wu_far, wd_far = (swap(w_gate, "fsdp"), swap(w_up, "fsdp"), swap(w_down, "fsdp"))
    ga_own, ga_far = (gain_attn.astype(F32), small_far[:half].astype(F32))
    gf_own, gf_far = (gain_ffn.astype(F32), small_far[half : 2 * half].astype(F32))
    bias_far = small_far[2 * half :].reshape(rel_bias.shape)
    bias_local = jnp.where(
        first,
        jnp.concatenate([rel_bias, bias_far]),
        jnp.concatenate([bias_far, rel_bias]),
    )
    tok_own, tok_far = halves(tokens)
    cot_own, cot_far = halves(cotangent)
    tok_own, tok_far = (tok_own.astype(F32), tok_far.astype(F32))

    def norm_scale(own, far):
        total = jnp.sum(own * own, axis=1, keepdims=True) + jnp.sum(far * far, axis=1, keepdims=True)
        return lax.rsqrt(total / (2 * half) + EPS)

    scale_a = norm_scale(tok_own, tok_far)
    normed_own = (tok_own * scale_a * ga_own).astype(BF16)
    normed_far = (tok_far * scale_a * ga_far).astype(BF16)
    queries = (dot_f32(normed_own, w_query) + dot_f32(normed_far, wq_far)).astype(BF16)
    keys_here = (dot_f32(normed_own, w_key) + dot_f32(normed_far, wk_far)).astype(BF16)
    values_here = (dot_f32(normed_own, w_value) + dot_f32(normed_far, wv_far)).astype(BF16)
    parts = lax.axis_size("ctx")

    def by_heads(items):
        mixed = jnp.concatenate([item.reshape(local_rows, parts, 1, PAIR) for item in items], axis=2)
        mixed = jnp.transpose(mixed.reshape(local_rows, parts, len(items) * PAIR), (1, 0, 2))
        moved = lax.all_to_all(mixed, "ctx", 0, 0, tiled=True)
        return moved.reshape(group_rows, len(items) * PAIR)

    def by_rows(array_in):
        count = array_in.shape[1] // PAIR
        moved = lax.all_to_all(
            array_in.reshape(parts, local_rows, count * PAIR), "ctx", 0, 0, tiled=True
        )
        moved = jnp.transpose(moved.reshape(parts, local_rows, count, PAIR), (2, 1, 0, 3))
        return moved.reshape(count, local_rows, parts * PAIR)

    order_row = token_order
    order_col = token_order.reshape(group_rows, 1)
    low, high, offsets = sequence_plan(seq_lengths[0], group_rows)
    bias_pair = lax.dynamic_slice_in_dim(bias_local, ctx * 2, 2, axis=1)
    table, table_back = bias_tables(rel_buckets, bias_pair)
    mixed = by_heads([queries, keys_here, values_here])
    mixed, normed_block = tie(mixed, jnp.concatenate([normed_own, normed_far], axis=1))
    normed_ring = RingGather(normed_block)
    normed_ring.send()
    ordered, context_heads, exact, inverse, tops = group_attention(
        low, high, offsets, order_row, order_col, table, mixed
    )
    context_heads, normed_ring.arrived = tie(context_heads, normed_ring.arrived)
    normed_ring.absorb()
    context = by_rows(context_heads)[0]
    context, normed_ring.ready = tie(context, normed_ring.ready)
    normed_ring.send()

    def tp_sum(own, far):
        own, far = (own.astype(BF16), far.astype(BF16))
        return (
            own.astype(F32) + swap(own, "tp").astype(F32),
            far.astype(F32) + swap(far, "tp").astype(F32),
        )

    attn_own, attn_far = tp_sum(dot_f32(context, w_out), dot_f32(context, wo_far))
    attn_own, attn_far = stage((attn_own, attn_far), normed_ring)
    hid_own, hid_far = (tok_own + attn_own, tok_far + attn_far)
    inner_grad = dot_nt(cot_own, w_down) + dot_nt(cot_far, wd_far)
    scale_f = norm_scale(hid_own, hid_far)
    nffn_own = (hid_own * scale_f * gf_own).astype(BF16)
    nffn_far = (hid_far * scale_f * gf_far).astype(BF16)
    gate_pre = dot_f32(nffn_own, w_gate) + dot_f32(nffn_far, wg_far)
    up_pre = dot_f32(nffn_own, w_up) + dot_f32(nffn_far, wu_far)
    inner_act = geglu(gate_pre, up_pre).astype(BF16)
    unused, geglu_back = jax.vjp(geglu, gate_pre, up_pre)
    gate_grad, up_grad = geglu_back(inner_grad)
    gate_grad = gate_grad.astype(BF16)
    up_grad = up_grad.astype(BF16)
    gate_grad, up_grad, inner_act = stage((gate_grad, up_grad, inner_act), normed_ring)
    dnf_own, dnf_far = tp_sum(
        dot_nt(gate_grad, w_gate) + dot_nt(up_grad, w_up),
        dot_nt(gate_grad, wg_far) + dot_nt(up_grad, wu_far),
    )

    def pair_rows(own):
        return jnp.concatenate([own, swap(own, "fsdp")])

    def pair_half(own, far):
        return jnp.concatenate([own, swap(far, "fsdp")])

    nffn_pair = pair_half(nffn_own, nffn_far)
    grad_gate = dot_tn(nffn_pair, pair_rows(gate_grad)).astype(BF16)
    grad_up = dot_tn(nffn_pair, pair_rows(up_grad)).astype(BF16)
    grad_down = dot_tn(pair_rows(inner_act), pair_half(cot_own, cot_far)).astype(BF16)
    def norm_back(own, far, scale, gain_own, gain_far, dy_own, dy_far):
        mean_term = (
            jnp.sum(gain_own * dy_own * own, axis=1, keepdims=True)
            + jnp.sum(gain_far * dy_far * far, axis=1, keepdims=True)
        ) / (2 * half)
        cubed = scale * scale * scale * mean_term
        return (
            scale * (gain_own * dy_own) - own * cubed,
            scale * (gain_far * dy_far) - far * cubed,
            jnp.sum(dy_own * own * scale, axis=0),
            jnp.sum(dy_far * far * scale, axis=0),
        )

    back_own, back_far, dgf_own, dgf_far = norm_back(
        hid_own, hid_far, scale_f, gf_own, gf_far, dnf_own, dnf_far
    )
    hgrad_own = cot_own.astype(F32) + back_own
    hgrad_far = cot_far.astype(F32) + back_far
    ag_own, ag_far = (hgrad_own.astype(BF16), hgrad_far.astype(BF16))
    grad_out = dot_tn(pair_rows(context), pair_half(ag_own, ag_far)).astype(BF16)
    context_grad = dot_nt(ag_own, w_out) + dot_nt(ag_far, wo_far)
    grad_rows = grad_gate.shape[0] // len(RING)
    down_rows = grad_down.shape[0] // (2 * len(RING))
    out_rows = w_out.shape[0] // (2 * len(RING))
    blanks = blank_arrays(
        [grad_gate.shape, grad_up.shape, grad_down.shape, grad_out.shape] + [w_query.shape] * 3
    )
    context_grad, grad_out = stage((context_grad.astype(BF16), grad_out), normed_ring)
    ring = RingSum(
        [
            (grad_gate, grad_rows, 0, 0),
            (grad_down, down_rows, 0, 2),
            (grad_out, out_rows, 0, 3),
        ],
        [
            (grad_up, grad_rows, 0, 1),
            (grad_down, down_rows, len(RING), 2),
            (grad_out, out_rows, len(RING), 3),
        ],
        blanks[:4],
    )
    ring.send()
    grad_mixed = by_heads([context_grad])
    grad_mixed = stage(grad_mixed, ring)
    outgoing, slanted = group_attention_back(
        low, high, offsets, order_row, order_col, table_back, ordered, exact, inverse, grad_mixed
    )
    outgoing, found, tops, inner_act = stage(
        (outgoing, [blocks for chip, blocks in normed_ring.found], tops, inner_act),
        ring,
    )
    query_grad, key_grad, value_grad = by_rows(outgoing)
    outgoing_turned = jnp.concatenate(
        [
            lax.dynamic_slice_in_dim(outgoing, chip * local_rows, local_rows)
            for chip, blocks in normed_ring.found
        ]
    )
    head_grads = dot_tn(jnp.concatenate(found), outgoing_turned)
    head_grads, head_grads_sent = (head_grads[:half], head_grads[half:].astype(BF16))
    head_grads = (head_grads + swap(head_grads_sent, "fsdp").astype(F32)).astype(BF16)
    dn_parts = (
        dot_nt(query_grad, w_query) + dot_nt(key_grad, w_key) + dot_nt(value_grad, w_value),
        dot_nt(query_grad, wq_far) + dot_nt(key_grad, wk_far) + dot_nt(value_grad, wv_far),
    )
    dn_parts = (dn_parts[0].astype(BF16), dn_parts[1].astype(BF16))
    head_grads, dn_parts = stage((head_grads, dn_parts), ring)
    head_ring = HeadRing(head_grads, blanks[4:])
    head_ring.send()
    head_ring.place()
    dn_own, dn_far = tp_sum(*dn_parts)
    dn_own, dn_far = stage((dn_own, dn_far), ring, head_ring)
    tback_own, tback_far, dga_own, dga_far = norm_back(
        tok_own, tok_far, scale_a, ga_own, ga_far, dn_own, dn_far
    )
    grad_tokens = whole(hgrad_own + tback_own, hgrad_far + tback_far)
    ffn_own, ffn_far = tp_sum(dot_f32(inner_act, w_down), dot_f32(inner_act, wd_far))
    output = whole(hid_own + ffn_own, hid_far + ffn_far).astype(BF16)
    grad_tokens, output, dga_own, dga_far, tops = stage(
        (grad_tokens, output, dga_own, dga_far, tops), ring, head_ring
    )
    pair_top = jnp.max(tops, axis=(1, 2))
    pair_top = jnp.maximum(pair_top, swap(pair_top, "fsdp"))
    here = jnp.arange(parts, dtype=jnp.int32)[:, None] == ctx
    head_maxima = tiny_gather(pair_top).reshape(head_count)
    pair_bias = bucket_sums(rel_buckets, slanted)
    grad_bias = jnp.transpose(
        jnp.where(here[:, :, None], pair_bias[None], 0.0).reshape(head_count, NB)
    )
    small_own = jnp.concatenate([dga_own, dgf_own])
    small_sent = jnp.concatenate([dga_far, dgf_far])
    bias_flat = grad_bias.reshape(2, -1)
    small_own = jnp.concatenate([small_own, jnp.where(first, bias_flat[0], bias_flat[1])])
    small_sent = jnp.concatenate([small_sent, jnp.where(first, bias_flat[1], bias_flat[0])])
    small_sum = jnp.sum(tiny_gather(small_own + swap(small_sent, "fsdp")), axis=0)
    final_gain_a, final_gain_f = (small_sum[:half], small_sum[half : 2 * half])
    final_bias = small_sum[2 * half :].reshape(rel_bias.shape)
    clip_scale = TAU_CLIP / jnp.maximum(head_maxima, TAU_CLIP)
    column_scale = jnp.repeat(jnp.sqrt(clip_scale), DH)
    query_clipped = (w_query.astype(F32) * column_scale[None, :]).astype(BF16)
    key_clipped = (w_key.astype(F32) * column_scale[None, :]).astype(BF16)
    others = (
        grad_tokens,
        output,
        final_gain_a,
        final_gain_f,
        final_bias,
        head_maxima,
        query_clipped,
        key_clipped,
    )
    while not ring.done:
        stage((), ring, head_ring)
        if ring.step == len(RING) + 1:
            others, ring.arrived = tie(others, ring.arrived)
    final_gate, final_up, final_down, final_out = ring.results
    final_query, final_key, final_value = head_ring.results
    (
        grad_tokens,
        output,
        final_gain_a,
        final_gain_f,
        final_bias,
        head_maxima,
        query_clipped,
        key_clipped,
    ) = others
    return (
        output,
        grad_tokens,
        final_gain_a,
        final_query,
        final_key,
        final_value,
        final_out,
        final_bias,
        final_gain_f,
        final_gate,
        final_up,
        final_down,
        head_maxima,
        query_clipped,
        key_clipped,
    )


def pick_program(mesh):
    sizes = dict(mesh.shape)
    if sizes["fsdp"] == 2 and sizes["ctx"] == len(RING) and sizes["tp"] == 2:
        return per_device_ring
    return per_device_generic


def solution(mesh):
    in_specs = (
        P(("fsdp", "ctx"), None),
        P(("fsdp", "ctx"), None),
        P("fsdp", None),
        P("fsdp", None),
        P(),
        P("fsdp"),
        P("fsdp", "tp"),
        P("fsdp", "tp"),
        P("fsdp", "tp"),
        P("tp", "fsdp"),
        P("fsdp", "tp"),
        P("fsdp"),
        P("fsdp", "tp"),
        P("fsdp", "tp"),
        P("tp", "fsdp"),
    )
    out_specs = (
        P(("fsdp", "ctx"), None),
        P(("fsdp", "ctx"), None),
        P("fsdp"),
        P("fsdp", "tp"),
        P("fsdp", "tp"),
        P("fsdp", "tp"),
        P("tp", "fsdp"),
        P("fsdp", "tp"),
        P("fsdp"),
        P("fsdp", "tp"),
        P("fsdp", "tp"),
        P("tp", "fsdp"),
        P("tp"),
        P("fsdp", "tp"),
        P("fsdp", "tp"),
    )
    per_device = pick_program(mesh)
    return jax.shard_map(
        per_device, mesh=mesh, in_specs=in_specs, out_specs=out_specs, check_vma=False
    )
```

```python
import functools

import jax
import jax.numpy as jnp
from jax import lax
from jax.experimental import pallas as pl
from jax.experimental.pallas import tpu as pltpu
from jax.sharding import PartitionSpec as P

DH = 64
NB = 32


EPS = 1e-06
TAU_CLIP = 6.0


def rms_norm(values, gain):
    return values * lax.rsqrt(jnp.mean(values * values, axis=-1, keepdims=True) + EPS) * gain


def geglu(gate_pre, up_pre):
    return jax.nn.gelu(gate_pre, approximate=True) * up_pre


def segment_of(positions, lengths_row):
    offsets = jnp.cumsum(lengths_row) - lengths_row
    return jnp.sum((positions[:, None] >= offsets[None, :]).astype(jnp.int32), axis=1) - 1


def bucket_ranges(rel_buckets):
    table_len = rel_buckets.shape[0]
    index_all = jnp.arange(table_len, dtype=jnp.int32)
    bucket_ids = jnp.arange(NB, dtype=jnp.int32)
    matched = rel_buckets[:, None] == bucket_ids[None, :]
    range_first = jnp.min(jnp.where(matched, index_all[:, None], table_len), axis=0)
    range_last = jnp.max(jnp.where(matched, index_all[:, None], -1), axis=0)
    return (range_first, range_last, table_len)


def pair_terms(query_pos, query_seg, key_pos, key_seg, ranges, bias_table):
    range_first, range_last, table_len = ranges
    longest = (table_len + 1) // 2
    offset = jnp.clip(key_pos[None, :] - query_pos[:, None] + longest - 1, 0, 2 * longest - 2)
    inside = (offset[None, :, :] >= range_first[:, None, None]) & (
        offset[None, :, :] <= range_last[:, None, None]
    )
    bucket_hot = inside.astype(jnp.bfloat16)
    pair_bias = jnp.einsum(
        "btk,bh->htk", bucket_hot, bias_table, preferred_element_type=jnp.float32
    )
    same_seq = (query_seg[:, None] == key_seg[None, :])[None]
    return (bucket_hot, pair_bias, same_seq)


def per_device_generic(
    tokens,
    cotangent,
    token_order,
    seq_lengths,
    rel_buckets,
    gain_attn,
    w_query,
    w_key,
    w_value,
    w_out,
    rel_bias,
    gain_ffn,
    w_gate,
    w_up,
    w_down,
):
    local_rows = tokens.shape[0]
    head_count = w_query.shape[1] // DH
    group_rows = local_rows * lax.axis_size("ctx")
    key_block = min(512, group_rows)
    block_count = group_rows // key_block
    ranges = bucket_ranges(rel_buckets)
    gain_a, full_query, full_key, full_value, full_out, bias_local = (
        lax.all_gather(gain_attn, "fsdp", axis=0, tiled=True),
        lax.all_gather(w_query, "fsdp", axis=0, tiled=True),
        lax.all_gather(w_key, "fsdp", axis=0, tiled=True),
        lax.all_gather(w_value, "fsdp", axis=0, tiled=True),
        lax.all_gather(w_out, "fsdp", axis=1, tiled=True),
        lax.all_gather(rel_bias, "fsdp", axis=0, tiled=True),
    )
    tokens_f = tokens.astype(jnp.float32)
    gain_a32 = gain_a.astype(jnp.float32)
    normed = rms_norm(tokens_f, gain_a32).astype(jnp.bfloat16)
    queries = jnp.dot(normed, full_query, preferred_element_type=jnp.float32).astype(jnp.bfloat16)
    keys_here = jnp.dot(normed, full_key, preferred_element_type=jnp.float32).astype(jnp.bfloat16)
    values_here = jnp.dot(normed, full_value, preferred_element_type=jnp.float32).astype(
        jnp.bfloat16
    )
    order_row = token_order[0]
    seq_ids = segment_of(order_row, seq_lengths[0])
    row_start = lax.axis_index("ctx") * local_rows
    query_pos = lax.dynamic_slice_in_dim(order_row, row_start, local_rows)
    query_seg = lax.dynamic_slice_in_dim(seq_ids, row_start, local_rows)
    pos_blocks = order_row.reshape(block_count, key_block)
    seg_blocks = seq_ids.reshape(block_count, key_block)
    query_heads = queries.reshape(local_rows, head_count, DH)
    key_all, value_all = (
        lax.all_gather(keys_here, "ctx", axis=0, tiled=True),
        lax.all_gather(values_here, "ctx", axis=0, tiled=True),
    )

    def blocked(array_in):
        return array_in.reshape(block_count, key_block, head_count, DH)

    def forward_block(running, inputs):
        summed, totals, head_top = running
        key_blk, value_blk, pos_blk, seg_blk = inputs
        raw_scores = jnp.einsum(
            "thd,khd->htk", query_heads, key_blk, preferred_element_type=jnp.float32
        )
        bucket_hot, pair_bias, same_seq = pair_terms(
            query_pos, query_seg, pos_blk, seg_blk, ranges, bias_local
        )
        weights = jnp.where(same_seq, jnp.exp(raw_scores + pair_bias), 0.0)
        totals = totals + jnp.sum(weights, axis=2)
        summed = summed + jnp.einsum(
            "htk,khd->thd",
            weights.astype(jnp.bfloat16),
            value_blk,
            preferred_element_type=jnp.float32,
        )
        head_top = jnp.maximum(
            head_top, jnp.max(jnp.where(same_seq, raw_scores, -1e30), axis=(1, 2))
        )
        return ((summed, totals, head_top), None)

    start_state = (
        jnp.zeros((local_rows, head_count, DH), jnp.float32),
        jnp.zeros((head_count, local_rows), jnp.float32),
        jnp.full((head_count,), -1e30, jnp.float32),
    )
    (summed, totals, head_top), unused = lax.scan(
        forward_block, start_state, (blocked(key_all), blocked(value_all), pos_blocks, seg_blocks)
    )
    row_totals = jnp.transpose(totals)[:, :, None]
    context_exact = summed / row_totals
    context = context_exact.reshape(local_rows, head_count * DH).astype(jnp.bfloat16)
    head_maxima = lax.pmax(head_top, ("fsdp", "ctx"))
    attn_out = lax.psum(
        jnp.dot(context, full_out, preferred_element_type=jnp.float32).astype(jnp.bfloat16), "tp"
    ).astype(jnp.float32)
    hidden_state = tokens_f + attn_out
    gain_f, full_gate, full_up, full_down = (
        lax.all_gather(gain_ffn, "fsdp", axis=0, tiled=True),
        lax.all_gather(w_gate, "fsdp", axis=0, tiled=True),
        lax.all_gather(w_up, "fsdp", axis=0, tiled=True),
        lax.all_gather(w_down, "fsdp", axis=1, tiled=True),
    )
    gain_f32 = gain_f.astype(jnp.float32)
    normed_ffn = rms_norm(hidden_state, gain_f32).astype(jnp.bfloat16)
    gate_pre = jnp.dot(normed_ffn, full_gate, preferred_element_type=jnp.float32)
    up_pre = jnp.dot(normed_ffn, full_up, preferred_element_type=jnp.float32)
    inner_act = geglu(gate_pre, up_pre).astype(jnp.bfloat16)
    ffn_out = lax.psum(
        jnp.dot(inner_act, full_down, preferred_element_type=jnp.float32).astype(jnp.bfloat16), "tp"
    ).astype(jnp.float32)
    output = (hidden_state + ffn_out).astype(jnp.bfloat16)
    grad_down = jnp.einsum("tf,td->fd", inner_act, cotangent, preferred_element_type=jnp.float32)
    inner_grad = jnp.einsum("td,fd->tf", cotangent, full_down, preferred_element_type=jnp.float32)
    unused, geglu_back = jax.vjp(geglu, gate_pre, up_pre)
    gate_grad, up_grad = geglu_back(inner_grad)
    gate_grad = gate_grad.astype(jnp.bfloat16)
    up_grad = up_grad.astype(jnp.bfloat16)
    grad_gate = jnp.einsum("tc,tf->cf", normed_ffn, gate_grad, preferred_element_type=jnp.float32)
    grad_up = jnp.einsum("tc,tf->cf", normed_ffn, up_grad, preferred_element_type=jnp.float32)
    ffn_term = jnp.einsum(
        "tf,cf->tc", gate_grad, full_gate, preferred_element_type=jnp.float32
    ) + jnp.einsum("tf,cf->tc", up_grad, full_up, preferred_element_type=jnp.float32)
    normed_ffn_grad = lax.psum(ffn_term.astype(jnp.bfloat16), "tp").astype(jnp.float32)
    unused, norm_ffn_back = jax.vjp(rms_norm, hidden_state, gain_f32)
    hidden_norm_grad, grad_gain_ffn = norm_ffn_back(normed_ffn_grad)
    hidden_grad = cotangent.astype(jnp.float32) + hidden_norm_grad
    attn_grad = hidden_grad.astype(jnp.bfloat16)
    grad_out = jnp.einsum("tc,td->cd", context, attn_grad, preferred_element_type=jnp.float32)
    context_grad = jnp.einsum(
        "td,cd->tc", attn_grad, full_out, preferred_element_type=jnp.float32
    ).reshape(local_rows, head_count, DH)
    summed_grad = (context_grad / row_totals).astype(jnp.bfloat16)
    total_grad = jnp.transpose(-jnp.sum(context_grad * context_exact, axis=2) / row_totals[:, :, 0])
    key_back, value_back = (key_all, value_all)

    def backward_block(running, inputs):
        query_acc, bias_acc = running
        key_blk, value_blk, pos_blk, seg_blk = inputs
        raw_scores = jnp.einsum(
            "thd,khd->htk", query_heads, key_blk, preferred_element_type=jnp.float32
        )
        bucket_hot, pair_bias, same_seq = pair_terms(
            query_pos, query_seg, pos_blk, seg_blk, ranges, bias_local
        )
        weights = jnp.where(same_seq, jnp.exp(raw_scores + pair_bias), 0.0)
        prob_grad = (
            jnp.einsum("thd,khd->htk", summed_grad, value_blk, preferred_element_type=jnp.float32)
            + total_grad[:, :, None]
        )
        score_grad = (weights * prob_grad).astype(jnp.bfloat16)
        query_acc = query_acc + jnp.einsum(
            "htk,khd->thd", score_grad, key_blk, preferred_element_type=jnp.float32
        )
        key_grad = jnp.einsum(
            "htk,thd->khd", score_grad, query_heads, preferred_element_type=jnp.float32
        )
        value_grad = jnp.einsum(
            "htk,thd->khd",
            weights.astype(jnp.bfloat16),
            summed_grad,
            preferred_element_type=jnp.float32,
        )
        bucket_sums = jnp.einsum(
            "htk,btk->hb", score_grad, bucket_hot, preferred_element_type=jnp.float32
        )
        return ((query_acc, bias_acc + bucket_sums), (key_grad, value_grad))

    zero_state = (
        jnp.zeros((local_rows, head_count, DH), jnp.float32),
        jnp.zeros((head_count, NB), jnp.float32),
    )
    (query_acc, bias_acc), (key_grads, value_grads) = lax.scan(
        backward_block, zero_state, (blocked(key_back), blocked(value_back), pos_blocks, seg_blocks)
    )
    key_grad_all, value_grad_all = (
        lax.psum_scatter(
            key_grads.reshape(group_rows, head_count * DH).astype(jnp.bfloat16),
            "ctx",
            scatter_dimension=0,
            tiled=True,
        ).astype(jnp.float32),
        lax.psum_scatter(
            value_grads.reshape(group_rows, head_count * DH).astype(jnp.bfloat16),
            "ctx",
            scatter_dimension=0,
            tiled=True,
        ).astype(jnp.float32),
    )
    query_grad = query_acc.reshape(local_rows, head_count * DH).astype(jnp.bfloat16)
    key_grad = key_grad_all.astype(jnp.bfloat16)
    value_grad = value_grad_all.astype(jnp.bfloat16)
    attn_term = jnp.einsum("tc,dc->td", query_grad, full_query, preferred_element_type=jnp.float32)
    attn_term = attn_term + jnp.einsum(
        "tc,dc->td", key_grad, full_key, preferred_element_type=jnp.float32
    )
    attn_term = attn_term + jnp.einsum(
        "tc,dc->td", value_grad, full_value, preferred_element_type=jnp.float32
    )
    normed_grad = lax.psum(attn_term.astype(jnp.bfloat16), "tp").astype(jnp.float32)
    unused, norm_attn_back = jax.vjp(rms_norm, tokens_f, gain_a32)
    token_norm_grad, grad_gain_attn = norm_attn_back(normed_grad)
    grad_tokens = hidden_grad + token_norm_grad
    grad_query = jnp.einsum("td,tc->dc", normed, query_grad, preferred_element_type=jnp.float32)
    grad_key = jnp.einsum("td,tc->dc", normed, key_grad, preferred_element_type=jnp.float32)
    grad_value = jnp.einsum("td,tc->dc", normed, value_grad, preferred_element_type=jnp.float32)
    grad_bias = jnp.transpose(bias_acc)
    (
        share_gain_a,
        share_query,
        share_key,
        share_value,
        share_out,
        share_bias,
        share_gain_f,
        share_gate,
        share_up,
        share_down,
    ) = (
        lax.psum_scatter(
            grad_gain_attn.astype(jnp.bfloat16), "fsdp", scatter_dimension=0, tiled=True
        ).astype(jnp.float32),
        lax.psum_scatter(
            grad_query.astype(jnp.bfloat16), "fsdp", scatter_dimension=0, tiled=True
        ).astype(jnp.float32),
        lax.psum_scatter(
            grad_key.astype(jnp.bfloat16), "fsdp", scatter_dimension=0, tiled=True
        ).astype(jnp.float32),
        lax.psum_scatter(
            grad_value.astype(jnp.bfloat16), "fsdp", scatter_dimension=0, tiled=True
        ).astype(jnp.float32),
        lax.psum_scatter(
            grad_out.astype(jnp.bfloat16), "fsdp", scatter_dimension=1, tiled=True
        ).astype(jnp.float32),
        lax.psum_scatter(
            grad_bias.astype(jnp.bfloat16), "fsdp", scatter_dimension=0, tiled=True
        ).astype(jnp.float32),
        lax.psum_scatter(
            grad_gain_ffn.astype(jnp.bfloat16), "fsdp", scatter_dimension=0, tiled=True
        ).astype(jnp.float32),
        lax.psum_scatter(
            grad_gate.astype(jnp.bfloat16), "fsdp", scatter_dimension=0, tiled=True
        ).astype(jnp.float32),
        lax.psum_scatter(
            grad_up.astype(jnp.bfloat16), "fsdp", scatter_dimension=0, tiled=True
        ).astype(jnp.float32),
        lax.psum_scatter(
            grad_down.astype(jnp.bfloat16), "fsdp", scatter_dimension=1, tiled=True
        ).astype(jnp.float32),
    )
    (
        final_gain_a,
        final_query,
        final_key,
        final_value,
        final_out,
        final_bias,
        final_gain_f,
        final_gate,
        final_up,
        final_down,
    ) = (
        lax.psum(share_gain_a.astype(jnp.bfloat16), "ctx").astype(jnp.float32),
        lax.psum(share_query.astype(jnp.bfloat16), "ctx").astype(jnp.float32),
        lax.psum(share_key.astype(jnp.bfloat16), "ctx").astype(jnp.float32),
        lax.psum(share_value.astype(jnp.bfloat16), "ctx").astype(jnp.float32),
        lax.psum(share_out.astype(jnp.bfloat16), "ctx").astype(jnp.float32),
        lax.psum(share_bias.astype(jnp.bfloat16), "ctx").astype(jnp.float32),
        lax.psum(share_gain_f.astype(jnp.bfloat16), "ctx").astype(jnp.float32),
        lax.psum(share_gate.astype(jnp.bfloat16), "ctx").astype(jnp.float32),
        lax.psum(share_up.astype(jnp.bfloat16), "ctx").astype(jnp.float32),
        lax.psum(share_down.astype(jnp.bfloat16), "ctx").astype(jnp.float32),
    )
    clip_scale = TAU_CLIP / jnp.maximum(head_maxima, TAU_CLIP)
    column_scale = jnp.repeat(jnp.sqrt(clip_scale), DH)
    query_clipped = (w_query.astype(jnp.float32) * column_scale[None, :]).astype(jnp.bfloat16)
    key_clipped = (w_key.astype(jnp.float32) * column_scale[None, :]).astype(jnp.bfloat16)
    return (
        output,
        grad_tokens,
        final_gain_a,
        final_query,
        final_key,
        final_value,
        final_out,
        final_bias,
        final_gain_f,
        final_gate,
        final_up,
        final_down,
        head_maxima,
        query_clipped,
        key_clipped,
    )


RING = (0, 2, 4, 6, 7, 5, 3, 1)
OUT_ROUND = 1
F32 = jnp.float32
BF16 = jnp.bfloat16


def look_up(table, index):
    found = jnp.int32(table[0])
    for place in range(1, len(table)):
        found = jnp.where(index == place, table[place], found)
    return found


def swap(array_in, axis_name):
    return lax.ppermute(array_in, axis_name, [(0, 1), (1, 0)])


def dot_f32(left, right):
    return jnp.dot(left, right, preferred_element_type=F32)


def dot_nt(left, right):
    return lax.dot_general(left, right, (((1,), (1,)), ((), ())), preferred_element_type=F32)


def dot_tn(left, right):
    return lax.dot_general(left, right, (((0,), (0,)), ((), ())), preferred_element_type=F32)


BAND = 512


TILE = 256
PAIR = 2 * DH
FAR_OFF = 1e30


def lane_of(rows):
    return lax.broadcasted_iota(jnp.int32, (rows, PAIR), 1)


def head_lanes(lane, head):
    own = lane < DH if head == 0 else lane >= DH
    spare = lane - DH if head == 0 else lane
    return (own, spare)


def sequence_of(offsets, start):
    position = start + lax.broadcasted_iota(jnp.int32, (TILE, PAIR), 0)
    sequence = jnp.zeros((TILE, PAIR), jnp.int32)
    for item in range(1, offsets.shape[0]):
        sequence = sequence + (position >= offsets[item]).astype(jnp.int32)
    return sequence


def tile_rows(index):
    return pl.ds(pl.multiple_of(index * TILE, TILE), TILE)


MOVED = 1024


def moved_rows(index):
    return pl.ds(pl.multiple_of(index * MOVED, MOVED), MOVED)


def put_in_order(order_row, source, target):
    @pl.loop(0, source.shape[0] // MOVED)
    def part(index):
        position = index * MOVED + lax.broadcasted_iota(jnp.int32, (MOVED, source.shape[0]), 0)
        hot = (order_row[...] == position).astype(F32).astype(BF16)
        target[moved_rows(index), :] = dot_f32(hot, source[...]).astype(BF16)


def put_back(order_col, source, target):
    @pl.loop(0, source.shape[0] // MOVED)
    def part(index):
        position = lax.broadcasted_iota(jnp.int32, (MOVED, source.shape[0]), 1)
        hot = (order_col[moved_rows(index), :] == position).astype(F32).astype(BF16)
        target[moved_rows(index), :] = dot_f32(hot, source[...]).astype(BF16)


def tile_pairs(low, high, tiles):
    pairs = (high - low + 1) // 2
    return (jnp.minimum(low, tiles - 2 * pairs), pairs)


def strip_place(distance, reach):
    return tile_rows(jnp.clip(distance + reach, 0, 2 * reach))


def fill_strip(strip, table):
    width = table.shape[1]
    for head in range(2):
        row = jnp.broadcast_to(table[pl.ds(head, 1), :], (TILE, width))
        strip[head] = pltpu.roll(row, 1, 1, stride=1, stride_axis=0)


def score_operands(query, key, sequence, head):
    own, spare = head_lanes(lane_of(TILE), head)
    differs = jnp.where((spare < 8) & (sequence != spare), 1.0, 0.0)
    blocked = jnp.where(sequence == spare, -FAR_OFF, 0.0)
    return (
        jnp.where(own, query, differs).astype(BF16),
        jnp.where(own, key, blocked).astype(BF16),
    )


def attend_kernel(
    low, high, offsets, order_row, order_col, table, mixed,
    ordered, context, exact, inverse, tops,
    query_aug, key_aug, value_aug, strip, total, held,
):
    tiles = mixed.shape[0] // TILE
    reach = strip.shape[2] // TILE // 2
    lane = lane_of(TILE)
    fill_strip(strip, table)
    put_in_order(order_row, mixed, ordered)
    tops[...] = jnp.full(tops.shape, -FAR_OFF, F32)

    @pl.loop(0, tiles)
    def arrange(index):
        rows = tile_rows(index)
        block = ordered[rows, :].astype(F32)
        sequence = sequence_of(offsets, index * TILE)
        for head in range(2):
            own, spare = head_lanes(lane, head)
            query, key = score_operands(
                block[:, :PAIR], block[:, PAIR : 2 * PAIR], sequence, head
            )
            query_aug[head, rows, :] = query
            key_aug[head, rows, :] = key
            value_aug[head, rows, :] = jnp.where(
                own, block[:, 2 * PAIR :], jnp.where(spare == 0, 1.0, 0.0)
            ).astype(BF16)

    @pl.loop(0, tiles)
    def attend(index):
        rows = tile_rows(index)
        total[...] = jnp.zeros(total.shape, F32)

        start, pairs = tile_pairs(low[index], high[index], tiles)

        @pl.loop(0, pairs)
        def keys(pair):
            others = [start + 2 * pair, start + 2 * pair + 1]
            columns = [tile_rows(other) for other in others]
            places = [strip_place(other - index, reach) for other in others]
            cases = [(head, side) for head in range(2) for side in range(2)]
            raws = [
                dot_nt(query_aug[head, rows, :], key_aug[head, columns[side], :])
                for head, side in cases
            ]
            weights = [
                jnp.exp(raw + strip[head, :, places[side]]).astype(BF16)
                for raw, (head, side) in zip(raws, cases)
            ]
            for head in range(2):
                tops[head] = jnp.maximum(
                    tops[head],
                    jnp.max(
                        jnp.maximum(raws[2 * head], raws[2 * head + 1]).reshape(
                            TILE // 8, 8, TILE
                        ),
                        axis=0,
                    ),
                )
                total[head] += dot_f32(
                    weights[2 * head], value_aug[head, columns[0], :]
                ) + dot_f32(weights[2 * head + 1], value_aug[head, columns[1], :])

        parts = []
        for head in range(2):
            summed = total[head]
            spot = DH if head == 0 else 0
            row_total = summed[:, spot : spot + 1]
            parts.append((summed / row_total, jnp.broadcast_to(1.0 / row_total, summed.shape)))
        first = lane < DH
        result = jnp.where(first, parts[0][0], parts[1][0])
        exact[rows, :] = result
        inverse[rows, :] = jnp.where(first, parts[0][1], parts[1][1])
        held[rows, :] = result.astype(BF16)

    put_back(order_col, held, context)


def attend_back_kernel(
    low, high, offsets, order_row, order_col, table, ordered, exact, inverse, incoming,
    *refs,
):
    (
        outgoing, slanted,
        query_aug, key_aug, value_aug, grad_aug, grad_plain, key_turned,
        strip, gathered, query_turned, key_sum, value_sum, held, moved,
    ) = refs[-15:]
    rows_all = ordered.shape[0]
    tiles = rows_all // TILE
    reach = strip.shape[2] // TILE // 2
    lane = lane_of(TILE)
    fill_strip(strip, table)
    put_in_order(order_row, incoming, moved)
    gathered[...] = jnp.zeros(gathered.shape, F32)
    key_sum[...] = jnp.zeros(key_sum.shape, F32)
    value_sum[...] = jnp.zeros(value_sum.shape, F32)

    @pl.loop(0, tiles)
    def arrange(index):
        rows = tile_rows(index)
        block = ordered[rows, :].astype(F32)
        sequence = sequence_of(offsets, index * TILE)
        arrived = moved[rows, :].astype(F32)
        scaled = arrived * inverse[rows, :]
        grad_plain[rows, :] = scaled.astype(BF16)
        product = scaled * exact[rows, :]
        key_turned[:, rows] = block[:, PAIR : 2 * PAIR].T.astype(BF16)
        for head in range(2):
            own, spare = head_lanes(lane, head)
            query, key = score_operands(
                block[:, :PAIR], block[:, PAIR : 2 * PAIR], sequence, head
            )
            query_aug[head, rows, :] = query
            key_aug[head, rows, :] = key
            value_aug[head, rows, :] = jnp.where(
                own, block[:, 2 * PAIR :], jnp.where(spare < 2, 1.0, 0.0)
            ).astype(BF16)
            shift = -jnp.sum(jnp.where(own, product, 0.0), axis=1, keepdims=True)
            coarse = shift.astype(BF16).astype(F32)
            fine = shift - coarse
            extra = jnp.where(spare == 0, coarse, jnp.where(spare == 1, fine, 0.0))
            grad_aug[head, rows, :] = jnp.where(own, scaled, extra).astype(BF16)

    @pl.loop(0, tiles)
    def attend(index):
        rows = tile_rows(index)
        query_turned[...] = jnp.zeros(query_turned.shape, F32)

        @pl.loop(low[index], high[index])
        def keys(other):
            columns = tile_rows(other)
            place = tile_rows(index - other + reach)
            query_plain = ordered[rows, pl.ds(0, PAIR)]
            key_parts, value_parts = ([], [])
            for head in range(2):
                raw = dot_nt(key_aug[head, columns, :], query_aug[head, rows, :])
                weight = jnp.exp(raw + strip[head, :, place])
                slope = dot_nt(value_aug[head, columns, :], grad_aug[head, rows, :])
                score = weight * slope
                gathered[head, :, place] += score
                score = score.astype(BF16)
                key_parts.append(dot_f32(score, query_plain))
                value_parts.append(dot_f32(weight.astype(BF16), grad_plain[rows, :]))
                query_turned[pl.ds(head * DH, DH), :] += dot_f32(
                    key_turned[pl.ds(head * DH, DH), columns], score
                )
            first = lane < DH
            key_sum[columns, :] += jnp.where(first, key_parts[0], key_parts[1])
            value_sum[columns, :] += jnp.where(first, value_parts[0], value_parts[1])

        held[rows, pl.ds(0, PAIR)] = query_turned[...].T.astype(BF16)

    held[:, pl.ds(PAIR, PAIR)] = key_sum[...].astype(BF16)
    held[:, pl.ds(2 * PAIR, PAIR)] = value_sum[...].astype(BF16)

    put_back(order_col, held, outgoing)

    width = gathered.shape[2]
    for head in range(2):
        folded = gathered[head]
        size = TILE // 2
        while size >= 8:
            folded = folded[:size] + pltpu.roll(folded[size:], width - size, 1)
            size //= 2
        slanted[head] = folded


def group_attention(low, high, offsets, order_row, order_col, table, mixed):
    rows = mixed.shape[0]
    smem = pl.BlockSpec(memory_space=pltpu.SMEM)
    vmem = pl.BlockSpec(memory_space=pltpu.VMEM)
    width = table.shape[1]
    return pl.pallas_call(
        attend_kernel,
        out_shape=(
            jax.ShapeDtypeStruct((rows, 3 * PAIR), BF16),
            jax.ShapeDtypeStruct((rows, PAIR), BF16),
            jax.ShapeDtypeStruct((rows, PAIR), F32),
            jax.ShapeDtypeStruct((rows, PAIR), F32),
            jax.ShapeDtypeStruct((2, 8, TILE), F32),
        ),
        in_specs=[smem] * 3 + [vmem] * 4,
        out_specs=(vmem,) * 5,
        scratch_shapes=[
            pltpu.VMEM((2, rows, PAIR), BF16),
            pltpu.VMEM((2, rows, PAIR), BF16),
            pltpu.VMEM((2, rows, PAIR), BF16),
            pltpu.VMEM((2, TILE, width), F32),
            pltpu.VMEM((2, TILE, PAIR), F32),
            pltpu.VMEM((rows, PAIR), BF16),
        ],
        name="attend",
        compiler_params=pltpu.CompilerParams(vmem_limit_bytes=40 << 20),
        cost_estimate=pl.CostEstimate(
            flops=37_000_000_000, bytes_accessed=8_000_000, transcendentals=5_000_000
        ),
    )(low, high, offsets, order_row, order_col, table, mixed)


def group_attention_back(
    low, high, offsets, order_row, order_col, table, ordered, exact, inverse, incoming, before=()
):
    rows = ordered.shape[0]
    smem = pl.BlockSpec(memory_space=pltpu.SMEM)
    vmem = pl.BlockSpec(memory_space=pltpu.VMEM)
    width = table.shape[1]
    return pl.pallas_call(
        attend_back_kernel,
        out_shape=(
            jax.ShapeDtypeStruct((rows, 3 * PAIR), BF16),
            jax.ShapeDtypeStruct((2, 8, width), F32),
        ),
        in_specs=[smem] * 3 + [vmem] * 7 + [pl.BlockSpec(memory_space=pl.ANY)] * len(before),
        out_specs=(vmem,) * 2,
        scratch_shapes=[
            pltpu.VMEM((2, rows, PAIR), BF16),
            pltpu.VMEM((2, rows, PAIR), BF16),
            pltpu.VMEM((2, rows, PAIR), BF16),
            pltpu.VMEM((2, rows, PAIR), BF16),
            pltpu.VMEM((rows, PAIR), BF16),
            pltpu.VMEM((PAIR, rows), BF16),
            pltpu.VMEM((2, TILE, width), F32),
            pltpu.VMEM((2, TILE, width), F32),
            pltpu.VMEM((PAIR, TILE), F32),
            pltpu.VMEM((rows, PAIR), F32),
            pltpu.VMEM((rows, PAIR), F32),
            pltpu.VMEM((rows, 3 * PAIR), BF16),
            pltpu.VMEM((rows, PAIR), BF16),
        ],
        name="attend_back",
        compiler_params=pltpu.CompilerParams(vmem_limit_bytes=50 << 20),
        cost_estimate=pl.CostEstimate(
            flops=45_000_000_000, bytes_accessed=12_000_000, transcendentals=5_000_000
        ),
    )(low, high, offsets, order_row, order_col, table, ordered, exact, inverse, incoming, *before)


def sequence_plan(lengths, rows):
    offsets = jnp.cumsum(lengths) - lengths
    ends = offsets + lengths
    starts_at = jnp.arange(rows // TILE, dtype=jnp.int32) * TILE
    seq_first = jnp.sum((starts_at[:, None] >= offsets[None, :]).astype(jnp.int32), axis=1) - 1
    seq_last = (
        jnp.sum((starts_at[:, None] + TILE - 1 >= offsets[None, :]).astype(jnp.int32), axis=1) - 1
    )
    picks = jnp.arange(lengths.shape[0], dtype=jnp.int32)[None, :]
    low = jnp.sum(jnp.where(seq_first[:, None] == picks, offsets[None, :], 0), axis=1) // TILE
    high = jnp.sum(jnp.where(seq_last[:, None] == picks, ends[None, :], 0), axis=1)
    return (low, (high + TILE - 1) // TILE, offsets)


def bias_tables(rel_buckets, bias_pair):
    table_len = rel_buckets.shape[0]
    reach = (table_len + 1) // 2 // TILE
    width = (2 * reach + 1) * TILE
    hot = (rel_buckets[None, :] == jnp.arange(NB, dtype=jnp.int32)[:, None]).astype(BF16)
    table = dot_tn(bias_pair, hot)
    pad = ((0, 0), (0, width - table_len))
    return (jnp.pad(table, pad), jnp.pad(table[:, ::-1], pad))


def bucket_sums(rel_buckets, slanted):
    table_len = rel_buckets.shape[0]
    width = slanted.shape[2]
    total = jnp.zeros((2, table_len), F32)
    for row in range(8):
        total = total + slanted[:, row, row + 1 : row + 1 + table_len]
    hot = (rel_buckets[::-1][:, None] == jnp.arange(NB, dtype=jnp.int32)[None, :]).astype(F32)
    return jnp.dot(total, hot, precision=lax.Precision.HIGHEST, preferred_element_type=F32)


def blank_arrays(shapes):
    def leave(*refs):
        pass

    return pl.pallas_call(
        leave,
        out_shape=tuple(jax.ShapeDtypeStruct(shape, F32) for shape in shapes),
        out_specs=tuple(pl.BlockSpec(memory_space=pl.ANY) for shape in shapes),
        name="blank",
    )()


def bands_of(width):
    return [slice(band * BAND, (band + 1) * BAND) for band in range(width // BAND)]


def pick_kernel(plan, outs, chunks, *refs):
    picked = refs[len(refs) - outs :]
    for flow, start, source, count in plan:
        if source is None:
            picked[flow][pl.ds(start, count), :] = jnp.zeros((count, BAND), BF16)
            continue
        part = refs[source]
        rows = part.shape[0]
        for band, columns in enumerate(bands_of(part.shape[1])):
            picked[flow][pl.ds(start + band * rows, rows), :] = part[:, columns]


def spread_kernel(starts, chunks, message, *refs):
    parts = len(starts)
    results, wide, sems = (refs[parts : 2 * parts], refs[2 * parts : 3 * parts], refs[3 * parts])
    copies = []
    for index, start in enumerate(starts):
        rows = wide[index].shape[0]
        place = pl.ds(pl.multiple_of(chunks[index] * rows, rows), rows)
        for band, columns in enumerate(bands_of(wide[index].shape[1])):
            wide[index][:, columns] = message[pl.ds(start + band * rows, rows), :].astype(F32)
            copy = pltpu.make_async_copy(
                wide[index].at[:, columns],
                results[index].at[place, columns],
                sems.at[len(copies)],
            )
            copy.start()
            copies.append(copy)
    for copy in copies:
        copy.wait()


def whole_spec(shape):
    return pl.BlockSpec(shape, lambda step, chunk: (0,) * len(shape))


def row_spec(rows, width, place):
    return pl.BlockSpec((rows, width), lambda step, chunk: (chunk[place], 0))


def pick_chunks(plan, rows, chunks, sources):
    shapes = tuple(jax.ShapeDtypeStruct((count, BAND), BF16) for count in rows)
    return pl.pallas_call(
        functools.partial(pick_kernel, plan, len(rows)),
        grid_spec=pltpu.PrefetchScalarGridSpec(
            num_scalar_prefetch=1,
            grid=(1,),
            in_specs=[
                row_spec(count, array_in.shape[1], place)
                for place, (array_in, count) in enumerate(sources)
            ],
            out_specs=tuple(whole_spec(shape.shape) for shape in shapes),
        ),
        out_shape=shapes,
        name="pick",
        cost_estimate=pl.CostEstimate(
            flops=0, bytes_accessed=4 * sum(rows) * BAND, transcendentals=0
        ),
    )(chunks, *[array_in for array_in, count in sources])


def spread_chunks(starts, chunks, message, counts, results):
    kept = [pl.BlockSpec(memory_space=pl.ANY)] * len(results)
    shapes = [(count, result.shape[1]) for count, result in zip(counts, results)]
    copies = sum(width // BAND for count, width in shapes)
    return pl.pallas_call(
        functools.partial(spread_kernel, starts),
        in_specs=[
            pl.BlockSpec(memory_space=pltpu.SMEM),
            pl.BlockSpec(memory_space=pltpu.VMEM),
        ]
        + kept,
        out_specs=tuple(kept),
        out_shape=tuple(jax.ShapeDtypeStruct(result.shape, F32) for result in results),
        scratch_shapes=[pltpu.VMEM(shape, F32) for shape in shapes]
        + [pltpu.SemaphoreType.DMA((copies,))],
        input_output_aliases={2 + item: item for item in range(len(results))},
        name="spread",
        cost_estimate=pl.CostEstimate(
            flops=0, bytes_accessed=6 * message.size, transcendentals=0
        ),
    )(chunks, message, *results)


def heads_kernel(chunk, message, *refs):
    for item, result in enumerate(refs[-3:]):
        result[...] = message[:, item * PAIR : (item + 1) * PAIR].astype(F32)


def spread_heads(chip, message, results):
    rows, parts = message.shape[0], len(RING)
    shape = jax.ShapeDtypeStruct((rows, parts * PAIR), F32)
    spec = pl.BlockSpec((rows, PAIR), lambda step, chunk: (0, chunk[0]))
    return pl.pallas_call(
        heads_kernel,
        grid_spec=pltpu.PrefetchScalarGridSpec(
            num_scalar_prefetch=1,
            grid=(1,),
            in_specs=[whole_spec(message.shape)]
            + [pl.BlockSpec(memory_space=pl.ANY)] * len(results),
            out_specs=(spec,) * 3,
        ),
        out_shape=(shape,) * 3,
        input_output_aliases={2 + item: item for item in range(len(results))},
        name="spread_heads",
        cost_estimate=pl.CostEstimate(flops=0, bytes_accessed=6 * message.size, transcendentals=0),
    )(chip.reshape(1), message, *results)


def tie(*values):
    return lax.optimization_barrier(values)


def ring_pairs(way):
    count = len(RING)
    return [(RING[i], RING[(i + way) % count]) for i in range(count)]


def ring_place():
    return look_up([RING.index(c) for c in range(len(RING))], lax.axis_index("ctx"))


def ring_chip(place):
    return look_up(RING, jnp.mod(place, len(RING)))


def tiny_gather(values):
    sent = jnp.broadcast_to(values[None], (len(RING),) + values.shape)
    return lax.all_to_all(sent, "ctx", 0, 0, tiled=True)


class RingSum:
    def __init__(self, ahead, back, results, widths):
        self.flows = [(ahead, 1), (back, -1)]
        self.widths = widths
        self.me = ring_place()
        self.round = 0
        self.results = tuple(results)
        self.arrived = [None, None]
        self.ready = [None, None]
        self.arrays = {}
        self.last = 2 * (len(RING) - 1)
        self.rounds = self.last + max(part[4] for part in ahead)

    @property
    def done(self):
        return self.round == self.rounds

    def part_rows(self, part):
        return part[1] * (self.widths[part[3]] // BAND)

    def layout(self, parts, round_at):
        start, starts = (0, {})
        for index, part in enumerate(parts):
            if 0 <= round_at - part[4] < self.last:
                starts[index] = start
                start += self.part_rows(part)
        return (starts, start)

    def chunk(self, part, way, hops):
        return jnp.mod(self.me - way * hops, len(RING)) + part[2]

    def pick(self, round_at):
        self.picked = None
        plan, sources, chunks, message_rows = ([], [], [], [])
        for flow, (parts, way) in enumerate(self.flows):
            starts, rows = self.layout(parts, round_at)
            message_rows.append(rows)
            for index, start in starts.items():
                part = parts[index]
                hops = round_at - part[4]
                if hops < len(RING):
                    plan.append((flow, start, len(sources), self.part_rows(part)))
                    sources.append((self.arrays[part[3]], part[1]))
                    chunks.append(self.chunk(part, way, hops))
                else:
                    plan.append((flow, start, None, self.part_rows(part)))
        if sources:
            self.picked = pick_chunks(tuple(plan), message_rows, jnp.stack(chunks), sources)

    def make(self):
        self.ready = []
        for flow, (parts, way) in enumerate(self.flows):
            got = self.arrived[flow]
            if self.round == 0:
                self.ready.append(self.picked[flow])
                continue
            starts, rows = self.layout(parts, self.round)
            before, rows_before = self.layout(parts, self.round - 1)
            kept = [index for index in starts if index in before]
            if kept != list(before):
                got = jnp.concatenate(
                    [got[before[index] : before[index] + self.part_rows(parts[index])] for index in kept]
                )
            if self.picked is not None:
                picked = self.picked[flow]
                same = got.shape[0]
                added = (got.astype(F32) + picked[:same].astype(F32)).astype(BF16)
                got = added if same == rows else jnp.concatenate([added, picked[same:]])
            self.ready.append(got)

    def send(self):
        if self.done:
            return
        self.arrived = [
            lax.ppermute(held, "ctx", ring_pairs(way))
            for held, (parts, way) in zip(self.ready, self.flows)
        ]

    def absorb(self):
        if self.done:
            return
        self.round += 1
        self.landed = list(self.arrived)
        if not self.done:
            self.make()

    def prepare(self):
        if self.round + 1 < self.rounds:
            self.pick(self.round + 1)

    def place(self):
        results = list(self.results)
        for flow, (parts, way) in enumerate(self.flows):
            sent_starts, rows = self.layout(parts, self.round)
            came_starts, rows = self.layout(parts, self.round - 1)
            for starts, message, ends in (
                (sent_starts, self.ready[flow], False),
                (came_starts, self.landed[flow], True),
            ):
                picked, ids, counts, chunks = ([], [], [], [])
                for index, start in starts.items():
                    part = parts[index]
                    hops = self.round - part[4]
                    if hops < len(RING) - 1 or ends != (hops == self.last):
                        continue
                    picked.append(start)
                    ids.append(part[3])
                    counts.append(part[1])
                    chunks.append(self.chunk(part, way, hops))
                if picked:
                    written = spread_chunks(
                        tuple(picked),
                        jnp.stack(chunks),
                        message,
                        counts,
                        [results[item] for item in ids],
                    )
                    for item, result in zip(ids, written):
                        results[item] = result
        self.results = tuple(results)


class RingGather:
    def __init__(self, block):
        self.me = ring_place()
        self.step = 0
        self.ready = (block, block)
        self.arrived = None
        self.results = ()
        self.arrays = ()
        self.landed = ()
        self.found = [(lax.axis_index("ctx"), block)]

    def send(self):
        if self.step == len(RING) // 2:
            return
        self.step += 1
        ahead, back = self.ready
        if self.step == len(RING) // 2:
            rows = ahead.shape[0] // 2
            ahead, back = (ahead[:rows], back[rows:])
        self.arrived = (
            lax.ppermute(ahead, "ctx", ring_pairs(1)),
            lax.ppermute(back, "ctx", ring_pairs(-1)),
        )

    def place(self):
        pass

    def prepare(self):
        pass

    def absorb(self):
        if len(self.found) == len(RING):
            return
        self.ready = self.arrived
        ahead, back = self.arrived
        if self.step < len(RING) // 2:
            self.found.append((ring_chip(self.me - self.step), ahead))
            self.found.append((ring_chip(self.me + self.step), back))
        else:
            self.found.append((ring_chip(self.me - self.step), jnp.concatenate([ahead, back])))


class HeadRing(RingGather):
    def __init__(self, block, results):
        super().__init__(block)
        self.results = results
        self.placed = 0

    def place(self):
        for chip, block in self.found[self.placed :]:
            self.results = spread_heads(chip, block, self.results)
        self.placed = len(self.found)


def stage(values, *rings):
    values, arrived = tie(values, [(ring.arrived, ring.results, ring.arrays) for ring in rings])
    for ring, blocks in zip(rings, arrived):
        ring.arrived, ring.results, ring.arrays = blocks
        ring.absorb()
    values, ready = tie(values, [ring.ready for ring in rings])
    for ring, blocks in zip(rings, ready):
        ring.ready = blocks
        ring.send()
        ring.prepare()
        ring.place()
    return values


def per_device_ring(
    tokens,
    cotangent,
    token_order,
    seq_lengths,
    rel_buckets,
    gain_attn,
    w_query,
    w_key,
    w_value,
    w_out,
    rel_bias,
    gain_ffn,
    w_gate,
    w_up,
    w_down,
):
    core = lax.axis_index("fsdp")
    ctx = lax.axis_index("ctx")
    tp = lax.axis_index("tp")
    local_rows = tokens.shape[0]
    half = w_query.shape[0]
    head_count = w_query.shape[1] // DH
    group_rows = local_rows * lax.axis_size("ctx")
    first = core == 0

    def halves(array_in):
        left, right = (array_in[:, :half], array_in[:, half:])
        return (jnp.where(first, left, right), jnp.where(first, right, left))

    def whole(own, other):
        return jnp.concatenate(
            [jnp.where(first, own, other), jnp.where(first, other, own)], axis=1
        )

    small = jnp.concatenate([gain_attn, gain_ffn, rel_bias.reshape(-1)])
    small_far = swap(small, "fsdp")
    wq_far, wk_far, wv_far = (swap(w_query, "fsdp"), swap(w_key, "fsdp"), swap(w_value, "fsdp"))
    wo_far = swap(w_out, "fsdp")
    wg_far, wu_far, wd_far = (swap(w_gate, "fsdp"), swap(w_up, "fsdp"), swap(w_down, "fsdp"))
    ga_own, ga_far = (gain_attn.astype(F32), small_far[:half].astype(F32))
    gf_own, gf_far = (gain_ffn.astype(F32), small_far[half : 2 * half].astype(F32))
    bias_far = small_far[2 * half :].reshape(rel_bias.shape)
    bias_local = jnp.where(
        first,
        jnp.concatenate([rel_bias, bias_far]),
        jnp.concatenate([bias_far, rel_bias]),
    )
    tok_own, tok_far = halves(tokens)
    cot_own, cot_far = halves(cotangent)
    tok_own, tok_far = (tok_own.astype(F32), tok_far.astype(F32))

    def norm_scale(own, far):
        total = jnp.sum(own * own, axis=1, keepdims=True) + jnp.sum(far * far, axis=1, keepdims=True)
        return lax.rsqrt(total / (2 * half) + EPS)

    scale_a = norm_scale(tok_own, tok_far)
    normed_own = (tok_own * scale_a * ga_own).astype(BF16)
    normed_far = (tok_far * scale_a * ga_far).astype(BF16)
    queries = (dot_f32(normed_own, w_query) + dot_f32(normed_far, wq_far)).astype(BF16)
    keys_here = (dot_f32(normed_own, w_key) + dot_f32(normed_far, wk_far)).astype(BF16)
    values_here = (dot_f32(normed_own, w_value) + dot_f32(normed_far, wv_far)).astype(BF16)
    parts = lax.axis_size("ctx")

    def by_heads(items):
        mixed = jnp.concatenate([item.reshape(local_rows, parts, 1, PAIR) for item in items], axis=2)
        mixed = jnp.transpose(mixed.reshape(local_rows, parts, len(items) * PAIR), (1, 0, 2))
        moved = lax.all_to_all(mixed, "ctx", 0, 0, tiled=True)
        return moved.reshape(group_rows, len(items) * PAIR)

    def by_rows(array_in):
        count = array_in.shape[1] // PAIR
        moved = lax.all_to_all(
            array_in.reshape(parts, local_rows, count * PAIR), "ctx", 0, 0, tiled=True
        )
        moved = jnp.transpose(moved.reshape(parts, local_rows, count, PAIR), (2, 1, 0, 3))
        return moved.reshape(count, local_rows, parts * PAIR)

    order_row = token_order
    order_col = token_order.reshape(group_rows, 1)
    low, high, offsets = sequence_plan(seq_lengths[0], group_rows)
    bias_pair = lax.dynamic_slice_in_dim(bias_local, ctx * 2, 2, axis=1)
    table, table_back = bias_tables(rel_buckets, bias_pair)
    mixed = by_heads([queries, keys_here, values_here])
    mixed, normed_block = tie(mixed, jnp.concatenate([normed_own, normed_far], axis=1))
    normed_ring = RingGather(normed_block)
    normed_ring.send()
    ordered, context_heads, exact, inverse, tops = group_attention(
        low, high, offsets, order_row, order_col, table, mixed
    )
    context_heads, normed_ring.arrived = tie(context_heads, normed_ring.arrived)
    normed_ring.absorb()
    context = by_rows(context_heads)[0]
    context, normed_ring.ready = tie(context, normed_ring.ready)
    normed_ring.send()

    def tp_sum(own, far):
        own, far = (own.astype(BF16), far.astype(BF16))
        return (
            own.astype(F32) + swap(own, "tp").astype(F32),
            far.astype(F32) + swap(far, "tp").astype(F32),
        )

    attn_own, attn_far = tp_sum(dot_f32(context, w_out), dot_f32(context, wo_far))
    attn_own = stage(attn_own, normed_ring)
    hid_own, hid_far = (tok_own + attn_own, tok_far + attn_far)
    inner_grad = dot_nt(cot_own, w_down) + dot_nt(cot_far, wd_far)
    scale_f = norm_scale(hid_own, hid_far)
    nffn_own = (hid_own * scale_f * gf_own).astype(BF16)
    nffn_far = (hid_far * scale_f * gf_far).astype(BF16)
    gate_pre = dot_f32(nffn_own, w_gate) + dot_f32(nffn_far, wg_far)
    up_pre = dot_f32(nffn_own, w_up) + dot_f32(nffn_far, wu_far)
    inner_act = geglu(gate_pre, up_pre).astype(BF16)
    unused, geglu_back = jax.vjp(geglu, gate_pre, up_pre)
    gate_grad, up_grad = geglu_back(inner_grad)
    gate_grad = gate_grad.astype(BF16)
    up_grad = up_grad.astype(BF16)

    def pair_rows(own):
        return jnp.concatenate([own, swap(own, "fsdp")])

    def pair_half(own, far):
        return jnp.concatenate([own, swap(far, "fsdp")])

    nffn_pair = pair_half(nffn_own, nffn_far)
    gate_pair, up_pair, act_pair = (pair_rows(gate_grad), pair_rows(up_grad), pair_rows(inner_act))
    cot_pair = pair_half(cot_own, cot_far)
    dnf_parts = [
        (dot_nt(gate_grad, w_gate) + dot_nt(up_grad, w_up)).astype(BF16),
        (dot_nt(gate_grad, wg_far) + dot_nt(up_grad, wu_far)).astype(BF16),
    ]
    dnf_parts, nffn_pair, act_pair = tie(dnf_parts, nffn_pair, act_pair)
    dnf_own, dnf_far = tp_sum(*dnf_parts)
    grad_down = dot_tn(act_pair, cot_pair).astype(BF16)
    grad_gate = dot_tn(nffn_pair, gate_pair).astype(BF16)
    grad_up = dot_tn(nffn_pair, up_pair).astype(BF16)
    parts_round = len(RING)
    grad_rows = grad_gate.shape[0] // parts_round
    down_rows = grad_down.shape[0] // (2 * parts_round)
    out_rows = w_out.shape[0] // (2 * parts_round)
    out_shape = (w_out.shape[0], half)
    blanks = blank_arrays(
        [grad_gate.shape, grad_up.shape, grad_down.shape, out_shape] + [w_query.shape] * 3
    )
    ring = RingSum(
        [
            (None, grad_rows, 0, 0, 0),
            (None, down_rows, 0, 2, 0),
            (None, out_rows, 0, 3, OUT_ROUND),
        ],
        [
            (None, grad_rows, 0, 1, 0),
            (None, down_rows, parts_round, 2, 0),
            (None, out_rows, parts_round, 3, OUT_ROUND),
        ],
        blanks[:4],
        [grad_gate.shape[1], grad_up.shape[1], half, half],
    )
    ring.arrays = {0: grad_gate, 1: grad_up, 2: grad_down}
    ring.pick(0)
    ring.make()
    ring.send()

    def norm_back(own, far, scale, gain_own, gain_far, dy_own, dy_far):
        mean_term = (
            jnp.sum(gain_own * dy_own * own, axis=1, keepdims=True)
            + jnp.sum(gain_far * dy_far * far, axis=1, keepdims=True)
        ) / (2 * half)
        cubed = scale * scale * scale * mean_term
        return (
            scale * (gain_own * dy_own) - own * cubed,
            scale * (gain_far * dy_far) - far * cubed,
            jnp.sum(dy_own * own * scale, axis=0),
            jnp.sum(dy_far * far * scale, axis=0),
        )

    back_own, back_far, dgf_own, dgf_far = norm_back(
        hid_own, hid_far, scale_f, gf_own, gf_far, dnf_own, dnf_far
    )
    hgrad_own = cot_own.astype(F32) + back_own
    hgrad_far = cot_far.astype(F32) + back_far
    ag_own, ag_far = (hgrad_own.astype(BF16), hgrad_far.astype(BF16))
    grad_out = dot_tn(pair_rows(context), pair_half(ag_own, ag_far)).astype(BF16)
    context_grad = dot_nt(ag_own, w_out) + dot_nt(ag_far, wo_far)
    context_grad, ring.ready = tie(context_grad.astype(BF16), ring.ready)
    grad_mixed = by_heads([context_grad])
    ring.arrays[3] = grad_out
    ring.prepare()
    grad_mixed = stage(grad_mixed, normed_ring, ring)
    outgoing, slanted = group_attention_back(
        low, high, offsets, order_row, order_col, table_back, ordered, exact, inverse, grad_mixed, ring.picked
    )
    outgoing, tops, inner_act = stage((outgoing, tops, inner_act), ring)
    outgoing = stage(outgoing, normed_ring)
    outgoing, found = tie(outgoing, [block for chip, block in normed_ring.found])
    query_grad, key_grad, value_grad = by_rows(outgoing)
    outgoing_turned = jnp.concatenate(
        [
            lax.dynamic_slice_in_dim(outgoing, chip * local_rows, local_rows)
            for chip, blocks in normed_ring.found
        ]
    )
    head_grads = dot_tn(jnp.concatenate(found), outgoing_turned)
    head_grads, head_grads_sent = (head_grads[:half], head_grads[half:].astype(BF16))
    head_grads = (head_grads + swap(head_grads_sent, "fsdp").astype(F32)).astype(BF16)
    head_grads = stage(head_grads, ring)
    head_ring = HeadRing(head_grads, blanks[4:])
    head_ring.send()
    head_ring.place()
    dn_parts = (
        dot_nt(query_grad, w_query) + dot_nt(key_grad, w_key) + dot_nt(value_grad, w_value),
        dot_nt(query_grad, wq_far) + dot_nt(key_grad, wk_far) + dot_nt(value_grad, wv_far),
    )
    dn_parts = (dn_parts[0].astype(BF16), dn_parts[1].astype(BF16))
    dn_own, dn_far = tp_sum(*dn_parts)
    dn_own, dn_far = stage((dn_own, dn_far), ring, head_ring)
    tback_own, tback_far, dga_own, dga_far = norm_back(
        tok_own, tok_far, scale_a, ga_own, ga_far, dn_own, dn_far
    )
    grad_tokens = whole(hgrad_own + tback_own, hgrad_far + tback_far)
    ffn_own, ffn_far = tp_sum(dot_f32(inner_act, w_down), dot_f32(inner_act, wd_far))
    output = whole(hid_own + ffn_own, hid_far + ffn_far).astype(BF16)
    pair_top = jnp.max(tops, axis=(1, 2))
    here = jnp.arange(parts, dtype=jnp.int32)[:, None] == ctx
    pair_bias = bucket_sums(rel_buckets, slanted)
    grad_bias = jnp.transpose(
        jnp.where(here[:, :, None], pair_bias[None], 0.0).reshape(head_count, NB)
    )
    bias_flat = grad_bias.reshape(2, -1)
    small_own = jnp.concatenate(
        [dga_own, dgf_own, jnp.where(first, bias_flat[0], bias_flat[1]), pair_top]
    )
    small_sent = jnp.concatenate(
        [dga_far, dgf_far, jnp.where(first, bias_flat[1], bias_flat[0]), pair_top]
    )
    small_got = swap(small_sent, "fsdp")
    grad_tokens, output, small_own, small_got = stage(
        (grad_tokens, output, small_own, small_got), ring, head_ring
    )
    small_both = jnp.concatenate(
        [small_own[:-2] + small_got[:-2], jnp.maximum(small_own[-2:], small_got[-2:])]
    )
    small_all = tiny_gather(small_both)
    stage((), ring, head_ring)
    head_maxima = small_all[:, -2:].reshape(head_count)
    small_sum = jnp.sum(small_all[:, :-2], axis=0)
    final_gain_a, final_gain_f = (small_sum[:half], small_sum[half : 2 * half])
    final_bias = small_sum[2 * half :].reshape(rel_bias.shape)
    clip_scale = TAU_CLIP / jnp.maximum(head_maxima, TAU_CLIP)
    column_scale = jnp.repeat(jnp.sqrt(clip_scale), DH)
    query_clipped = (w_query.astype(F32) * column_scale[None, :]).astype(BF16)
    key_clipped = (w_key.astype(F32) * column_scale[None, :]).astype(BF16)
    others = (
        grad_tokens,
        output,
        final_gain_a,
        final_gain_f,
        final_bias,
        head_maxima,
        query_clipped,
        key_clipped,
    )
    while not ring.done:
        stage((), ring, head_ring)
        if ring.round == len(RING) + 2:
            others, ring.arrived = tie(others, ring.arrived)
    final_gate, final_up, final_down, final_out = ring.results
    final_query, final_key, final_value = head_ring.results
    (
        grad_tokens,
        output,
        final_gain_a,
        final_gain_f,
        final_bias,
        head_maxima,
        query_clipped,
        key_clipped,
    ) = others
    return (
        output,
        grad_tokens,
        final_gain_a,
        final_query,
        final_key,
        final_value,
        final_out,
        final_bias,
        final_gain_f,
        final_gate,
        final_up,
        final_down,
        head_maxima,
        query_clipped,
        key_clipped,
    )


def pick_program(mesh):
    sizes = dict(mesh.shape)
    if sizes["fsdp"] == 2 and sizes["ctx"] == len(RING) and sizes["tp"] == 2:
        return per_device_ring
    return per_device_generic


def solution(mesh):
    in_specs = (
        P(("fsdp", "ctx"), None),
        P(("fsdp", "ctx"), None),
        P("fsdp", None),
        P("fsdp", None),
        P(),
        P("fsdp"),
        P("fsdp", "tp"),
        P("fsdp", "tp"),
        P("fsdp", "tp"),
        P("tp", "fsdp"),
        P("fsdp", "tp"),
        P("fsdp"),
        P("fsdp", "tp"),
        P("fsdp", "tp"),
        P("tp", "fsdp"),
    )
    out_specs = (
        P(("fsdp", "ctx"), None),
        P(("fsdp", "ctx"), None),
        P("fsdp"),
        P("fsdp", "tp"),
        P("fsdp", "tp"),
        P("fsdp", "tp"),
        P("tp", "fsdp"),
        P("fsdp", "tp"),
        P("fsdp"),
        P("fsdp", "tp"),
        P("fsdp", "tp"),
        P("tp", "fsdp"),
        P("tp"),
        P("fsdp", "tp"),
        P("fsdp", "tp"),
    )
    per_device = pick_program(mesh)
    return jax.shard_map(
        per_device, mesh=mesh, in_specs=in_specs, out_specs=out_specs, check_vma=False
    )
```

```python
import functools

import jax
import jax.numpy as jnp
from jax import lax
from jax.experimental import pallas as pl
from jax.experimental.pallas import tpu as pltpu
from jax.sharding import PartitionSpec as P

DH = 64
NB = 32


EPS = 1e-06
TAU_CLIP = 6.0


def rms_norm(values, gain):
    return values * lax.rsqrt(jnp.mean(values * values, axis=-1, keepdims=True) + EPS) * gain


def geglu(gate_pre, up_pre):
    return jax.nn.gelu(gate_pre, approximate=True) * up_pre


def segment_of(positions, lengths_row):
    offsets = jnp.cumsum(lengths_row) - lengths_row
    return jnp.sum((positions[:, None] >= offsets[None, :]).astype(jnp.int32), axis=1) - 1


def bucket_ranges(rel_buckets):
    table_len = rel_buckets.shape[0]
    index_all = jnp.arange(table_len, dtype=jnp.int32)
    bucket_ids = jnp.arange(NB, dtype=jnp.int32)
    matched = rel_buckets[:, None] == bucket_ids[None, :]
    range_first = jnp.min(jnp.where(matched, index_all[:, None], table_len), axis=0)
    range_last = jnp.max(jnp.where(matched, index_all[:, None], -1), axis=0)
    return (range_first, range_last, table_len)


def pair_terms(query_pos, query_seg, key_pos, key_seg, ranges, bias_table):
    range_first, range_last, table_len = ranges
    longest = (table_len + 1) // 2
    offset = jnp.clip(key_pos[None, :] - query_pos[:, None] + longest - 1, 0, 2 * longest - 2)
    inside = (offset[None, :, :] >= range_first[:, None, None]) & (
        offset[None, :, :] <= range_last[:, None, None]
    )
    bucket_hot = inside.astype(jnp.bfloat16)
    pair_bias = jnp.einsum(
        "btk,bh->htk", bucket_hot, bias_table, preferred_element_type=jnp.float32
    )
    same_seq = (query_seg[:, None] == key_seg[None, :])[None]
    return (bucket_hot, pair_bias, same_seq)


def per_device_generic(
    tokens,
    cotangent,
    token_order,
    seq_lengths,
    rel_buckets,
    gain_attn,
    w_query,
    w_key,
    w_value,
    w_out,
    rel_bias,
    gain_ffn,
    w_gate,
    w_up,
    w_down,
):
    local_rows = tokens.shape[0]
    head_count = w_query.shape[1] // DH
    group_rows = local_rows * lax.axis_size("ctx")
    key_block = min(512, group_rows)
    block_count = group_rows // key_block
    ranges = bucket_ranges(rel_buckets)
    gain_a, full_query, full_key, full_value, full_out, bias_local = (
        lax.all_gather(gain_attn, "fsdp", axis=0, tiled=True),
        lax.all_gather(w_query, "fsdp", axis=0, tiled=True),
        lax.all_gather(w_key, "fsdp", axis=0, tiled=True),
        lax.all_gather(w_value, "fsdp", axis=0, tiled=True),
        lax.all_gather(w_out, "fsdp", axis=1, tiled=True),
        lax.all_gather(rel_bias, "fsdp", axis=0, tiled=True),
    )
    tokens_f = tokens.astype(jnp.float32)
    gain_a32 = gain_a.astype(jnp.float32)
    normed = rms_norm(tokens_f, gain_a32).astype(jnp.bfloat16)
    queries = jnp.dot(normed, full_query, preferred_element_type=jnp.float32).astype(jnp.bfloat16)
    keys_here = jnp.dot(normed, full_key, preferred_element_type=jnp.float32).astype(jnp.bfloat16)
    values_here = jnp.dot(normed, full_value, preferred_element_type=jnp.float32).astype(
        jnp.bfloat16
    )
    order_row = token_order[0]
    seq_ids = segment_of(order_row, seq_lengths[0])
    row_start = lax.axis_index("ctx") * local_rows
    query_pos = lax.dynamic_slice_in_dim(order_row, row_start, local_rows)
    query_seg = lax.dynamic_slice_in_dim(seq_ids, row_start, local_rows)
    pos_blocks = order_row.reshape(block_count, key_block)
    seg_blocks = seq_ids.reshape(block_count, key_block)
    query_heads = queries.reshape(local_rows, head_count, DH)
    key_all, value_all = (
        lax.all_gather(keys_here, "ctx", axis=0, tiled=True),
        lax.all_gather(values_here, "ctx", axis=0, tiled=True),
    )

    def blocked(array_in):
        return array_in.reshape(block_count, key_block, head_count, DH)

    def forward_block(running, inputs):
        summed, totals, head_top = running
        key_blk, value_blk, pos_blk, seg_blk = inputs
        raw_scores = jnp.einsum(
            "thd,khd->htk", query_heads, key_blk, preferred_element_type=jnp.float32
        )
        bucket_hot, pair_bias, same_seq = pair_terms(
            query_pos, query_seg, pos_blk, seg_blk, ranges, bias_local
        )
        weights = jnp.where(same_seq, jnp.exp(raw_scores + pair_bias), 0.0)
        totals = totals + jnp.sum(weights, axis=2)
        summed = summed + jnp.einsum(
            "htk,khd->thd",
            weights.astype(jnp.bfloat16),
            value_blk,
            preferred_element_type=jnp.float32,
        )
        head_top = jnp.maximum(
            head_top, jnp.max(jnp.where(same_seq, raw_scores, -1e30), axis=(1, 2))
        )
        return ((summed, totals, head_top), None)

    start_state = (
        jnp.zeros((local_rows, head_count, DH), jnp.float32),
        jnp.zeros((head_count, local_rows), jnp.float32),
        jnp.full((head_count,), -1e30, jnp.float32),
    )
    (summed, totals, head_top), unused = lax.scan(
        forward_block, start_state, (blocked(key_all), blocked(value_all), pos_blocks, seg_blocks)
    )
    row_totals = jnp.transpose(totals)[:, :, None]
    context_exact = summed / row_totals
    context = context_exact.reshape(local_rows, head_count * DH).astype(jnp.bfloat16)
    head_maxima = lax.pmax(head_top, ("fsdp", "ctx"))
    attn_out = lax.psum(
        jnp.dot(context, full_out, preferred_element_type=jnp.float32).astype(jnp.bfloat16), "tp"
    ).astype(jnp.float32)
    hidden_state = tokens_f + attn_out
    gain_f, full_gate, full_up, full_down = (
        lax.all_gather(gain_ffn, "fsdp", axis=0, tiled=True),
        lax.all_gather(w_gate, "fsdp", axis=0, tiled=True),
        lax.all_gather(w_up, "fsdp", axis=0, tiled=True),
        lax.all_gather(w_down, "fsdp", axis=1, tiled=True),
    )
    gain_f32 = gain_f.astype(jnp.float32)
    normed_ffn = rms_norm(hidden_state, gain_f32).astype(jnp.bfloat16)
    gate_pre = jnp.dot(normed_ffn, full_gate, preferred_element_type=jnp.float32)
    up_pre = jnp.dot(normed_ffn, full_up, preferred_element_type=jnp.float32)
    inner_act = geglu(gate_pre, up_pre).astype(jnp.bfloat16)
    ffn_out = lax.psum(
        jnp.dot(inner_act, full_down, preferred_element_type=jnp.float32).astype(jnp.bfloat16), "tp"
    ).astype(jnp.float32)
    output = (hidden_state + ffn_out).astype(jnp.bfloat16)
    grad_down = jnp.einsum("tf,td->fd", inner_act, cotangent, preferred_element_type=jnp.float32)
    inner_grad = jnp.einsum("td,fd->tf", cotangent, full_down, preferred_element_type=jnp.float32)
    unused, geglu_back = jax.vjp(geglu, gate_pre, up_pre)
    gate_grad, up_grad = geglu_back(inner_grad)
    gate_grad = gate_grad.astype(jnp.bfloat16)
    up_grad = up_grad.astype(jnp.bfloat16)
    grad_gate = jnp.einsum("tc,tf->cf", normed_ffn, gate_grad, preferred_element_type=jnp.float32)
    grad_up = jnp.einsum("tc,tf->cf", normed_ffn, up_grad, preferred_element_type=jnp.float32)
    ffn_term = jnp.einsum(
        "tf,cf->tc", gate_grad, full_gate, preferred_element_type=jnp.float32
    ) + jnp.einsum("tf,cf->tc", up_grad, full_up, preferred_element_type=jnp.float32)
    normed_ffn_grad = lax.psum(ffn_term.astype(jnp.bfloat16), "tp").astype(jnp.float32)
    unused, norm_ffn_back = jax.vjp(rms_norm, hidden_state, gain_f32)
    hidden_norm_grad, grad_gain_ffn = norm_ffn_back(normed_ffn_grad)
    hidden_grad = cotangent.astype(jnp.float32) + hidden_norm_grad
    attn_grad = hidden_grad.astype(jnp.bfloat16)
    grad_out = jnp.einsum("tc,td->cd", context, attn_grad, preferred_element_type=jnp.float32)
    context_grad = jnp.einsum(
        "td,cd->tc", attn_grad, full_out, preferred_element_type=jnp.float32
    ).reshape(local_rows, head_count, DH)
    summed_grad = (context_grad / row_totals).astype(jnp.bfloat16)
    total_grad = jnp.transpose(-jnp.sum(context_grad * context_exact, axis=2) / row_totals[:, :, 0])
    key_back, value_back = (key_all, value_all)

    def backward_block(running, inputs):
        query_acc, bias_acc = running
        key_blk, value_blk, pos_blk, seg_blk = inputs
        raw_scores = jnp.einsum(
            "thd,khd->htk", query_heads, key_blk, preferred_element_type=jnp.float32
        )
        bucket_hot, pair_bias, same_seq = pair_terms(
            query_pos, query_seg, pos_blk, seg_blk, ranges, bias_local
        )
        weights = jnp.where(same_seq, jnp.exp(raw_scores + pair_bias), 0.0)
        prob_grad = (
            jnp.einsum("thd,khd->htk", summed_grad, value_blk, preferred_element_type=jnp.float32)
            + total_grad[:, :, None]
        )
        score_grad = (weights * prob_grad).astype(jnp.bfloat16)
        query_acc = query_acc + jnp.einsum(
            "htk,khd->thd", score_grad, key_blk, preferred_element_type=jnp.float32
        )
        key_grad = jnp.einsum(
            "htk,thd->khd", score_grad, query_heads, preferred_element_type=jnp.float32
        )
        value_grad = jnp.einsum(
            "htk,thd->khd",
            weights.astype(jnp.bfloat16),
            summed_grad,
            preferred_element_type=jnp.float32,
        )
        bucket_sums = jnp.einsum(
            "htk,btk->hb", score_grad, bucket_hot, preferred_element_type=jnp.float32
        )
        return ((query_acc, bias_acc + bucket_sums), (key_grad, value_grad))

    zero_state = (
        jnp.zeros((local_rows, head_count, DH), jnp.float32),
        jnp.zeros((head_count, NB), jnp.float32),
    )
    (query_acc, bias_acc), (key_grads, value_grads) = lax.scan(
        backward_block, zero_state, (blocked(key_back), blocked(value_back), pos_blocks, seg_blocks)
    )
    key_grad_all, value_grad_all = (
        lax.psum_scatter(
            key_grads.reshape(group_rows, head_count * DH).astype(jnp.bfloat16),
            "ctx",
            scatter_dimension=0,
            tiled=True,
        ).astype(jnp.float32),
        lax.psum_scatter(
            value_grads.reshape(group_rows, head_count * DH).astype(jnp.bfloat16),
            "ctx",
            scatter_dimension=0,
            tiled=True,
        ).astype(jnp.float32),
    )
    query_grad = query_acc.reshape(local_rows, head_count * DH).astype(jnp.bfloat16)
    key_grad = key_grad_all.astype(jnp.bfloat16)
    value_grad = value_grad_all.astype(jnp.bfloat16)
    attn_term = jnp.einsum("tc,dc->td", query_grad, full_query, preferred_element_type=jnp.float32)
    attn_term = attn_term + jnp.einsum(
        "tc,dc->td", key_grad, full_key, preferred_element_type=jnp.float32
    )
    attn_term = attn_term + jnp.einsum(
        "tc,dc->td", value_grad, full_value, preferred_element_type=jnp.float32
    )
    normed_grad = lax.psum(attn_term.astype(jnp.bfloat16), "tp").astype(jnp.float32)
    unused, norm_attn_back = jax.vjp(rms_norm, tokens_f, gain_a32)
    token_norm_grad, grad_gain_attn = norm_attn_back(normed_grad)
    grad_tokens = hidden_grad + token_norm_grad
    grad_query = jnp.einsum("td,tc->dc", normed, query_grad, preferred_element_type=jnp.float32)
    grad_key = jnp.einsum("td,tc->dc", normed, key_grad, preferred_element_type=jnp.float32)
    grad_value = jnp.einsum("td,tc->dc", normed, value_grad, preferred_element_type=jnp.float32)
    grad_bias = jnp.transpose(bias_acc)
    (
        share_gain_a,
        share_query,
        share_key,
        share_value,
        share_out,
        share_bias,
        share_gain_f,
        share_gate,
        share_up,
        share_down,
    ) = (
        lax.psum_scatter(
            grad_gain_attn.astype(jnp.bfloat16), "fsdp", scatter_dimension=0, tiled=True
        ).astype(jnp.float32),
        lax.psum_scatter(
            grad_query.astype(jnp.bfloat16), "fsdp", scatter_dimension=0, tiled=True
        ).astype(jnp.float32),
        lax.psum_scatter(
            grad_key.astype(jnp.bfloat16), "fsdp", scatter_dimension=0, tiled=True
        ).astype(jnp.float32),
        lax.psum_scatter(
            grad_value.astype(jnp.bfloat16), "fsdp", scatter_dimension=0, tiled=True
        ).astype(jnp.float32),
        lax.psum_scatter(
            grad_out.astype(jnp.bfloat16), "fsdp", scatter_dimension=1, tiled=True
        ).astype(jnp.float32),
        lax.psum_scatter(
            grad_bias.astype(jnp.bfloat16), "fsdp", scatter_dimension=0, tiled=True
        ).astype(jnp.float32),
        lax.psum_scatter(
            grad_gain_ffn.astype(jnp.bfloat16), "fsdp", scatter_dimension=0, tiled=True
        ).astype(jnp.float32),
        lax.psum_scatter(
            grad_gate.astype(jnp.bfloat16), "fsdp", scatter_dimension=0, tiled=True
        ).astype(jnp.float32),
        lax.psum_scatter(
            grad_up.astype(jnp.bfloat16), "fsdp", scatter_dimension=0, tiled=True
        ).astype(jnp.float32),
        lax.psum_scatter(
            grad_down.astype(jnp.bfloat16), "fsdp", scatter_dimension=1, tiled=True
        ).astype(jnp.float32),
    )
    (
        final_gain_a,
        final_query,
        final_key,
        final_value,
        final_out,
        final_bias,
        final_gain_f,
        final_gate,
        final_up,
        final_down,
    ) = (
        lax.psum(share_gain_a.astype(jnp.bfloat16), "ctx").astype(jnp.float32),
        lax.psum(share_query.astype(jnp.bfloat16), "ctx").astype(jnp.float32),
        lax.psum(share_key.astype(jnp.bfloat16), "ctx").astype(jnp.float32),
        lax.psum(share_value.astype(jnp.bfloat16), "ctx").astype(jnp.float32),
        lax.psum(share_out.astype(jnp.bfloat16), "ctx").astype(jnp.float32),
        lax.psum(share_bias.astype(jnp.bfloat16), "ctx").astype(jnp.float32),
        lax.psum(share_gain_f.astype(jnp.bfloat16), "ctx").astype(jnp.float32),
        lax.psum(share_gate.astype(jnp.bfloat16), "ctx").astype(jnp.float32),
        lax.psum(share_up.astype(jnp.bfloat16), "ctx").astype(jnp.float32),
        lax.psum(share_down.astype(jnp.bfloat16), "ctx").astype(jnp.float32),
    )
    clip_scale = TAU_CLIP / jnp.maximum(head_maxima, TAU_CLIP)
    column_scale = jnp.repeat(jnp.sqrt(clip_scale), DH)
    query_clipped = (w_query.astype(jnp.float32) * column_scale[None, :]).astype(jnp.bfloat16)
    key_clipped = (w_key.astype(jnp.float32) * column_scale[None, :]).astype(jnp.bfloat16)
    return (
        output,
        grad_tokens,
        final_gain_a,
        final_query,
        final_key,
        final_value,
        final_out,
        final_bias,
        final_gain_f,
        final_gate,
        final_up,
        final_down,
        head_maxima,
        query_clipped,
        key_clipped,
    )


RING = (0, 2, 4, 6, 7, 5, 3, 1)
OUT_ROUND = 1
F32 = jnp.float32
BF16 = jnp.bfloat16


def look_up(table, index):
    found = jnp.int32(table[0])
    for place in range(1, len(table)):
        found = jnp.where(index == place, table[place], found)
    return found


def swap(array_in, axis_name):
    return lax.ppermute(array_in, axis_name, [(0, 1), (1, 0)])


def dot_f32(left, right):
    return jnp.dot(left, right, preferred_element_type=F32)


def dot_nt(left, right):
    return lax.dot_general(left, right, (((1,), (1,)), ((), ())), preferred_element_type=F32)


def dot_tn(left, right):
    return lax.dot_general(left, right, (((0,), (0,)), ((), ())), preferred_element_type=F32)


BAND = 512


TILE = 256
PAIR = 2 * DH
FAR_OFF = 1e30


def lane_of(rows):
    return lax.broadcasted_iota(jnp.int32, (rows, PAIR), 1)


def head_lanes(lane, head):
    own = lane < DH if head == 0 else lane >= DH
    spare = lane - DH if head == 0 else lane
    return (own, spare)


def sequence_of(offsets, start):
    position = start + lax.broadcasted_iota(jnp.int32, (TILE, PAIR), 0)
    sequence = jnp.zeros((TILE, PAIR), jnp.int32)
    for item in range(1, offsets.shape[0]):
        sequence = sequence + (position >= offsets[item]).astype(jnp.int32)
    return sequence


def tile_rows(index):
    return pl.ds(pl.multiple_of(index * TILE, TILE), TILE)


MOVED = 1024


def moved_rows(index):
    return pl.ds(pl.multiple_of(index * MOVED, MOVED), MOVED)


def put_in_order(order_row, source, target):
    @pl.loop(0, source.shape[0] // MOVED)
    def part(index):
        position = index * MOVED + lax.broadcasted_iota(jnp.int32, (MOVED, source.shape[0]), 0)
        hot = (order_row[...] == position).astype(F32).astype(BF16)
        target[moved_rows(index), :] = dot_f32(hot, source[...]).astype(BF16)


def put_back(order_col, source, target):
    @pl.loop(0, source.shape[0] // MOVED)
    def part(index):
        position = lax.broadcasted_iota(jnp.int32, (MOVED, source.shape[0]), 1)
        hot = (order_col[moved_rows(index), :] == position).astype(F32).astype(BF16)
        target[moved_rows(index), :] = dot_f32(hot, source[...]).astype(BF16)


def tile_pairs(low, high, tiles):
    pairs = (high - low + 1) // 2
    return (jnp.minimum(low, tiles - 2 * pairs), pairs)


def strip_place(distance, reach):
    return tile_rows(jnp.clip(distance + reach, 0, 2 * reach))


def fill_strip(strip, table):
    width = table.shape[1]
    for head in range(2):
        row = jnp.broadcast_to(table[pl.ds(head, 1), :], (TILE, width))
        strip[head] = pltpu.roll(row, 1, 1, stride=1, stride_axis=0)


def score_operands(query, key, sequence, head):
    own, spare = head_lanes(lane_of(TILE), head)
    differs = jnp.where((spare < 8) & (sequence != spare), 1.0, 0.0)
    blocked = jnp.where(sequence == spare, -FAR_OFF, 0.0)
    return (
        jnp.where(own, query, differs).astype(BF16),
        jnp.where(own, key, blocked).astype(BF16),
    )


def attend_kernel(
    low, high, offsets, order_row, order_col, table, mixed,
    ordered, context, exact, inverse, tops,
    query_aug, key_aug, value_aug, strip, total, held,
):
    tiles = mixed.shape[0] // TILE
    reach = strip.shape[2] // TILE // 2
    lane = lane_of(TILE)
    fill_strip(strip, table)
    put_in_order(order_row, mixed, ordered)
    tops[...] = jnp.full(tops.shape, -FAR_OFF, F32)

    @pl.loop(0, tiles)
    def arrange(index):
        rows = tile_rows(index)
        block = ordered[rows, :].astype(F32)
        sequence = sequence_of(offsets, index * TILE)
        for head in range(2):
            own, spare = head_lanes(lane, head)
            query, key = score_operands(
                block[:, :PAIR], block[:, PAIR : 2 * PAIR], sequence, head
            )
            query_aug[head, rows, :] = query
            key_aug[head, rows, :] = key
            value_aug[head, rows, :] = jnp.where(
                own, block[:, 2 * PAIR :], jnp.where(spare == 0, 1.0, 0.0)
            ).astype(BF16)

    @pl.loop(0, tiles)
    def attend(index):
        rows = tile_rows(index)
        total[...] = jnp.zeros(total.shape, F32)

        start, pairs = tile_pairs(low[index], high[index], tiles)

        @pl.loop(0, pairs)
        def keys(pair):
            others = [start + 2 * pair, start + 2 * pair + 1]
            columns = [tile_rows(other) for other in others]
            places = [strip_place(other - index, reach) for other in others]
            cases = [(head, side) for head in range(2) for side in range(2)]
            raws = [
                dot_nt(query_aug[head, rows, :], key_aug[head, columns[side], :])
                for head, side in cases
            ]
            weights = [
                jnp.exp(raw + strip[head, :, places[side]]).astype(BF16)
                for raw, (head, side) in zip(raws, cases)
            ]
            for head in range(2):
                tops[head] = jnp.maximum(
                    tops[head],
                    jnp.max(
                        jnp.maximum(raws[2 * head], raws[2 * head + 1]).reshape(
                            TILE // 8, 8, TILE
                        ),
                        axis=0,
                    ),
                )
                total[head] += dot_f32(
                    weights[2 * head], value_aug[head, columns[0], :]
                ) + dot_f32(weights[2 * head + 1], value_aug[head, columns[1], :])

        parts = []
        for head in range(2):
            summed = total[head]
            spot = DH if head == 0 else 0
            row_total = summed[:, spot : spot + 1]
            parts.append((summed / row_total, jnp.broadcast_to(1.0 / row_total, summed.shape)))
        first = lane < DH
        result = jnp.where(first, parts[0][0], parts[1][0])
        exact[rows, :] = result
        inverse[rows, :] = jnp.where(first, parts[0][1], parts[1][1])
        held[rows, :] = result.astype(BF16)

    put_back(order_col, held, context)


def attend_back_kernel(
    low, high, offsets, order_row, order_col, table, ordered, exact, inverse, incoming,
    *refs,
):
    (
        outgoing, slanted,
        query_aug, key_aug, value_aug, grad_aug, grad_plain, key_turned,
        strip, gathered, query_turned, key_sum, value_sum, held, moved, weights, scores,
    ) = refs[-17:]
    rows_all = ordered.shape[0]
    tiles = rows_all // TILE
    reach = strip.shape[2] // TILE // 2
    lane = lane_of(TILE)
    fill_strip(strip, table)
    put_in_order(order_row, incoming, moved)
    gathered[...] = jnp.zeros(gathered.shape, F32)
    key_sum[...] = jnp.zeros(key_sum.shape, F32)
    value_sum[...] = jnp.zeros(value_sum.shape, F32)

    @pl.loop(0, tiles)
    def arrange(index):
        rows = tile_rows(index)
        block = ordered[rows, :].astype(F32)
        sequence = sequence_of(offsets, index * TILE)
        arrived = moved[rows, :].astype(F32)
        scaled = arrived * inverse[rows, :]
        grad_plain[rows, :] = scaled.astype(BF16)
        product = scaled * exact[rows, :]
        key_turned[:, rows] = block[:, PAIR : 2 * PAIR].T.astype(BF16)
        for head in range(2):
            own, spare = head_lanes(lane, head)
            query, key = score_operands(
                block[:, :PAIR], block[:, PAIR : 2 * PAIR], sequence, head
            )
            query_aug[head, rows, :] = query
            key_aug[head, rows, :] = key
            value_aug[head, rows, :] = jnp.where(
                own, block[:, 2 * PAIR :], jnp.where(spare < 2, 1.0, 0.0)
            ).astype(BF16)
            shift = -jnp.sum(jnp.where(own, product, 0.0), axis=1, keepdims=True)
            coarse = shift.astype(BF16).astype(F32)
            fine = shift - coarse
            extra = jnp.where(spare == 0, coarse, jnp.where(spare == 1, fine, 0.0))
            grad_aug[head, rows, :] = jnp.where(own, scaled, extra).astype(BF16)

    @pl.loop(0, tiles)
    def attend(index):
        rows = tile_rows(index)
        query_turned[...] = jnp.zeros(query_turned.shape, F32)

        start, pairs = tile_pairs(low[index], high[index], tiles)

        @pl.loop(0, pairs)
        def keys(pair):
            first = lane < DH
            others = [start + 2 * pair, start + 2 * pair + 1]
            for side, other in enumerate(others):
                columns = tile_rows(other)
                place = strip_place(index - other, reach)
                for head in range(2):
                    raw = dot_nt(key_aug[head, columns, :], query_aug[head, rows, :])
                    weight = jnp.exp(raw + strip[head, :, place])
                    slope = dot_nt(value_aug[head, columns, :], grad_aug[head, rows, :])
                    score = weight * slope
                    gathered[head, :, place] += score
                    both = pl.ds((2 * side + head) * TILE, TILE)
                    weights[both, :] = weight.astype(BF16)
                    scores[both, :] = score.astype(BF16)
            key_parts = dot_f32(scores[...], ordered[rows, pl.ds(0, PAIR)])
            value_parts = dot_f32(weights[...], grad_plain[rows, :])
            for side, other in enumerate(others):
                columns = tile_rows(other)
                near, far = (2 * side * TILE, (2 * side + 1) * TILE)
                for head in range(2):
                    query_turned[pl.ds(head * DH, DH), :] += dot_f32(
                        key_turned[pl.ds(head * DH, DH), columns],
                        scores[pl.ds((2 * side + head) * TILE, TILE), :],
                    )
                key_sum[columns, :] += jnp.where(
                    first, key_parts[near:far], key_parts[far : far + TILE]
                )
                value_sum[columns, :] += jnp.where(
                    first, value_parts[near:far], value_parts[far : far + TILE]
                )

        held[rows, pl.ds(0, PAIR)] = query_turned[...].T.astype(BF16)

    held[:, pl.ds(PAIR, PAIR)] = key_sum[...].astype(BF16)
    held[:, pl.ds(2 * PAIR, PAIR)] = value_sum[...].astype(BF16)

    put_back(order_col, held, outgoing)

    width = gathered.shape[2]
    for head in range(2):
        folded = gathered[head]
        size = TILE // 2
        while size >= 8:
            folded = folded[:size] + pltpu.roll(folded[size:], width - size, 1)
            size //= 2
        slanted[head] = folded


def group_attention(low, high, offsets, order_row, order_col, table, mixed):
    rows = mixed.shape[0]
    smem = pl.BlockSpec(memory_space=pltpu.SMEM)
    vmem = pl.BlockSpec(memory_space=pltpu.VMEM)
    width = table.shape[1]
    return pl.pallas_call(
        attend_kernel,
        out_shape=(
            jax.ShapeDtypeStruct((rows, 3 * PAIR), BF16),
            jax.ShapeDtypeStruct((rows, PAIR), BF16),
            jax.ShapeDtypeStruct((rows, PAIR), F32),
            jax.ShapeDtypeStruct((rows, PAIR), F32),
            jax.ShapeDtypeStruct((2, 8, TILE), F32),
        ),
        in_specs=[smem] * 3 + [vmem] * 4,
        out_specs=(vmem,) * 5,
        scratch_shapes=[
            pltpu.VMEM((2, rows, PAIR), BF16),
            pltpu.VMEM((2, rows, PAIR), BF16),
            pltpu.VMEM((2, rows, PAIR), BF16),
            pltpu.VMEM((2, TILE, width), F32),
            pltpu.VMEM((2, TILE, PAIR), F32),
            pltpu.VMEM((rows, PAIR), BF16),
        ],
        name="attend",
        compiler_params=pltpu.CompilerParams(vmem_limit_bytes=40 << 20),
        cost_estimate=pl.CostEstimate(
            flops=37_000_000_000, bytes_accessed=8_000_000, transcendentals=5_000_000
        ),
    )(low, high, offsets, order_row, order_col, table, mixed)


def group_attention_back(
    low, high, offsets, order_row, order_col, table, ordered, exact, inverse, incoming, before=()
):
    rows = ordered.shape[0]
    smem = pl.BlockSpec(memory_space=pltpu.SMEM)
    vmem = pl.BlockSpec(memory_space=pltpu.VMEM)
    width = table.shape[1]
    return pl.pallas_call(
        attend_back_kernel,
        out_shape=(
            jax.ShapeDtypeStruct((rows, 3 * PAIR), BF16),
            jax.ShapeDtypeStruct((2, 8, width), F32),
        ),
        in_specs=[smem] * 3 + [vmem] * 7 + [pl.BlockSpec(memory_space=pl.ANY)] * len(before),
        out_specs=(vmem,) * 2,
        scratch_shapes=[
            pltpu.VMEM((2, rows, PAIR), BF16),
            pltpu.VMEM((2, rows, PAIR), BF16),
            pltpu.VMEM((2, rows, PAIR), BF16),
            pltpu.VMEM((2, rows, PAIR), BF16),
            pltpu.VMEM((rows, PAIR), BF16),
            pltpu.VMEM((PAIR, rows), BF16),
            pltpu.VMEM((2, TILE, width), F32),
            pltpu.VMEM((2, TILE, width), F32),
            pltpu.VMEM((PAIR, TILE), F32),
            pltpu.VMEM((rows, PAIR), F32),
            pltpu.VMEM((rows, PAIR), F32),
            pltpu.VMEM((rows, 3 * PAIR), BF16),
            pltpu.VMEM((rows, PAIR), BF16),
            pltpu.VMEM((4 * TILE, TILE), BF16),
            pltpu.VMEM((4 * TILE, TILE), BF16),
        ],
        name="attend_back",
        compiler_params=pltpu.CompilerParams(vmem_limit_bytes=50 << 20),
        cost_estimate=pl.CostEstimate(
            flops=45_000_000_000, bytes_accessed=12_000_000, transcendentals=5_000_000
        ),
    )(low, high, offsets, order_row, order_col, table, ordered, exact, inverse, incoming, *before)


def sequence_plan(lengths, rows):
    offsets = jnp.cumsum(lengths) - lengths
    ends = offsets + lengths
    starts_at = jnp.arange(rows // TILE, dtype=jnp.int32) * TILE
    seq_first = jnp.sum((starts_at[:, None] >= offsets[None, :]).astype(jnp.int32), axis=1) - 1
    seq_last = (
        jnp.sum((starts_at[:, None] + TILE - 1 >= offsets[None, :]).astype(jnp.int32), axis=1) - 1
    )
    picks = jnp.arange(lengths.shape[0], dtype=jnp.int32)[None, :]
    low = jnp.sum(jnp.where(seq_first[:, None] == picks, offsets[None, :], 0), axis=1) // TILE
    high = jnp.sum(jnp.where(seq_last[:, None] == picks, ends[None, :], 0), axis=1)
    return (low, (high + TILE - 1) // TILE, offsets)


def bias_tables(rel_buckets, bias_pair):
    table_len = rel_buckets.shape[0]
    reach = (table_len + 1) // 2 // TILE
    width = (2 * reach + 1) * TILE
    hot = (rel_buckets[None, :] == jnp.arange(NB, dtype=jnp.int32)[:, None]).astype(BF16)
    table = dot_tn(bias_pair, hot)
    pad = ((0, 0), (0, width - table_len))
    return (jnp.pad(table, pad), jnp.pad(table[:, ::-1], pad))


def bucket_sums(rel_buckets, slanted):
    table_len = rel_buckets.shape[0]
    width = slanted.shape[2]
    total = jnp.zeros((2, table_len), F32)
    for row in range(8):
        total = total + slanted[:, row, row + 1 : row + 1 + table_len]
    hot = (rel_buckets[::-1][:, None] == jnp.arange(NB, dtype=jnp.int32)[None, :]).astype(F32)
    return jnp.dot(total, hot, precision=lax.Precision.HIGHEST, preferred_element_type=F32)


def blank_arrays(shapes):
    def leave(*refs):
        pass

    return pl.pallas_call(
        leave,
        out_shape=tuple(jax.ShapeDtypeStruct(shape, F32) for shape in shapes),
        out_specs=tuple(pl.BlockSpec(memory_space=pl.ANY) for shape in shapes),
        name="blank",
    )()


def bands_of(width):
    return [slice(band * BAND, (band + 1) * BAND) for band in range(width // BAND)]


def pick_kernel(plan, outs, chunks, *refs):
    picked = refs[len(refs) - outs :]
    for flow, start, source, count in plan:
        if source is None:
            picked[flow][pl.ds(start, count), :] = jnp.zeros((count, BAND), BF16)
            continue
        part = refs[source]
        rows = part.shape[0]
        for band, columns in enumerate(bands_of(part.shape[1])):
            picked[flow][pl.ds(start + band * rows, rows), :] = part[:, columns]


def spread_kernel(starts, chunks, message, *refs):
    parts = len(starts)
    results, wide, sems = (refs[parts : 2 * parts], refs[2 * parts : 3 * parts], refs[3 * parts])
    copies = []
    for index, start in enumerate(starts):
        rows = wide[index].shape[0]
        place = pl.ds(pl.multiple_of(chunks[index] * rows, rows), rows)
        for band, columns in enumerate(bands_of(wide[index].shape[1])):
            wide[index][:, columns] = message[pl.ds(start + band * rows, rows), :].astype(F32)
            copy = pltpu.make_async_copy(
                wide[index].at[:, columns],
                results[index].at[place, columns],
                sems.at[len(copies)],
            )
            copy.start()
            copies.append(copy)
    for copy in copies:
        copy.wait()


def whole_spec(shape):
    return pl.BlockSpec(shape, lambda step, chunk: (0,) * len(shape))


def row_spec(rows, width, place):
    return pl.BlockSpec((rows, width), lambda step, chunk: (chunk[place], 0))


def pick_chunks(plan, rows, chunks, sources):
    shapes = tuple(jax.ShapeDtypeStruct((count, BAND), BF16) for count in rows)
    return pl.pallas_call(
        functools.partial(pick_kernel, plan, len(rows)),
        grid_spec=pltpu.PrefetchScalarGridSpec(
            num_scalar_prefetch=1,
            grid=(1,),
            in_specs=[
                row_spec(count, array_in.shape[1], place)
                for place, (array_in, count) in enumerate(sources)
            ],
            out_specs=tuple(whole_spec(shape.shape) for shape in shapes),
        ),
        out_shape=shapes,
        name="pick",
        cost_estimate=pl.CostEstimate(
            flops=0, bytes_accessed=4 * sum(rows) * BAND, transcendentals=0
        ),
    )(chunks, *[array_in for array_in, count in sources])


def spread_chunks(starts, chunks, message, counts, results):
    kept = [pl.BlockSpec(memory_space=pl.ANY)] * len(results)
    shapes = [(count, result.shape[1]) for count, result in zip(counts, results)]
    copies = sum(width // BAND for count, width in shapes)
    return pl.pallas_call(
        functools.partial(spread_kernel, starts),
        in_specs=[
            pl.BlockSpec(memory_space=pltpu.SMEM),
            pl.BlockSpec(memory_space=pltpu.VMEM),
        ]
        + kept,
        out_specs=tuple(kept),
        out_shape=tuple(jax.ShapeDtypeStruct(result.shape, F32) for result in results),
        scratch_shapes=[pltpu.VMEM(shape, F32) for shape in shapes]
        + [pltpu.SemaphoreType.DMA((copies,))],
        input_output_aliases={2 + item: item for item in range(len(results))},
        name="spread",
        cost_estimate=pl.CostEstimate(
            flops=0, bytes_accessed=6 * message.size, transcendentals=0
        ),
    )(chunks, message, *results)


def heads_kernel(chunk, message, *refs):
    for item, result in enumerate(refs[-3:]):
        result[...] = message[:, item * PAIR : (item + 1) * PAIR].astype(F32)


def spread_heads(chip, message, results):
    rows, parts = message.shape[0], len(RING)
    shape = jax.ShapeDtypeStruct((rows, parts * PAIR), F32)
    spec = pl.BlockSpec((rows, PAIR), lambda step, chunk: (0, chunk[0]))
    return pl.pallas_call(
        heads_kernel,
        grid_spec=pltpu.PrefetchScalarGridSpec(
            num_scalar_prefetch=1,
            grid=(1,),
            in_specs=[whole_spec(message.shape)]
            + [pl.BlockSpec(memory_space=pl.ANY)] * len(results),
            out_specs=(spec,) * 3,
        ),
        out_shape=(shape,) * 3,
        input_output_aliases={2 + item: item for item in range(len(results))},
        name="spread_heads",
        cost_estimate=pl.CostEstimate(flops=0, bytes_accessed=6 * message.size, transcendentals=0),
    )(chip.reshape(1), message, *results)


def tie(*values):
    return lax.optimization_barrier(values)


def ring_pairs(way):
    count = len(RING)
    return [(RING[i], RING[(i + way) % count]) for i in range(count)]


def ring_place():
    return look_up([RING.index(c) for c in range(len(RING))], lax.axis_index("ctx"))


def ring_chip(place):
    return look_up(RING, jnp.mod(place, len(RING)))


def tiny_gather(values):
    sent = jnp.broadcast_to(values[None], (len(RING),) + values.shape)
    return lax.all_to_all(sent, "ctx", 0, 0, tiled=True)


class RingSum:
    def __init__(self, ahead, back, results, widths):
        self.flows = [(ahead, 1), (back, -1)]
        self.widths = widths
        self.me = ring_place()
        self.round = 0
        self.results = tuple(results)
        self.arrived = [None, None]
        self.ready = [None, None]
        self.arrays = {}
        self.last = 2 * (len(RING) - 1)
        self.rounds = self.last + max(part[4] for part in ahead)

    @property
    def done(self):
        return self.round == self.rounds

    def part_rows(self, part):
        return part[1] * (self.widths[part[3]] // BAND)

    def layout(self, parts, round_at):
        start, starts = (0, {})
        for index, part in enumerate(parts):
            if 0 <= round_at - part[4] < self.last:
                starts[index] = start
                start += self.part_rows(part)
        return (starts, start)

    def chunk(self, part, way, hops):
        return jnp.mod(self.me - way * hops, len(RING)) + part[2]

    def pick(self, round_at):
        self.picked = None
        plan, sources, chunks, message_rows = ([], [], [], [])
        for flow, (parts, way) in enumerate(self.flows):
            starts, rows = self.layout(parts, round_at)
            message_rows.append(rows)
            for index, start in starts.items():
                part = parts[index]
                hops = round_at - part[4]
                if hops < len(RING):
                    plan.append((flow, start, len(sources), self.part_rows(part)))
                    sources.append((self.arrays[part[3]], part[1]))
                    chunks.append(self.chunk(part, way, hops))
                else:
                    plan.append((flow, start, None, self.part_rows(part)))
        if sources:
            self.picked = pick_chunks(tuple(plan), message_rows, jnp.stack(chunks), sources)

    def make(self):
        self.ready = []
        for flow, (parts, way) in enumerate(self.flows):
            got = self.arrived[flow]
            if self.round == 0:
                self.ready.append(self.picked[flow])
                continue
            starts, rows = self.layout(parts, self.round)
            before, rows_before = self.layout(parts, self.round - 1)
            kept = [index for index in starts if index in before]
            if kept != list(before):
                got = jnp.concatenate(
                    [got[before[index] : before[index] + self.part_rows(parts[index])] for index in kept]
                )
            if self.picked is not None:
                picked = self.picked[flow]
                same = got.shape[0]
                added = (got.astype(F32) + picked[:same].astype(F32)).astype(BF16)
                got = added if same == rows else jnp.concatenate([added, picked[same:]])
            self.ready.append(got)

    def send(self):
        if self.done:
            return
        self.arrived = [
            lax.ppermute(held, "ctx", ring_pairs(way))
            for held, (parts, way) in zip(self.ready, self.flows)
        ]

    def absorb(self):
        if self.done:
            return
        self.round += 1
        self.landed = list(self.arrived)
        if not self.done:
            self.make()

    def prepare(self):
        if self.round + 1 < self.rounds:
            self.pick(self.round + 1)

    def place(self):
        results = list(self.results)
        for flow, (parts, way) in enumerate(self.flows):
            sent_starts, rows = self.layout(parts, self.round)
            came_starts, rows = self.layout(parts, self.round - 1)
            for starts, message, ends in (
                (sent_starts, self.ready[flow], False),
                (came_starts, self.landed[flow], True),
            ):
                picked, ids, counts, chunks = ([], [], [], [])
                for index, start in starts.items():
                    part = parts[index]
                    hops = self.round - part[4]
                    if hops < len(RING) - 1 or ends != (hops == self.last):
                        continue
                    picked.append(start)
                    ids.append(part[3])
                    counts.append(part[1])
                    chunks.append(self.chunk(part, way, hops))
                if picked:
                    written = spread_chunks(
                        tuple(picked),
                        jnp.stack(chunks),
                        message,
                        counts,
                        [results[item] for item in ids],
                    )
                    for item, result in zip(ids, written):
                        results[item] = result
        self.results = tuple(results)


class RingGather:
    def __init__(self, block):
        self.me = ring_place()
        self.step = 0
        self.ready = (block, block)
        self.arrived = None
        self.results = ()
        self.arrays = ()
        self.landed = ()
        self.found = [(lax.axis_index("ctx"), block)]

    def send(self):
        if self.step == len(RING) // 2:
            return
        self.step += 1
        ahead, back = self.ready
        if self.step == len(RING) // 2:
            rows = ahead.shape[0] // 2
            ahead, back = (ahead[:rows], back[rows:])
        self.arrived = (
            lax.ppermute(ahead, "ctx", ring_pairs(1)),
            lax.ppermute(back, "ctx", ring_pairs(-1)),
        )

    def place(self):
        pass

    def prepare(self):
        pass

    def absorb(self):
        if len(self.found) == len(RING):
            return
        self.ready = self.arrived
        ahead, back = self.arrived
        if self.step < len(RING) // 2:
            self.found.append((ring_chip(self.me - self.step), ahead))
            self.found.append((ring_chip(self.me + self.step), back))
        else:
            self.found.append((ring_chip(self.me - self.step), jnp.concatenate([ahead, back])))


class HeadRing(RingGather):
    def __init__(self, block, results):
        super().__init__(block)
        self.results = results
        self.placed = 0

    def place(self):
        for chip, block in self.found[self.placed :]:
            self.results = spread_heads(chip, block, self.results)
        self.placed = len(self.found)


def stage(values, *rings):
    values, arrived = tie(values, [(ring.arrived, ring.results, ring.arrays) for ring in rings])
    for ring, blocks in zip(rings, arrived):
        ring.arrived, ring.results, ring.arrays = blocks
        ring.absorb()
    values, ready = tie(values, [ring.ready for ring in rings])
    for ring, blocks in zip(rings, ready):
        ring.ready = blocks
        ring.send()
        ring.prepare()
        ring.place()
    return values


def per_device_ring(
    tokens,
    cotangent,
    token_order,
    seq_lengths,
    rel_buckets,
    gain_attn,
    w_query,
    w_key,
    w_value,
    w_out,
    rel_bias,
    gain_ffn,
    w_gate,
    w_up,
    w_down,
):
    core = lax.axis_index("fsdp")
    ctx = lax.axis_index("ctx")
    tp = lax.axis_index("tp")
    local_rows = tokens.shape[0]
    half = w_query.shape[0]
    head_count = w_query.shape[1] // DH
    group_rows = local_rows * lax.axis_size("ctx")
    first = core == 0

    def halves(array_in):
        left, right = (array_in[:, :half], array_in[:, half:])
        return (jnp.where(first, left, right), jnp.where(first, right, left))

    def whole(own, other):
        return jnp.concatenate(
            [jnp.where(first, own, other), jnp.where(first, other, own)], axis=1
        )

    small = jnp.concatenate([gain_attn, gain_ffn, rel_bias.reshape(-1)])
    small_far = swap(small, "fsdp")
    wq_far, wk_far, wv_far = (swap(w_query, "fsdp"), swap(w_key, "fsdp"), swap(w_value, "fsdp"))
    wo_far = swap(w_out, "fsdp")
    wg_far, wu_far, wd_far = (swap(w_gate, "fsdp"), swap(w_up, "fsdp"), swap(w_down, "fsdp"))
    ga_own, ga_far = (gain_attn.astype(F32), small_far[:half].astype(F32))
    gf_own, gf_far = (gain_ffn.astype(F32), small_far[half : 2 * half].astype(F32))
    bias_far = small_far[2 * half :].reshape(rel_bias.shape)
    bias_local = jnp.where(
        first,
        jnp.concatenate([rel_bias, bias_far]),
        jnp.concatenate([bias_far, rel_bias]),
    )
    tok_own, tok_far = halves(tokens)
    cot_own, cot_far = halves(cotangent)
    tok_own, tok_far = (tok_own.astype(F32), tok_far.astype(F32))

    def norm_scale(own, far):
        total = jnp.sum(own * own, axis=1, keepdims=True) + jnp.sum(far * far, axis=1, keepdims=True)
        return lax.rsqrt(total / (2 * half) + EPS)

    scale_a = norm_scale(tok_own, tok_far)
    normed_own = (tok_own * scale_a * ga_own).astype(BF16)
    normed_far = (tok_far * scale_a * ga_far).astype(BF16)
    queries = (dot_f32(normed_own, w_query) + dot_f32(normed_far, wq_far)).astype(BF16)
    keys_here = (dot_f32(normed_own, w_key) + dot_f32(normed_far, wk_far)).astype(BF16)
    values_here = (dot_f32(normed_own, w_value) + dot_f32(normed_far, wv_far)).astype(BF16)
    parts = lax.axis_size("ctx")

    def by_heads(items):
        mixed = jnp.concatenate([item.reshape(local_rows, parts, 1, PAIR) for item in items], axis=2)
        mixed = jnp.transpose(mixed.reshape(local_rows, parts, len(items) * PAIR), (1, 0, 2))
        moved = lax.all_to_all(mixed, "ctx", 0, 0, tiled=True)
        return moved.reshape(group_rows, len(items) * PAIR)

    def by_rows(array_in):
        count = array_in.shape[1] // PAIR
        moved = lax.all_to_all(
            array_in.reshape(parts, local_rows, count * PAIR), "ctx", 0, 0, tiled=True
        )
        moved = jnp.transpose(moved.reshape(parts, local_rows, count, PAIR), (2, 1, 0, 3))
        return moved.reshape(count, local_rows, parts * PAIR)

    order_row = token_order
    order_col = token_order.reshape(group_rows, 1)
    low, high, offsets = sequence_plan(seq_lengths[0], group_rows)
    bias_pair = lax.dynamic_slice_in_dim(bias_local, ctx * 2, 2, axis=1)
    table, table_back = bias_tables(rel_buckets, bias_pair)
    mixed = by_heads([queries, keys_here, values_here])
    mixed, normed_block = tie(mixed, jnp.concatenate([normed_own, normed_far], axis=1))
    normed_ring = RingGather(normed_block)
    normed_ring.send()
    ordered, context_heads, exact, inverse, tops = group_attention(
        low, high, offsets, order_row, order_col, table, mixed
    )
    context_heads, normed_ring.arrived = tie(context_heads, normed_ring.arrived)
    normed_ring.absorb()
    context = by_rows(context_heads)[0]
    context, normed_ring.ready = tie(context, normed_ring.ready)
    normed_ring.send()

    def tp_sum(own, far):
        own, far = (own.astype(BF16), far.astype(BF16))
        return (
            own.astype(F32) + swap(own, "tp").astype(F32),
            far.astype(F32) + swap(far, "tp").astype(F32),
        )

    attn_parts = [dot_f32(context, w_out).astype(BF16), dot_f32(context, wo_far).astype(BF16)]
    attn_parts, cot_own, cot_far = tie(attn_parts, cot_own, cot_far)
    attn_own, attn_far = tp_sum(*attn_parts)
    attn_own, normed_ring.arrived = tie(attn_own, normed_ring.arrived)
    normed_ring.absorb()
    block_rows = local_rows // 2
    near, far = (slice(0, block_rows), slice(block_rows, local_rows))

    def both_ways(rows):
        ahead, back = normed_ring.ready
        return (
            lax.ppermute(ahead[rows], "ctx", ring_pairs(1)),
            lax.ppermute(back[rows], "ctx", ring_pairs(-1)),
        )

    third_near = both_ways(near)
    attn_far, normed_ring.ready = tie(attn_far, normed_ring.ready)
    third_far = both_ways(far)
    hid_own, hid_far = (tok_own + attn_own, tok_far + attn_far)
    inner_grad = dot_nt(cot_own, w_down) + dot_nt(cot_far, wd_far)
    scale_f = norm_scale(hid_own, hid_far)
    nffn_own = (hid_own * scale_f * gf_own).astype(BF16)
    nffn_far = (hid_far * scale_f * gf_far).astype(BF16)
    gate_pre = dot_f32(nffn_own, w_gate) + dot_f32(nffn_far, wg_far)
    up_pre = dot_f32(nffn_own, w_up) + dot_f32(nffn_far, wu_far)
    inner_act = geglu(gate_pre, up_pre).astype(BF16)
    unused, geglu_back = jax.vjp(geglu, gate_pre, up_pre)
    gate_grad, up_grad = geglu_back(inner_grad)
    gate_grad = gate_grad.astype(BF16)
    up_grad = up_grad.astype(BF16)

    gate_grad, up_grad, inner_act, third_near, third_far = tie(
        gate_grad, up_grad, inner_act, third_near, third_far
    )
    last = (
        lax.ppermute(third_near[0], "ctx", ring_pairs(1)),
        lax.ppermute(third_far[1], "ctx", ring_pairs(-1)),
    )

    def pair_rows(own):
        return jnp.concatenate([own, swap(own, "fsdp")])

    def pair_half(own, far):
        return jnp.concatenate([own, swap(far, "fsdp")])

    nffn_pair = pair_half(nffn_own, nffn_far)
    gate_pair, up_pair, act_pair = (pair_rows(gate_grad), pair_rows(up_grad), pair_rows(inner_act))
    cot_pair = pair_half(cot_own, cot_far)
    dnf_parts = [
        (dot_nt(gate_grad, w_gate) + dot_nt(up_grad, w_up)).astype(BF16),
        (dot_nt(gate_grad, wg_far) + dot_nt(up_grad, wu_far)).astype(BF16),
    ]
    dnf_parts, nffn_pair, act_pair = tie(dnf_parts, nffn_pair, act_pair)
    dnf_own, dnf_far = tp_sum(*dnf_parts)
    grad_down = dot_tn(act_pair, cot_pair).astype(BF16)
    grad_gate = dot_tn(nffn_pair, gate_pair).astype(BF16)
    grad_up = dot_tn(nffn_pair, up_pair).astype(BF16)
    parts_round = len(RING)
    grad_rows = grad_gate.shape[0] // parts_round
    down_rows = grad_down.shape[0] // (2 * parts_round)
    out_rows = w_out.shape[0] // (2 * parts_round)
    out_shape = (w_out.shape[0], half)
    blanks = blank_arrays(
        [grad_gate.shape, grad_up.shape, grad_down.shape, out_shape] + [w_query.shape] * 3
    )
    ring = RingSum(
        [
            (None, grad_rows, 0, 0, 0),
            (None, down_rows, 0, 2, 0),
            (None, out_rows, 0, 3, OUT_ROUND),
        ],
        [
            (None, grad_rows, 0, 1, 0),
            (None, down_rows, parts_round, 2, 0),
            (None, out_rows, parts_round, 3, OUT_ROUND),
        ],
        blanks[:4],
        [grad_gate.shape[1], grad_up.shape[1], half, half],
    )
    ring.arrays = {0: grad_gate, 1: grad_up, 2: grad_down}
    ring.pick(0)
    ring.make()
    ring.send()

    def norm_back(own, far, scale, gain_own, gain_far, dy_own, dy_far):
        mean_term = (
            jnp.sum(gain_own * dy_own * own, axis=1, keepdims=True)
            + jnp.sum(gain_far * dy_far * far, axis=1, keepdims=True)
        ) / (2 * half)
        cubed = scale * scale * scale * mean_term
        return (
            scale * (gain_own * dy_own) - own * cubed,
            scale * (gain_far * dy_far) - far * cubed,
            jnp.sum(dy_own * own * scale, axis=0),
            jnp.sum(dy_far * far * scale, axis=0),
        )

    back_own, back_far, dgf_own, dgf_far = norm_back(
        hid_own, hid_far, scale_f, gf_own, gf_far, dnf_own, dnf_far
    )
    hgrad_own = cot_own.astype(F32) + back_own
    hgrad_far = cot_far.astype(F32) + back_far
    ag_own, ag_far = (hgrad_own.astype(BF16), hgrad_far.astype(BF16))
    grad_out = dot_tn(pair_rows(context), pair_half(ag_own, ag_far)).astype(BF16)
    context_grad = dot_nt(ag_own, w_out) + dot_nt(ag_far, wo_far)
    context_grad, ring.ready = tie(context_grad.astype(BF16), ring.ready)
    grad_mixed = by_heads([context_grad])
    ring.arrays[3] = grad_out
    ring.prepare()
    stage((), ring)
    grad_mixed, last = tie(grad_mixed, last)
    outgoing, slanted = group_attention_back(
        low, high, offsets, order_row, order_col, table_back, ordered, exact, inverse, grad_mixed,
        (*ring.picked, *ring.ready),
    )
    outgoing, tops = stage((outgoing, tops), ring)
    found = [(chip * local_rows, block) for chip, block in normed_ring.found]
    for hops, ends in ((-3, (third_near[0], third_far[0])), (3, (third_near[1], third_far[1])), (4, last)):
        start = ring_chip(ring_place() + hops) * local_rows
        found += [(start, ends[0]), (start + block_rows, ends[1])]
    outgoing, blocks = tie(outgoing, [block for start, block in found])
    query_grad, key_grad, value_grad = by_rows(outgoing)
    outgoing_turned = jnp.concatenate(
        [
            lax.dynamic_slice_in_dim(outgoing, start, block.shape[0])
            for start, block in found
        ]
    )
    head_grads = dot_tn(jnp.concatenate(blocks), outgoing_turned)
    head_grads, head_grads_sent = (head_grads[:half], head_grads[half:].astype(BF16))
    head_grads = (head_grads + swap(head_grads_sent, "fsdp").astype(F32)).astype(BF16)
    head_grads = stage(head_grads, ring)
    head_ring = HeadRing(head_grads, blanks[4:])
    head_ring.send()
    head_ring.place()
    dn_parts = (
        dot_nt(query_grad, w_query) + dot_nt(key_grad, w_key) + dot_nt(value_grad, w_value),
        dot_nt(query_grad, wq_far) + dot_nt(key_grad, wk_far) + dot_nt(value_grad, wv_far),
    )
    dn_parts = (dn_parts[0].astype(BF16), dn_parts[1].astype(BF16))
    dn_own, dn_far = tp_sum(*dn_parts)
    dn_own, dn_far, inner_act = stage((dn_own, dn_far, inner_act), ring, head_ring)
    tback_own, tback_far, dga_own, dga_far = norm_back(
        tok_own, tok_far, scale_a, ga_own, ga_far, dn_own, dn_far
    )
    grad_tokens = whole(hgrad_own + tback_own, hgrad_far + tback_far)
    ffn_own, ffn_far = tp_sum(dot_f32(inner_act, w_down), dot_f32(inner_act, wd_far))
    output = whole(hid_own + ffn_own, hid_far + ffn_far).astype(BF16)
    pair_top = jnp.max(tops, axis=(1, 2))
    here = jnp.arange(parts, dtype=jnp.int32)[:, None] == ctx
    pair_bias = bucket_sums(rel_buckets, slanted)
    grad_bias = jnp.transpose(
        jnp.where(here[:, :, None], pair_bias[None], 0.0).reshape(head_count, NB)
    )
    bias_flat = grad_bias.reshape(2, -1)
    small_own = jnp.concatenate(
        [dga_own, dgf_own, jnp.where(first, bias_flat[0], bias_flat[1]), pair_top]
    )
    small_sent = jnp.concatenate(
        [dga_far, dgf_far, jnp.where(first, bias_flat[1], bias_flat[0]), pair_top]
    )
    small_got = swap(small_sent, "fsdp")
    grad_tokens, output, small_own, small_got = stage(
        (grad_tokens, output, small_own, small_got), ring, head_ring
    )
    small_both = jnp.concatenate(
        [small_own[:-2] + small_got[:-2], jnp.maximum(small_own[-2:], small_got[-2:])]
    )
    small_all = tiny_gather(small_both)
    stage((), ring, head_ring)
    head_maxima = small_all[:, -2:].reshape(head_count)
    small_sum = jnp.sum(small_all[:, :-2], axis=0)
    final_gain_a, final_gain_f = (small_sum[:half], small_sum[half : 2 * half])
    final_bias = small_sum[2 * half :].reshape(rel_bias.shape)
    clip_scale = TAU_CLIP / jnp.maximum(head_maxima, TAU_CLIP)
    column_scale = jnp.repeat(jnp.sqrt(clip_scale), DH)
    query_clipped = (w_query.astype(F32) * column_scale[None, :]).astype(BF16)
    key_clipped = (w_key.astype(F32) * column_scale[None, :]).astype(BF16)
    others = (
        grad_tokens,
        output,
        final_gain_a,
        final_gain_f,
        final_bias,
        head_maxima,
        query_clipped,
        key_clipped,
    )
    while not ring.done:
        stage((), ring, head_ring)
        if ring.round == len(RING) + 2:
            others, ring.arrived = tie(others, ring.arrived)
    final_gate, final_up, final_down, final_out = ring.results
    final_query, final_key, final_value = head_ring.results
    (
        grad_tokens,
        output,
        final_gain_a,
        final_gain_f,
        final_bias,
        head_maxima,
        query_clipped,
        key_clipped,
    ) = others
    return (
        output,
        grad_tokens,
        final_gain_a,
        final_query,
        final_key,
        final_value,
        final_out,
        final_bias,
        final_gain_f,
        final_gate,
        final_up,
        final_down,
        head_maxima,
        query_clipped,
        key_clipped,
    )


def pick_program(mesh):
    sizes = dict(mesh.shape)
    if sizes["fsdp"] == 2 and sizes["ctx"] == len(RING) and sizes["tp"] == 2:
        return per_device_ring
    return per_device_generic


def solution(mesh):
    in_specs = (
        P(("fsdp", "ctx"), None),
        P(("fsdp", "ctx"), None),
        P("fsdp", None),
        P("fsdp", None),
        P(),
        P("fsdp"),
        P("fsdp", "tp"),
        P("fsdp", "tp"),
        P("fsdp", "tp"),
        P("tp", "fsdp"),
        P("fsdp", "tp"),
        P("fsdp"),
        P("fsdp", "tp"),
        P("fsdp", "tp"),
        P("tp", "fsdp"),
    )
    out_specs = (
        P(("fsdp", "ctx"), None),
        P(("fsdp", "ctx"), None),
        P("fsdp"),
        P("fsdp", "tp"),
        P("fsdp", "tp"),
        P("fsdp", "tp"),
        P("tp", "fsdp"),
        P("fsdp", "tp"),
        P("fsdp"),
        P("fsdp", "tp"),
        P("fsdp", "tp"),
        P("tp", "fsdp"),
        P("tp"),
        P("fsdp", "tp"),
        P("fsdp", "tp"),
    )
    per_device = pick_program(mesh)
    return jax.shard_map(
        per_device, mesh=mesh, in_specs=in_specs, out_specs=out_specs, check_vma=False
    )
```

```python
import functools

import jax
import jax.numpy as jnp
from jax import lax
from jax.experimental import pallas as pl
from jax.experimental.pallas import tpu as pltpu
from jax.sharding import PartitionSpec as P

DH = 64
NB = 32


EPS = 1e-06
TAU_CLIP = 6.0


def rms_norm(values, gain):
    return values * lax.rsqrt(jnp.mean(values * values, axis=-1, keepdims=True) + EPS) * gain


def geglu(gate_pre, up_pre):
    return jax.nn.gelu(gate_pre, approximate=True) * up_pre


def segment_of(positions, lengths_row):
    offsets = jnp.cumsum(lengths_row) - lengths_row
    return jnp.sum((positions[:, None] >= offsets[None, :]).astype(jnp.int32), axis=1) - 1


def bucket_ranges(rel_buckets):
    table_len = rel_buckets.shape[0]
    index_all = jnp.arange(table_len, dtype=jnp.int32)
    bucket_ids = jnp.arange(NB, dtype=jnp.int32)
    matched = rel_buckets[:, None] == bucket_ids[None, :]
    range_first = jnp.min(jnp.where(matched, index_all[:, None], table_len), axis=0)
    range_last = jnp.max(jnp.where(matched, index_all[:, None], -1), axis=0)
    return (range_first, range_last, table_len)


def pair_terms(query_pos, query_seg, key_pos, key_seg, ranges, bias_table):
    range_first, range_last, table_len = ranges
    longest = (table_len + 1) // 2
    offset = jnp.clip(key_pos[None, :] - query_pos[:, None] + longest - 1, 0, 2 * longest - 2)
    inside = (offset[None, :, :] >= range_first[:, None, None]) & (
        offset[None, :, :] <= range_last[:, None, None]
    )
    bucket_hot = inside.astype(jnp.bfloat16)
    pair_bias = jnp.einsum(
        "btk,bh->htk", bucket_hot, bias_table, preferred_element_type=jnp.float32
    )
    same_seq = (query_seg[:, None] == key_seg[None, :])[None]
    return (bucket_hot, pair_bias, same_seq)


def per_device_generic(
    tokens,
    cotangent,
    token_order,
    seq_lengths,
    rel_buckets,
    gain_attn,
    w_query,
    w_key,
    w_value,
    w_out,
    rel_bias,
    gain_ffn,
    w_gate,
    w_up,
    w_down,
):
    local_rows = tokens.shape[0]
    head_count = w_query.shape[1] // DH
    group_rows = local_rows * lax.axis_size("ctx")
    key_block = min(512, group_rows)
    block_count = group_rows // key_block
    ranges = bucket_ranges(rel_buckets)
    gain_a, full_query, full_key, full_value, full_out, bias_local = (
        lax.all_gather(gain_attn, "fsdp", axis=0, tiled=True),
        lax.all_gather(w_query, "fsdp", axis=0, tiled=True),
        lax.all_gather(w_key, "fsdp", axis=0, tiled=True),
        lax.all_gather(w_value, "fsdp", axis=0, tiled=True),
        lax.all_gather(w_out, "fsdp", axis=1, tiled=True),
        lax.all_gather(rel_bias, "fsdp", axis=0, tiled=True),
    )
    tokens_f = tokens.astype(jnp.float32)
    gain_a32 = gain_a.astype(jnp.float32)
    normed = rms_norm(tokens_f, gain_a32).astype(jnp.bfloat16)
    queries = jnp.dot(normed, full_query, preferred_element_type=jnp.float32).astype(jnp.bfloat16)
    keys_here = jnp.dot(normed, full_key, preferred_element_type=jnp.float32).astype(jnp.bfloat16)
    values_here = jnp.dot(normed, full_value, preferred_element_type=jnp.float32).astype(
        jnp.bfloat16
    )
    order_row = token_order[0]
    seq_ids = segment_of(order_row, seq_lengths[0])
    row_start = lax.axis_index("ctx") * local_rows
    query_pos = lax.dynamic_slice_in_dim(order_row, row_start, local_rows)
    query_seg = lax.dynamic_slice_in_dim(seq_ids, row_start, local_rows)
    pos_blocks = order_row.reshape(block_count, key_block)
    seg_blocks = seq_ids.reshape(block_count, key_block)
    query_heads = queries.reshape(local_rows, head_count, DH)
    key_all, value_all = (
        lax.all_gather(keys_here, "ctx", axis=0, tiled=True),
        lax.all_gather(values_here, "ctx", axis=0, tiled=True),
    )

    def blocked(array_in):
        return array_in.reshape(block_count, key_block, head_count, DH)

    def forward_block(running, inputs):
        summed, totals, head_top = running
        key_blk, value_blk, pos_blk, seg_blk = inputs
        raw_scores = jnp.einsum(
            "thd,khd->htk", query_heads, key_blk, preferred_element_type=jnp.float32
        )
        bucket_hot, pair_bias, same_seq = pair_terms(
            query_pos, query_seg, pos_blk, seg_blk, ranges, bias_local
        )
        weights = jnp.where(same_seq, jnp.exp(raw_scores + pair_bias), 0.0)
        totals = totals + jnp.sum(weights, axis=2)
        summed = summed + jnp.einsum(
            "htk,khd->thd",
            weights.astype(jnp.bfloat16),
            value_blk,
            preferred_element_type=jnp.float32,
        )
        head_top = jnp.maximum(
            head_top, jnp.max(jnp.where(same_seq, raw_scores, -1e30), axis=(1, 2))
        )
        return ((summed, totals, head_top), None)

    start_state = (
        jnp.zeros((local_rows, head_count, DH), jnp.float32),
        jnp.zeros((head_count, local_rows), jnp.float32),
        jnp.full((head_count,), -1e30, jnp.float32),
    )
    (summed, totals, head_top), unused = lax.scan(
        forward_block, start_state, (blocked(key_all), blocked(value_all), pos_blocks, seg_blocks)
    )
    row_totals = jnp.transpose(totals)[:, :, None]
    context_exact = summed / row_totals
    context = context_exact.reshape(local_rows, head_count * DH).astype(jnp.bfloat16)
    head_maxima = lax.pmax(head_top, ("fsdp", "ctx"))
    attn_out = lax.psum(
        jnp.dot(context, full_out, preferred_element_type=jnp.float32).astype(jnp.bfloat16), "tp"
    ).astype(jnp.float32)
    hidden_state = tokens_f + attn_out
    gain_f, full_gate, full_up, full_down = (
        lax.all_gather(gain_ffn, "fsdp", axis=0, tiled=True),
        lax.all_gather(w_gate, "fsdp", axis=0, tiled=True),
        lax.all_gather(w_up, "fsdp", axis=0, tiled=True),
        lax.all_gather(w_down, "fsdp", axis=1, tiled=True),
    )
    gain_f32 = gain_f.astype(jnp.float32)
    normed_ffn = rms_norm(hidden_state, gain_f32).astype(jnp.bfloat16)
    gate_pre = jnp.dot(normed_ffn, full_gate, preferred_element_type=jnp.float32)
    up_pre = jnp.dot(normed_ffn, full_up, preferred_element_type=jnp.float32)
    inner_act = geglu(gate_pre, up_pre).astype(jnp.bfloat16)
    ffn_out = lax.psum(
        jnp.dot(inner_act, full_down, preferred_element_type=jnp.float32).astype(jnp.bfloat16), "tp"
    ).astype(jnp.float32)
    output = (hidden_state + ffn_out).astype(jnp.bfloat16)
    grad_down = jnp.einsum("tf,td->fd", inner_act, cotangent, preferred_element_type=jnp.float32)
    inner_grad = jnp.einsum("td,fd->tf", cotangent, full_down, preferred_element_type=jnp.float32)
    unused, geglu_back = jax.vjp(geglu, gate_pre, up_pre)
    gate_grad, up_grad = geglu_back(inner_grad)
    gate_grad = gate_grad.astype(jnp.bfloat16)
    up_grad = up_grad.astype(jnp.bfloat16)
    grad_gate = jnp.einsum("tc,tf->cf", normed_ffn, gate_grad, preferred_element_type=jnp.float32)
    grad_up = jnp.einsum("tc,tf->cf", normed_ffn, up_grad, preferred_element_type=jnp.float32)
    ffn_term = jnp.einsum(
        "tf,cf->tc", gate_grad, full_gate, preferred_element_type=jnp.float32
    ) + jnp.einsum("tf,cf->tc", up_grad, full_up, preferred_element_type=jnp.float32)
    normed_ffn_grad = lax.psum(ffn_term.astype(jnp.bfloat16), "tp").astype(jnp.float32)
    unused, norm_ffn_back = jax.vjp(rms_norm, hidden_state, gain_f32)
    hidden_norm_grad, grad_gain_ffn = norm_ffn_back(normed_ffn_grad)
    hidden_grad = cotangent.astype(jnp.float32) + hidden_norm_grad
    attn_grad = hidden_grad.astype(jnp.bfloat16)
    grad_out = jnp.einsum("tc,td->cd", context, attn_grad, preferred_element_type=jnp.float32)
    context_grad = jnp.einsum(
        "td,cd->tc", attn_grad, full_out, preferred_element_type=jnp.float32
    ).reshape(local_rows, head_count, DH)
    summed_grad = (context_grad / row_totals).astype(jnp.bfloat16)
    total_grad = jnp.transpose(-jnp.sum(context_grad * context_exact, axis=2) / row_totals[:, :, 0])
    key_back, value_back = (key_all, value_all)

    def backward_block(running, inputs):
        query_acc, bias_acc = running
        key_blk, value_blk, pos_blk, seg_blk = inputs
        raw_scores = jnp.einsum(
            "thd,khd->htk", query_heads, key_blk, preferred_element_type=jnp.float32
        )
        bucket_hot, pair_bias, same_seq = pair_terms(
            query_pos, query_seg, pos_blk, seg_blk, ranges, bias_local
        )
        weights = jnp.where(same_seq, jnp.exp(raw_scores + pair_bias), 0.0)
        prob_grad = (
            jnp.einsum("thd,khd->htk", summed_grad, value_blk, preferred_element_type=jnp.float32)
            + total_grad[:, :, None]
        )
        score_grad = (weights * prob_grad).astype(jnp.bfloat16)
        query_acc = query_acc + jnp.einsum(
            "htk,khd->thd", score_grad, key_blk, preferred_element_type=jnp.float32
        )
        key_grad = jnp.einsum(
            "htk,thd->khd", score_grad, query_heads, preferred_element_type=jnp.float32
        )
        value_grad = jnp.einsum(
            "htk,thd->khd",
            weights.astype(jnp.bfloat16),
            summed_grad,
            preferred_element_type=jnp.float32,
        )
        bucket_sums = jnp.einsum(
            "htk,btk->hb", score_grad, bucket_hot, preferred_element_type=jnp.float32
        )
        return ((query_acc, bias_acc + bucket_sums), (key_grad, value_grad))

    zero_state = (
        jnp.zeros((local_rows, head_count, DH), jnp.float32),
        jnp.zeros((head_count, NB), jnp.float32),
    )
    (query_acc, bias_acc), (key_grads, value_grads) = lax.scan(
        backward_block, zero_state, (blocked(key_back), blocked(value_back), pos_blocks, seg_blocks)
    )
    key_grad_all, value_grad_all = (
        lax.psum_scatter(
            key_grads.reshape(group_rows, head_count * DH).astype(jnp.bfloat16),
            "ctx",
            scatter_dimension=0,
            tiled=True,
        ).astype(jnp.float32),
        lax.psum_scatter(
            value_grads.reshape(group_rows, head_count * DH).astype(jnp.bfloat16),
            "ctx",
            scatter_dimension=0,
            tiled=True,
        ).astype(jnp.float32),
    )
    query_grad = query_acc.reshape(local_rows, head_count * DH).astype(jnp.bfloat16)
    key_grad = key_grad_all.astype(jnp.bfloat16)
    value_grad = value_grad_all.astype(jnp.bfloat16)
    attn_term = jnp.einsum("tc,dc->td", query_grad, full_query, preferred_element_type=jnp.float32)
    attn_term = attn_term + jnp.einsum(
        "tc,dc->td", key_grad, full_key, preferred_element_type=jnp.float32
    )
    attn_term = attn_term + jnp.einsum(
        "tc,dc->td", value_grad, full_value, preferred_element_type=jnp.float32
    )
    normed_grad = lax.psum(attn_term.astype(jnp.bfloat16), "tp").astype(jnp.float32)
    unused, norm_attn_back = jax.vjp(rms_norm, tokens_f, gain_a32)
    token_norm_grad, grad_gain_attn = norm_attn_back(normed_grad)
    grad_tokens = hidden_grad + token_norm_grad
    grad_query = jnp.einsum("td,tc->dc", normed, query_grad, preferred_element_type=jnp.float32)
    grad_key = jnp.einsum("td,tc->dc", normed, key_grad, preferred_element_type=jnp.float32)
    grad_value = jnp.einsum("td,tc->dc", normed, value_grad, preferred_element_type=jnp.float32)
    grad_bias = jnp.transpose(bias_acc)
    (
        share_gain_a,
        share_query,
        share_key,
        share_value,
        share_out,
        share_bias,
        share_gain_f,
        share_gate,
        share_up,
        share_down,
    ) = (
        lax.psum_scatter(
            grad_gain_attn.astype(jnp.bfloat16), "fsdp", scatter_dimension=0, tiled=True
        ).astype(jnp.float32),
        lax.psum_scatter(
            grad_query.astype(jnp.bfloat16), "fsdp", scatter_dimension=0, tiled=True
        ).astype(jnp.float32),
        lax.psum_scatter(
            grad_key.astype(jnp.bfloat16), "fsdp", scatter_dimension=0, tiled=True
        ).astype(jnp.float32),
        lax.psum_scatter(
            grad_value.astype(jnp.bfloat16), "fsdp", scatter_dimension=0, tiled=True
        ).astype(jnp.float32),
        lax.psum_scatter(
            grad_out.astype(jnp.bfloat16), "fsdp", scatter_dimension=1, tiled=True
        ).astype(jnp.float32),
        lax.psum_scatter(
            grad_bias.astype(jnp.bfloat16), "fsdp", scatter_dimension=0, tiled=True
        ).astype(jnp.float32),
        lax.psum_scatter(
            grad_gain_ffn.astype(jnp.bfloat16), "fsdp", scatter_dimension=0, tiled=True
        ).astype(jnp.float32),
        lax.psum_scatter(
            grad_gate.astype(jnp.bfloat16), "fsdp", scatter_dimension=0, tiled=True
        ).astype(jnp.float32),
        lax.psum_scatter(
            grad_up.astype(jnp.bfloat16), "fsdp", scatter_dimension=0, tiled=True
        ).astype(jnp.float32),
        lax.psum_scatter(
            grad_down.astype(jnp.bfloat16), "fsdp", scatter_dimension=1, tiled=True
        ).astype(jnp.float32),
    )
    (
        final_gain_a,
        final_query,
        final_key,
        final_value,
        final_out,
        final_bias,
        final_gain_f,
        final_gate,
        final_up,
        final_down,
    ) = (
        lax.psum(share_gain_a.astype(jnp.bfloat16), "ctx").astype(jnp.float32),
        lax.psum(share_query.astype(jnp.bfloat16), "ctx").astype(jnp.float32),
        lax.psum(share_key.astype(jnp.bfloat16), "ctx").astype(jnp.float32),
        lax.psum(share_value.astype(jnp.bfloat16), "ctx").astype(jnp.float32),
        lax.psum(share_out.astype(jnp.bfloat16), "ctx").astype(jnp.float32),
        lax.psum(share_bias.astype(jnp.bfloat16), "ctx").astype(jnp.float32),
        lax.psum(share_gain_f.astype(jnp.bfloat16), "ctx").astype(jnp.float32),
        lax.psum(share_gate.astype(jnp.bfloat16), "ctx").astype(jnp.float32),
        lax.psum(share_up.astype(jnp.bfloat16), "ctx").astype(jnp.float32),
        lax.psum(share_down.astype(jnp.bfloat16), "ctx").astype(jnp.float32),
    )
    clip_scale = TAU_CLIP / jnp.maximum(head_maxima, TAU_CLIP)
    column_scale = jnp.repeat(jnp.sqrt(clip_scale), DH)
    query_clipped = (w_query.astype(jnp.float32) * column_scale[None, :]).astype(jnp.bfloat16)
    key_clipped = (w_key.astype(jnp.float32) * column_scale[None, :]).astype(jnp.bfloat16)
    return (
        output,
        grad_tokens,
        final_gain_a,
        final_query,
        final_key,
        final_value,
        final_out,
        final_bias,
        final_gain_f,
        final_gate,
        final_up,
        final_down,
        head_maxima,
        query_clipped,
        key_clipped,
    )


RING = (0, 2, 4, 6, 7, 5, 3, 1)
F32 = jnp.float32
BF16 = jnp.bfloat16


def look_up(table, index):
    found = jnp.int32(table[0])
    for place in range(1, len(table)):
        found = jnp.where(index == place, table[place], found)
    return found


def swap(array_in, axis_name):
    return lax.ppermute(array_in, axis_name, [(0, 1), (1, 0)])


def dot_f32(left, right):
    return jnp.dot(left, right, preferred_element_type=F32)


def dot_nt(left, right):
    return lax.dot_general(left, right, (((1,), (1,)), ((), ())), preferred_element_type=F32)


def dot_tn(left, right):
    return lax.dot_general(left, right, (((0,), (0,)), ((), ())), preferred_element_type=F32)


BAND = 512


TILE = 256
PAIR = 2 * DH
FAR_OFF = 1e30


def lane_of(rows):
    return lax.broadcasted_iota(jnp.int32, (rows, PAIR), 1)


def head_lanes(lane, head):
    own = lane < DH if head == 0 else lane >= DH
    spare = lane - DH if head == 0 else lane
    return (own, spare)


def sequence_of(offsets, start):
    position = start + lax.broadcasted_iota(jnp.int32, (TILE, PAIR), 0)
    sequence = jnp.zeros((TILE, PAIR), jnp.int32)
    for item in range(1, offsets.shape[0]):
        sequence = sequence + (position >= offsets[item]).astype(jnp.int32)
    return sequence


def tile_rows(index):
    return pl.ds(pl.multiple_of(index * TILE, TILE), TILE)


MOVED = 1024


def moved_rows(index):
    return pl.ds(pl.multiple_of(index * MOVED, MOVED), MOVED)


def put_in_order(order_row, source, target):
    @pl.loop(0, source.shape[0] // MOVED)
    def part(index):
        position = index * MOVED + lax.broadcasted_iota(jnp.int32, (MOVED, source.shape[0]), 0)
        hot = (order_row[...] == position).astype(F32).astype(BF16)
        target[moved_rows(index), :] = dot_f32(hot, source[...]).astype(BF16)


def put_back(order_col, source, target):
    @pl.loop(0, source.shape[0] // MOVED)
    def part(index):
        position = lax.broadcasted_iota(jnp.int32, (MOVED, source.shape[0]), 1)
        hot = (order_col[moved_rows(index), :] == position).astype(F32).astype(BF16)
        target[moved_rows(index), :] = dot_f32(hot, source[...]).astype(BF16)


def tile_pairs(low, high, tiles):
    pairs = (high - low + 1) // 2
    return (jnp.minimum(low, tiles - 2 * pairs), pairs)


def strip_place(distance, reach):
    return tile_rows(jnp.clip(distance + reach, 0, 2 * reach))


def fill_strip(strip, table):
    width = table.shape[1]
    for head in range(2):
        row = jnp.broadcast_to(table[pl.ds(head, 1), :], (TILE, width))
        strip[head] = pltpu.roll(row, 1, 1, stride=1, stride_axis=0)


def score_operands(query, key, sequence, head):
    own, spare = head_lanes(lane_of(TILE), head)
    differs = jnp.where((spare < 8) & (sequence != spare), 1.0, 0.0)
    blocked = jnp.where(sequence == spare, -FAR_OFF, 0.0)
    return (
        jnp.where(own, query, differs).astype(BF16),
        jnp.where(own, key, blocked).astype(BF16),
    )


def attend_kernel(
    low, high, offsets, order_row, order_col, table, mixed,
    ordered, context, exact, inverse, tops,
    query_aug, key_aug, value_aug, strip, total, held,
):
    tiles = mixed.shape[0] // TILE
    reach = strip.shape[2] // TILE // 2
    lane = lane_of(TILE)
    fill_strip(strip, table)
    put_in_order(order_row, mixed, ordered)
    tops[...] = jnp.full(tops.shape, -FAR_OFF, F32)

    @pl.loop(0, tiles)
    def arrange(index):
        rows = tile_rows(index)
        block = ordered[rows, :].astype(F32)
        sequence = sequence_of(offsets, index * TILE)
        for head in range(2):
            own, spare = head_lanes(lane, head)
            query, key = score_operands(
                block[:, :PAIR], block[:, PAIR : 2 * PAIR], sequence, head
            )
            query_aug[head, rows, :] = query
            key_aug[head, rows, :] = key
            value_aug[head, rows, :] = jnp.where(
                own, block[:, 2 * PAIR :], jnp.where(spare == 0, 1.0, 0.0)
            ).astype(BF16)

    @pl.loop(0, tiles)
    def attend(index):
        rows = tile_rows(index)
        total[...] = jnp.zeros(total.shape, F32)

        start, pairs = tile_pairs(low[index], high[index], tiles)

        @pl.loop(0, pairs)
        def keys(pair):
            others = [start + 2 * pair, start + 2 * pair + 1]
            columns = [tile_rows(other) for other in others]
            places = [strip_place(other - index, reach) for other in others]
            cases = [(head, side) for head in range(2) for side in range(2)]
            raws = [
                dot_nt(query_aug[head, rows, :], key_aug[head, columns[side], :])
                for head, side in cases
            ]
            weights = [
                jnp.exp(raw + strip[head, :, places[side]]).astype(BF16)
                for raw, (head, side) in zip(raws, cases)
            ]
            for head in range(2):
                tops[head] = jnp.maximum(
                    tops[head],
                    jnp.max(
                        jnp.maximum(raws[2 * head], raws[2 * head + 1]).reshape(
                            TILE // 8, 8, TILE
                        ),
                        axis=0,
                    ),
                )
                total[head] += dot_f32(
                    weights[2 * head], value_aug[head, columns[0], :]
                ) + dot_f32(weights[2 * head + 1], value_aug[head, columns[1], :])

        parts = []
        for head in range(2):
            summed = total[head]
            spot = DH if head == 0 else 0
            row_total = summed[:, spot : spot + 1]
            parts.append((summed / row_total, jnp.broadcast_to(1.0 / row_total, summed.shape)))
        first = lane < DH
        result = jnp.where(first, parts[0][0], parts[1][0])
        exact[rows, :] = result
        inverse[rows, :] = jnp.where(first, parts[0][1], parts[1][1])
        held[rows, :] = result.astype(BF16)

    put_back(order_col, held, context)


def attend_back_kernel(
    head, low, high, offsets, order_row, order_col, table, ordered, exact, inverse, incoming,
    other_held, *refs,
):
    outgoing, slanted, moved = refs[-17:-14]
    (
        query_aug, key_aug, value_aug, grad_aug, grad_plain, key_turned,
        strip, gathered, query_turned, key_sum, value_sum, held, weights, scores,
    ) = refs[-14:]
    rows_all = ordered.shape[0]
    tiles = rows_all // TILE
    width = gathered.shape[1]
    reach = width // TILE // 2
    own, spare = head_lanes(lane_of(TILE), head)
    strip[...] = pltpu.roll(
        jnp.broadcast_to(table[pl.ds(head, 1), :], (TILE, width)), 1, 1, stride=1, stride_axis=0
    )
    if head == 0:
        put_in_order(order_row, incoming, moved)
    else:
        moved = incoming
    gathered[...] = jnp.zeros(gathered.shape, F32)
    key_sum[...] = jnp.zeros(key_sum.shape, F32)
    value_sum[...] = jnp.zeros(value_sum.shape, F32)

    @pl.loop(0, tiles)
    def arrange(index):
        rows = tile_rows(index)
        block = ordered[rows, :].astype(F32)
        sequence = sequence_of(offsets, index * TILE)
        scaled = moved[rows, :].astype(F32) * inverse[rows, :]
        grad_plain[rows, :] = scaled.astype(BF16)
        key_turned[:, rows] = block[:, PAIR : 2 * PAIR].T.astype(BF16)
        query, key = score_operands(block[:, :PAIR], block[:, PAIR : 2 * PAIR], sequence, head)
        query_aug[rows, :] = query
        key_aug[rows, :] = key
        value_aug[rows, :] = jnp.where(
            own, block[:, 2 * PAIR :], jnp.where(spare < 2, 1.0, 0.0)
        ).astype(BF16)
        product = jnp.where(own, scaled * exact[rows, :], 0.0)
        shift = -jnp.sum(product, axis=1, keepdims=True)
        coarse = shift.astype(BF16).astype(F32)
        fine = shift - coarse
        extra = jnp.where(spare == 0, coarse, jnp.where(spare == 1, fine, 0.0))
        grad_aug[rows, :] = jnp.where(own, scaled, extra).astype(BF16)

    query_turned[...] = jnp.zeros(query_turned.shape, F32)
    turned = pl.ds(head * DH, DH)

    @pl.loop(0, tiles)
    def attend(index):
        rows = tile_rows(index)
        query_turned[turned, :] = jnp.zeros((DH, TILE), F32)
        start, pairs = tile_pairs(low[index], high[index], tiles)

        @pl.loop(0, pairs)
        def keys(pair):
            others = [start + 2 * pair, start + 2 * pair + 1]
            for side, other in enumerate(others):
                columns = tile_rows(other)
                place = strip_place(index - other, reach)
                raw = dot_nt(key_aug[columns, :], query_aug[rows, :])
                weight = jnp.exp(raw + strip[:, place])
                slope = dot_nt(value_aug[columns, :], grad_aug[rows, :])
                score = weight * slope
                gathered[:, place] += score
                both = pl.ds(side * TILE, TILE)
                weights[both, :] = weight.astype(BF16)
                scores[both, :] = score.astype(BF16)
            key_parts = dot_f32(scores[...], ordered[rows, pl.ds(0, PAIR)])
            value_parts = dot_f32(weights[...], grad_plain[rows, :])
            for side, other in enumerate(others):
                columns = tile_rows(other)
                both = pl.ds(side * TILE, TILE)
                query_turned[turned, :] += dot_f32(key_turned[turned, columns], scores[both, :])
                key_sum[columns, :] += key_parts[side * TILE : (side + 1) * TILE]
                value_sum[columns, :] += value_parts[side * TILE : (side + 1) * TILE]

        held[rows, pl.ds(0, PAIR)] = query_turned[...].T.astype(BF16)

    @pl.loop(0, tiles)
    def keep(index):
        rows = tile_rows(index)
        held[rows, pl.ds(PAIR, PAIR)] = jnp.where(own, key_sum[rows, :], 0.0).astype(BF16)
        held[rows, pl.ds(2 * PAIR, PAIR)] = jnp.where(own, value_sum[rows, :], 0.0).astype(BF16)
        if head == 0:
            outgoing[rows, :] = held[rows, :]
        else:
            held[rows, :] += other_held[rows, :]

    if head == 1:
        put_back(order_col, held, outgoing)
    folded = gathered[...]
    size = TILE // 2
    while size >= 8:
        folded = folded[:size] + pltpu.roll(folded[size:], width - size, 1)
        size //= 2
    slanted[...] = folded


def group_attention(low, high, offsets, order_row, order_col, table, mixed):
    rows = mixed.shape[0]
    smem = pl.BlockSpec(memory_space=pltpu.SMEM)
    vmem = pl.BlockSpec(memory_space=pltpu.VMEM)
    width = table.shape[1]
    return pl.pallas_call(
        attend_kernel,
        out_shape=(
            jax.ShapeDtypeStruct((rows, 3 * PAIR), BF16),
            jax.ShapeDtypeStruct((rows, PAIR), BF16),
            jax.ShapeDtypeStruct((rows, PAIR), F32),
            jax.ShapeDtypeStruct((rows, PAIR), F32),
            jax.ShapeDtypeStruct((2, 8, TILE), F32),
        ),
        in_specs=[smem] * 3 + [vmem] * 4,
        out_specs=(vmem,) * 5,
        scratch_shapes=[
            pltpu.VMEM((2, rows, PAIR), BF16),
            pltpu.VMEM((2, rows, PAIR), BF16),
            pltpu.VMEM((2, rows, PAIR), BF16),
            pltpu.VMEM((2, TILE, width), F32),
            pltpu.VMEM((2, TILE, PAIR), F32),
            pltpu.VMEM((rows, PAIR), BF16),
        ],
        name="attend",
        compiler_params=pltpu.CompilerParams(vmem_limit_bytes=40 << 20),
        cost_estimate=pl.CostEstimate(
            flops=37_000_000_000, bytes_accessed=8_000_000, transcendentals=5_000_000
        ),
    )(low, high, offsets, order_row, order_col, table, mixed)


def group_attention_back(
    head, low, high, offsets, order_row, order_col, table, ordered, exact, inverse, incoming,
    other_held, before=()
):
    rows = ordered.shape[0]
    smem = pl.BlockSpec(memory_space=pltpu.SMEM)
    vmem = pl.BlockSpec(memory_space=pltpu.VMEM)
    width = table.shape[1]
    return pl.pallas_call(
        functools.partial(attend_back_kernel, head),
        out_shape=(
            jax.ShapeDtypeStruct((rows, 3 * PAIR), BF16),
            jax.ShapeDtypeStruct((8, width), F32),
            jax.ShapeDtypeStruct((rows if head == 0 else 16, PAIR), BF16),
        ),
        in_specs=[smem] * 3 + [vmem] * 8 + [pl.BlockSpec(memory_space=pl.ANY)] * len(before),
        out_specs=(vmem,) * 3,
        scratch_shapes=[
            pltpu.VMEM((rows, PAIR), BF16),
            pltpu.VMEM((rows, PAIR), BF16),
            pltpu.VMEM((rows, PAIR), BF16),
            pltpu.VMEM((rows, PAIR), BF16),
            pltpu.VMEM((rows, PAIR), BF16),
            pltpu.VMEM((PAIR, rows), BF16),
            pltpu.VMEM((TILE, width), F32),
            pltpu.VMEM((TILE, width), F32),
            pltpu.VMEM((PAIR, TILE), F32),
            pltpu.VMEM((rows, PAIR), F32),
            pltpu.VMEM((rows, PAIR), F32),
            pltpu.VMEM((rows, 3 * PAIR), BF16),
            pltpu.VMEM((2 * TILE, TILE), BF16),
            pltpu.VMEM((2 * TILE, TILE), BF16),
        ],
        name="attend_back",
        compiler_params=pltpu.CompilerParams(vmem_limit_bytes=50 << 20),
        cost_estimate=pl.CostEstimate(
            flops=20_000_000_000, bytes_accessed=8_000_000, transcendentals=2_500_000
        ),
    )(
        low, high, offsets, order_row, order_col, table, ordered, exact, inverse, incoming,
        other_held, *before,
    )


def sequence_plan(lengths, rows):
    offsets = jnp.cumsum(lengths) - lengths
    ends = offsets + lengths
    starts_at = jnp.arange(rows // TILE, dtype=jnp.int32) * TILE
    seq_first = jnp.sum((starts_at[:, None] >= offsets[None, :]).astype(jnp.int32), axis=1) - 1
    seq_last = (
        jnp.sum((starts_at[:, None] + TILE - 1 >= offsets[None, :]).astype(jnp.int32), axis=1) - 1
    )
    picks = jnp.arange(lengths.shape[0], dtype=jnp.int32)[None, :]
    low = jnp.sum(jnp.where(seq_first[:, None] == picks, offsets[None, :], 0), axis=1) // TILE
    high = jnp.sum(jnp.where(seq_last[:, None] == picks, ends[None, :], 0), axis=1)
    return (low, (high + TILE - 1) // TILE, offsets)


def bias_tables(rel_buckets, bias_pair):
    table_len = rel_buckets.shape[0]
    reach = (table_len + 1) // 2 // TILE
    width = (2 * reach + 1) * TILE
    hot = (rel_buckets[None, :] == jnp.arange(NB, dtype=jnp.int32)[:, None]).astype(BF16)
    table = dot_tn(bias_pair, hot)
    pad = ((0, 0), (0, width - table_len))
    return (jnp.pad(table, pad), jnp.pad(table[:, ::-1], pad))


def bucket_sums(rel_buckets, slanted):
    table_len = rel_buckets.shape[0]
    width = slanted.shape[2]
    total = jnp.zeros((2, table_len), F32)
    for row in range(8):
        total = total + slanted[:, row, row + 1 : row + 1 + table_len]
    hot = (rel_buckets[::-1][:, None] == jnp.arange(NB, dtype=jnp.int32)[None, :]).astype(F32)
    return jnp.dot(total, hot, precision=lax.Precision.HIGHEST, preferred_element_type=F32)


def blank_arrays(shapes):
    def leave(*refs):
        pass

    return pl.pallas_call(
        leave,
        out_shape=tuple(jax.ShapeDtypeStruct(shape, F32) for shape in shapes),
        out_specs=tuple(pl.BlockSpec(memory_space=pl.ANY) for shape in shapes),
        name="blank",
    )()


def bands_of(width):
    return [slice(band * BAND, (band + 1) * BAND) for band in range(width // BAND)]


def pick_kernel(plan, outs, chunks, *refs):
    picked = refs[len(refs) - outs :]
    for flow, start, source, count in plan:
        if source is None:
            picked[flow][pl.ds(start, count), :] = jnp.zeros((count, BAND), BF16)
            continue
        part = refs[source]
        rows = part.shape[0]
        for band, columns in enumerate(bands_of(part.shape[1])):
            picked[flow][pl.ds(start + band * rows, rows), :] = part[:, columns]


def spread_kernel(starts, chunks, message, *refs):
    parts = len(starts)
    results, wide, sems = (refs[parts : 2 * parts], refs[2 * parts : 3 * parts], refs[3 * parts])
    copies = []
    for index, start in enumerate(starts):
        rows = wide[index].shape[0]
        place = pl.ds(pl.multiple_of(chunks[index] * rows, rows), rows)
        for band, columns in enumerate(bands_of(wide[index].shape[1])):
            wide[index][:, columns] = message[pl.ds(start + band * rows, rows), :].astype(F32)
            copy = pltpu.make_async_copy(
                wide[index].at[:, columns],
                results[index].at[place, columns],
                sems.at[len(copies)],
            )
            copy.start()
            copies.append(copy)
    for copy in copies:
        copy.wait()


def whole_spec(shape):
    return pl.BlockSpec(shape, lambda step, chunk: (0,) * len(shape))


def row_spec(rows, width, place):
    return pl.BlockSpec((rows, width), lambda step, chunk: (chunk[place], 0))


def pick_chunks(plan, rows, chunks, sources):
    shapes = tuple(jax.ShapeDtypeStruct((count, BAND), BF16) for count in rows)
    return pl.pallas_call(
        functools.partial(pick_kernel, plan, len(rows)),
        grid_spec=pltpu.PrefetchScalarGridSpec(
            num_scalar_prefetch=1,
            grid=(1,),
            in_specs=[
                row_spec(count, array_in.shape[1], place)
                for place, (array_in, count) in enumerate(sources)
            ],
            out_specs=tuple(whole_spec(shape.shape) for shape in shapes),
        ),
        out_shape=shapes,
        name="pick",
        cost_estimate=pl.CostEstimate(
            flops=0, bytes_accessed=4 * sum(rows) * BAND, transcendentals=0
        ),
    )(chunks, *[array_in for array_in, count in sources])


def spread_chunks(starts, chunks, message, counts, results):
    kept = [pl.BlockSpec(memory_space=pl.ANY)] * len(results)
    shapes = [(count, result.shape[1]) for count, result in zip(counts, results)]
    copies = sum(width // BAND for count, width in shapes)
    return pl.pallas_call(
        functools.partial(spread_kernel, starts),
        in_specs=[
            pl.BlockSpec(memory_space=pltpu.SMEM),
            pl.BlockSpec(memory_space=pltpu.VMEM),
        ]
        + kept,
        out_specs=tuple(kept),
        out_shape=tuple(jax.ShapeDtypeStruct(result.shape, F32) for result in results),
        scratch_shapes=[pltpu.VMEM(shape, F32) for shape in shapes]
        + [pltpu.SemaphoreType.DMA((copies,))],
        input_output_aliases={2 + item: item for item in range(len(results))},
        name="spread",
        cost_estimate=pl.CostEstimate(
            flops=0, bytes_accessed=6 * message.size, transcendentals=0
        ),
    )(chunks, message, *results)


def heads_kernel(chunk, message, *refs):
    for item, result in enumerate(refs[-3:]):
        result[...] = message[:, item * PAIR : (item + 1) * PAIR].astype(F32)


def spread_heads(chip, message, results):
    rows, parts = message.shape[0], len(RING)
    shape = jax.ShapeDtypeStruct((rows, parts * PAIR), F32)
    spec = pl.BlockSpec((rows, PAIR), lambda step, chunk: (0, chunk[0]))
    return pl.pallas_call(
        heads_kernel,
        grid_spec=pltpu.PrefetchScalarGridSpec(
            num_scalar_prefetch=1,
            grid=(1,),
            in_specs=[whole_spec(message.shape)]
            + [pl.BlockSpec(memory_space=pl.ANY)] * len(results),
            out_specs=(spec,) * 3,
        ),
        out_shape=(shape,) * 3,
        input_output_aliases={2 + item: item for item in range(len(results))},
        name="spread_heads",
        cost_estimate=pl.CostEstimate(flops=0, bytes_accessed=6 * message.size, transcendentals=0),
    )(chip.reshape(1), message, *results)


def tie(*values):
    return lax.optimization_barrier(values)


def ring_pairs(way):
    count = len(RING)
    return [(RING[i], RING[(i + way) % count]) for i in range(count)]


def ring_place():
    return look_up([RING.index(c) for c in range(len(RING))], lax.axis_index("ctx"))


def ring_chip(place):
    return look_up(RING, jnp.mod(place, len(RING)))


def tiny_gather(values):
    sent = jnp.broadcast_to(values[None], (len(RING),) + values.shape)
    return lax.all_to_all(sent, "ctx", 0, 0, tiled=True)


class RingSum:
    def __init__(self, ahead, back, results, widths):
        self.flows = [(ahead, 1), (back, -1)]
        self.widths = widths
        self.me = ring_place()
        self.round = 0
        self.results = tuple(results)
        self.arrived = [None, None]
        self.ready = [None, None]
        self.arrays = {}
        self.last = 2 * (len(RING) - 1)
        self.rounds = self.last

    @property
    def done(self):
        return self.round == self.rounds

    def part_rows(self, part):
        return part[1] * (self.widths[part[3]] // BAND)

    def layout(self, parts, round_at):
        start, starts = (0, {})
        for index, part in enumerate(parts):
            if 0 <= round_at < self.last and (round_at > 0 or not part[4]):
                starts[index] = start
                start += self.part_rows(part)
        return (starts, start)

    def chunk(self, part, way, hops):
        return jnp.mod(self.me - way * hops, len(RING)) + part[2]

    def pick(self, round_at):
        self.picked = None
        plan, sources, chunks, message_rows = ([], [], [], [])
        for flow, (parts, way) in enumerate(self.flows):
            starts, rows = self.layout(parts, round_at)
            message_rows.append(rows)
            for index, start in starts.items():
                part = parts[index]
                hops = round_at
                if hops < len(RING):
                    plan.append((flow, start, len(sources), self.part_rows(part)))
                    sources.append((self.arrays[part[3]], part[1]))
                    chunks.append(self.chunk(part, way, hops))
                else:
                    plan.append((flow, start, None, self.part_rows(part)))
        if sources:
            self.picked = pick_chunks(tuple(plan), message_rows, jnp.stack(chunks), sources)

    def send_apart(self):
        plan, sources, chunks, message_rows = ([], [], [], [])
        for flow, (parts, way) in enumerate(self.flows):
            rows = 0
            for part in parts:
                if part[4]:
                    plan.append((flow, rows, len(sources), self.part_rows(part)))
                    sources.append((self.arrays[part[3]], part[1]))
                    chunks.append(self.chunk(part, way, 0))
                    rows += self.part_rows(part)
            message_rows.append(rows)
        messages = pick_chunks(tuple(plan), message_rows, jnp.stack(chunks), sources)
        self.apart = [
            lax.ppermute(message, "ctx", ring_pairs(way))
            for message, (parts, way) in zip(messages, self.flows)
        ]

    def make(self):
        self.ready = []
        for flow, (parts, way) in enumerate(self.flows):
            got = self.arrived[flow]
            if self.round == 0:
                self.ready.append(self.picked[flow])
                continue
            starts, rows = self.layout(parts, self.round)
            before, rows_before = self.layout(parts, self.round - 1)
            kept = [index for index in starts if index in before]
            if kept != list(before):
                got = jnp.concatenate(
                    [got[before[index] : before[index] + self.part_rows(parts[index])] for index in kept]
                )
            if self.picked is not None:
                picked = self.picked[flow]
                same = got.shape[0]
                added = (got.astype(F32) + picked[:same].astype(F32)).astype(BF16)
                if same < rows:
                    apart = self.apart[flow].astype(F32) + picked[same:].astype(F32)
                    added = jnp.concatenate([added, apart.astype(BF16)])
                got = added
            self.ready.append(got)

    def send(self):
        if self.done:
            return
        self.arrived = [
            lax.ppermute(held, "ctx", ring_pairs(way))
            for held, (parts, way) in zip(self.ready, self.flows)
        ]

    def absorb(self):
        if self.done:
            return
        self.round += 1
        self.landed = list(self.arrived)
        if not self.done:
            self.make()

    def prepare(self):
        if self.round + 1 < self.rounds:
            self.pick(self.round + 1)

    def place(self):
        results = list(self.results)
        for flow, (parts, way) in enumerate(self.flows):
            sent_starts, rows = self.layout(parts, self.round)
            came_starts, rows = self.layout(parts, self.round - 1)
            for starts, message, ends in (
                (sent_starts, self.ready[flow], False),
                (came_starts, self.landed[flow], True),
            ):
                picked, ids, counts, chunks = ([], [], [], [])
                for index, start in starts.items():
                    part = parts[index]
                    hops = self.round
                    if hops < len(RING) - 1 or ends != (hops == self.last):
                        continue
                    picked.append(start)
                    ids.append(part[3])
                    counts.append(part[1])
                    chunks.append(self.chunk(part, way, hops))
                if picked:
                    written = spread_chunks(
                        tuple(picked),
                        jnp.stack(chunks),
                        message,
                        counts,
                        [results[item] for item in ids],
                    )
                    for item, result in zip(ids, written):
                        results[item] = result
        self.results = tuple(results)


class RingGather:
    def __init__(self, block):
        self.me = ring_place()
        self.step = 0
        self.ready = (block, block)
        self.arrived = None
        self.results = ()
        self.arrays = ()
        self.landed = ()
        self.found = [(lax.axis_index("ctx"), block)]

    def send(self):
        if self.step == len(RING) // 2:
            return
        self.step += 1
        ahead, back = self.ready
        if self.step == len(RING) // 2:
            rows = ahead.shape[0] // 2
            ahead, back = (ahead[:rows], back[rows:])
        self.arrived = (
            lax.ppermute(ahead, "ctx", ring_pairs(1)),
            lax.ppermute(back, "ctx", ring_pairs(-1)),
        )

    def place(self):
        pass

    def prepare(self):
        pass

    def absorb(self):
        if len(self.found) == len(RING):
            return
        self.ready = self.arrived
        ahead, back = self.arrived
        if self.step < len(RING) // 2:
            self.found.append((ring_chip(self.me - self.step), ahead))
            self.found.append((ring_chip(self.me + self.step), back))
        else:
            self.found.append((ring_chip(self.me - self.step), jnp.concatenate([ahead, back])))


class HeadRing(RingGather):
    def __init__(self, block, results):
        super().__init__(block)
        self.results = results
        self.placed = 0

    def place(self):
        for chip, block in self.found[self.placed :]:
            self.results = spread_heads(chip, block, self.results)
        self.placed = len(self.found)


def stage(values, *rings):
    values, arrived = tie(values, [(ring.arrived, ring.results, ring.arrays) for ring in rings])
    for ring, blocks in zip(rings, arrived):
        ring.arrived, ring.results, ring.arrays = blocks
        ring.absorb()
    for ring in rings:
        ring.ready = list(ring.ready)
        for way in range(len(ring.ready)):
            values, ring.ready[way] = tie(values, ring.ready[way])
        ring.send()
        ring.prepare()
        ring.place()
    return values


def per_device_ring(
    tokens,
    cotangent,
    token_order,
    seq_lengths,
    rel_buckets,
    gain_attn,
    w_query,
    w_key,
    w_value,
    w_out,
    rel_bias,
    gain_ffn,
    w_gate,
    w_up,
    w_down,
):
    core = lax.axis_index("fsdp")
    ctx = lax.axis_index("ctx")
    tp = lax.axis_index("tp")
    local_rows = tokens.shape[0]
    half = w_query.shape[0]
    head_count = w_query.shape[1] // DH
    group_rows = local_rows * lax.axis_size("ctx")
    first = core == 0

    def halves(array_in):
        left, right = (array_in[:, :half], array_in[:, half:])
        return (jnp.where(first, left, right), jnp.where(first, right, left))

    def whole(own, other):
        return jnp.concatenate(
            [jnp.where(first, own, other), jnp.where(first, other, own)], axis=1
        )

    small = jnp.concatenate([gain_attn, gain_ffn, rel_bias.reshape(-1)])
    small_far = swap(small, "fsdp")
    wq_far, wk_far, wv_far = (swap(w_query, "fsdp"), swap(w_key, "fsdp"), swap(w_value, "fsdp"))
    wo_far = swap(w_out, "fsdp")
    wg_far, wu_far, wd_far = (swap(w_gate, "fsdp"), swap(w_up, "fsdp"), swap(w_down, "fsdp"))
    ga_own, ga_far = (gain_attn.astype(F32), small_far[:half].astype(F32))
    gf_own, gf_far = (gain_ffn.astype(F32), small_far[half : 2 * half].astype(F32))
    bias_far = small_far[2 * half :].reshape(rel_bias.shape)
    bias_local = jnp.where(
        first,
        jnp.concatenate([rel_bias, bias_far]),
        jnp.concatenate([bias_far, rel_bias]),
    )
    tok_own, tok_far = halves(tokens)
    cot_own, cot_far = halves(cotangent)
    tok_own, tok_far = (tok_own.astype(F32), tok_far.astype(F32))

    def norm_scale(own, far):
        total = jnp.sum(own * own, axis=1, keepdims=True) + jnp.sum(far * far, axis=1, keepdims=True)
        return lax.rsqrt(total / (2 * half) + EPS)

    scale_a = norm_scale(tok_own, tok_far)
    normed_own = (tok_own * scale_a * ga_own).astype(BF16)
    normed_far = (tok_far * scale_a * ga_far).astype(BF16)
    queries = (dot_f32(normed_own, w_query) + dot_f32(normed_far, wq_far)).astype(BF16)
    keys_here = (dot_f32(normed_own, w_key) + dot_f32(normed_far, wk_far)).astype(BF16)
    values_here = (dot_f32(normed_own, w_value) + dot_f32(normed_far, wv_far)).astype(BF16)
    parts = lax.axis_size("ctx")

    def by_heads(items):
        mixed = jnp.concatenate([item.reshape(local_rows, parts, 1, PAIR) for item in items], axis=2)
        mixed = jnp.transpose(mixed.reshape(local_rows, parts, len(items) * PAIR), (1, 0, 2))
        moved = lax.all_to_all(mixed, "ctx", 0, 0, tiled=True)
        return moved.reshape(group_rows, len(items) * PAIR)

    def by_rows(array_in):
        count = array_in.shape[1] // PAIR
        moved = lax.all_to_all(
            array_in.reshape(parts, local_rows, count * PAIR), "ctx", 0, 0, tiled=True
        )
        moved = jnp.transpose(moved.reshape(parts, local_rows, count, PAIR), (2, 1, 0, 3))
        return moved.reshape(count, local_rows, parts * PAIR)

    order_row = token_order
    order_col = token_order.reshape(group_rows, 1)
    low, high, offsets = sequence_plan(seq_lengths[0], group_rows)
    bias_pair = lax.dynamic_slice_in_dim(bias_local, ctx * 2, 2, axis=1)
    table, table_back = bias_tables(rel_buckets, bias_pair)
    mixed = by_heads([queries, keys_here, values_here])
    mixed, normed_block = tie(mixed, jnp.concatenate([normed_own, normed_far], axis=1))
    normed_ring = RingGather(normed_block)
    normed_ring.send()
    ordered, context_heads, exact, inverse, tops = group_attention(
        low, high, offsets, order_row, order_col, table, mixed
    )
    context_heads, normed_ring.arrived = tie(context_heads, normed_ring.arrived)
    normed_ring.absorb()
    context = by_rows(context_heads)[0]
    context, normed_ring.ready = tie(context, normed_ring.ready)
    normed_ring.send()

    def tp_sum(own, far):
        own, far = (own.astype(BF16), far.astype(BF16))
        return (
            own.astype(F32) + swap(own, "tp").astype(F32),
            far.astype(F32) + swap(far, "tp").astype(F32),
        )

    attn_parts = [dot_f32(context, w_out).astype(BF16), dot_f32(context, wo_far).astype(BF16)]
    attn_parts, cot_own, cot_far = tie(attn_parts, cot_own, cot_far)
    attn_own, attn_far = tp_sum(*attn_parts)
    hid_own, hid_far = (tok_own + attn_own, tok_far + attn_far)
    inner_grad = dot_nt(cot_own, w_down) + dot_nt(cot_far, wd_far)
    scale_f = norm_scale(hid_own, hid_far)
    nffn_own = (hid_own * scale_f * gf_own).astype(BF16)
    nffn_far = (hid_far * scale_f * gf_far).astype(BF16)
    nffn_own, nffn_far, normed_ring.arrived = tie(nffn_own, nffn_far, normed_ring.arrived)
    normed_ring.absorb()
    block_rows = local_rows // 2
    near, far = (slice(0, block_rows), slice(block_rows, local_rows))

    def both_ways(rows):
        ahead, back = normed_ring.ready
        return (
            lax.ppermute(ahead[rows], "ctx", ring_pairs(1)),
            lax.ppermute(back[rows], "ctx", ring_pairs(-1)),
        )

    third_near, third_far = (both_ways(near), both_ways(far))
    gate_pre = dot_f32(nffn_own, w_gate) + dot_f32(nffn_far, wg_far)
    up_pre = dot_f32(nffn_own, w_up) + dot_f32(nffn_far, wu_far)
    inner_act = geglu(gate_pre, up_pre).astype(BF16)
    unused, geglu_back = jax.vjp(geglu, gate_pre, up_pre)
    gate_grad, up_grad = geglu_back(inner_grad)
    gate_grad = gate_grad.astype(BF16)
    up_grad = up_grad.astype(BF16)

    gate_grad, up_grad, inner_act, third_near, third_far = tie(
        gate_grad, up_grad, inner_act, third_near, third_far
    )
    last = (
        lax.ppermute(third_near[0], "ctx", ring_pairs(1)),
        lax.ppermute(third_far[1], "ctx", ring_pairs(-1)),
    )

    def pair_rows(own):
        return jnp.concatenate([own, swap(own, "fsdp")])

    def pair_half(own, far):
        return jnp.concatenate([own, swap(far, "fsdp")])

    nffn_pair = pair_half(nffn_own, nffn_far)
    gate_pair, up_pair, act_pair = (pair_rows(gate_grad), pair_rows(up_grad), pair_rows(inner_act))
    cot_pair = pair_half(cot_own, cot_far)
    dnf_parts = [
        (dot_nt(gate_grad, w_gate) + dot_nt(up_grad, w_up)).astype(BF16),
        (dot_nt(gate_grad, wg_far) + dot_nt(up_grad, wu_far)).astype(BF16),
    ]
    dnf_parts, nffn_pair, act_pair = tie(dnf_parts, nffn_pair, act_pair)
    dnf_own, dnf_far = tp_sum(*dnf_parts)
    grad_down = dot_tn(act_pair, cot_pair).astype(BF16)
    grad_gate = dot_tn(nffn_pair, gate_pair).astype(BF16)
    grad_up = dot_tn(nffn_pair, up_pair).astype(BF16)
    parts_round = len(RING)
    grad_rows = grad_gate.shape[0] // parts_round
    down_rows = grad_down.shape[0] // (2 * parts_round)
    out_rows = w_out.shape[0] // (2 * parts_round)
    out_shape = (w_out.shape[0], half)
    blanks = blank_arrays(
        [grad_gate.shape, grad_up.shape, grad_down.shape, out_shape] + [w_query.shape] * 3
    )
    ring = RingSum(
        [
            (None, grad_rows, 0, 0, False),
            (None, down_rows, 0, 2, False),
            (None, out_rows, 0, 3, True),
        ],
        [
            (None, grad_rows, 0, 1, False),
            (None, down_rows, parts_round, 2, False),
            (None, out_rows, parts_round, 3, True),
        ],
        blanks[:4],
        [grad_gate.shape[1], grad_up.shape[1], half, half],
    )
    ring.arrays = {0: grad_gate, 1: grad_up, 2: grad_down}
    ring.pick(0)
    ring.make()
    ring.send()

    def norm_back(own, far, scale, gain_own, gain_far, dy_own, dy_far):
        mean_term = (
            jnp.sum(gain_own * dy_own * own, axis=1, keepdims=True)
            + jnp.sum(gain_far * dy_far * far, axis=1, keepdims=True)
        ) / (2 * half)
        cubed = scale * scale * scale * mean_term
        return (
            scale * (gain_own * dy_own) - own * cubed,
            scale * (gain_far * dy_far) - far * cubed,
            jnp.sum(dy_own * own * scale, axis=0),
            jnp.sum(dy_far * far * scale, axis=0),
        )

    back_own, back_far, dgf_own, dgf_far = norm_back(
        hid_own, hid_far, scale_f, gf_own, gf_far, dnf_own, dnf_far
    )
    hgrad_own = cot_own.astype(F32) + back_own
    hgrad_far = cot_far.astype(F32) + back_far
    ag_own, ag_far = (hgrad_own.astype(BF16), hgrad_far.astype(BF16))
    grad_out = dot_tn(pair_rows(context), pair_half(ag_own, ag_far)).astype(BF16)
    context_grad = dot_nt(ag_own, w_out) + dot_nt(ag_far, wo_far)
    context_grad, ring.ready = tie(context_grad.astype(BF16), ring.ready)
    grad_mixed = by_heads([context_grad])
    ring.arrays[3] = grad_out
    ring.send_apart()
    ring.prepare()
    stage((), ring)
    plan = (low, high, offsets, order_row, order_col, table_back, ordered, exact, inverse)
    first_held, first_slanted, ordered_grad = group_attention_back(
        0, *plan, grad_mixed, jnp.zeros((16, 3 * PAIR), BF16), (*ring.picked, *ring.ready)
    )
    first_held, ordered_grad = stage((first_held, ordered_grad), ring)
    outgoing, second_slanted, unused = group_attention_back(
        1, *plan, ordered_grad, first_held, tuple(ring.ready)
    )
    slanted = jnp.stack([first_slanted, second_slanted])
    outgoing, tops = stage((outgoing, tops), ring)
    found = [(chip * local_rows, block) for chip, block in normed_ring.found]
    for hops, ends in ((-3, (third_near[0], third_far[0])), (3, (third_near[1], third_far[1])), (4, last)):
        start = ring_chip(ring_place() + hops) * local_rows
        found += [(start, ends[0]), (start + block_rows, ends[1])]
    outgoing, blocks = tie(outgoing, [block for start, block in found])
    query_grad, key_grad, value_grad = by_rows(outgoing)
    outgoing_turned = jnp.concatenate(
        [
            lax.dynamic_slice_in_dim(outgoing, start, block.shape[0])
            for start, block in found
        ]
    )
    head_grads = dot_tn(jnp.concatenate(blocks), outgoing_turned)
    head_grads, head_grads_sent = (head_grads[:half], head_grads[half:].astype(BF16))
    head_grads = (head_grads + swap(head_grads_sent, "fsdp").astype(F32)).astype(BF16)
    head_grads = stage(head_grads, ring)
    head_ring = HeadRing(head_grads, blanks[4:])
    head_ring.send()
    head_ring.place()
    dn_parts = (
        dot_nt(query_grad, w_query) + dot_nt(key_grad, w_key) + dot_nt(value_grad, w_value),
        dot_nt(query_grad, wq_far) + dot_nt(key_grad, wk_far) + dot_nt(value_grad, wv_far),
    )
    dn_parts = (dn_parts[0].astype(BF16), dn_parts[1].astype(BF16))
    dn_own, dn_far = tp_sum(*dn_parts)
    dn_own, dn_far, inner_act = stage((dn_own, dn_far, inner_act), ring, head_ring)
    tback_own, tback_far, dga_own, dga_far = norm_back(
        tok_own, tok_far, scale_a, ga_own, ga_far, dn_own, dn_far
    )
    grad_tokens = whole(hgrad_own + tback_own, hgrad_far + tback_far)
    ffn_own, ffn_far = tp_sum(dot_f32(inner_act, w_down), dot_f32(inner_act, wd_far))
    output = whole(hid_own + ffn_own, hid_far + ffn_far).astype(BF16)
    pair_top = jnp.max(tops, axis=(1, 2))
    here = jnp.arange(parts, dtype=jnp.int32)[:, None] == ctx
    pair_bias = bucket_sums(rel_buckets, slanted)
    grad_bias = jnp.transpose(
        jnp.where(here[:, :, None], pair_bias[None], 0.0).reshape(head_count, NB)
    )
    bias_flat = grad_bias.reshape(2, -1)
    small_own = jnp.concatenate(
        [dga_own, dgf_own, jnp.where(first, bias_flat[0], bias_flat[1]), pair_top]
    )
    small_sent = jnp.concatenate(
        [dga_far, dgf_far, jnp.where(first, bias_flat[1], bias_flat[0]), pair_top]
    )
    small_got = swap(small_sent, "fsdp")
    grad_tokens, output, small_own, small_got = stage(
        (grad_tokens, output, small_own, small_got), ring, head_ring
    )
    small_both = jnp.concatenate(
        [small_own[:-2] + small_got[:-2], jnp.maximum(small_own[-2:], small_got[-2:])]
    )
    small_all = tiny_gather(small_both)
    stage((), ring, head_ring)
    head_maxima = small_all[:, -2:].reshape(head_count)
    small_sum = jnp.sum(small_all[:, :-2], axis=0)
    final_gain_a, final_gain_f = (small_sum[:half], small_sum[half : 2 * half])
    final_bias = small_sum[2 * half :].reshape(rel_bias.shape)
    clip_scale = TAU_CLIP / jnp.maximum(head_maxima, TAU_CLIP)
    column_scale = jnp.repeat(jnp.sqrt(clip_scale), DH)
    query_clipped = (w_query.astype(F32) * column_scale[None, :]).astype(BF16)
    key_clipped = (w_key.astype(F32) * column_scale[None, :]).astype(BF16)
    others = (
        grad_tokens,
        output,
        final_gain_a,
        final_gain_f,
        final_bias,
        head_maxima,
        query_clipped,
        key_clipped,
    )
    while not ring.done:
        stage((), ring, head_ring)
        if ring.round == len(RING) + 2:
            others, ring.arrived = tie(others, ring.arrived)
    final_gate, final_up, final_down, final_out = ring.results
    final_query, final_key, final_value = head_ring.results
    (
        grad_tokens,
        output,
        final_gain_a,
        final_gain_f,
        final_bias,
        head_maxima,
        query_clipped,
        key_clipped,
    ) = others
    return (
        output,
        grad_tokens,
        final_gain_a,
        final_query,
        final_key,
        final_value,
        final_out,
        final_bias,
        final_gain_f,
        final_gate,
        final_up,
        final_down,
        head_maxima,
        query_clipped,
        key_clipped,
    )


def pick_program(mesh):
    sizes = dict(mesh.shape)
    if sizes["fsdp"] == 2 and sizes["ctx"] == len(RING) and sizes["tp"] == 2:
        return per_device_ring
    return per_device_generic


def solution(mesh):
    in_specs = (
        P(("fsdp", "ctx"), None),
        P(("fsdp", "ctx"), None),
        P("fsdp", None),
        P("fsdp", None),
        P(),
        P("fsdp"),
        P("fsdp", "tp"),
        P("fsdp", "tp"),
        P("fsdp", "tp"),
        P("tp", "fsdp"),
        P("fsdp", "tp"),
        P("fsdp"),
        P("fsdp", "tp"),
        P("fsdp", "tp"),
        P("tp", "fsdp"),
    )
    out_specs = (
        P(("fsdp", "ctx"), None),
        P(("fsdp", "ctx"), None),
        P("fsdp"),
        P("fsdp", "tp"),
        P("fsdp", "tp"),
        P("fsdp", "tp"),
        P("tp", "fsdp"),
        P("fsdp", "tp"),
        P("fsdp"),
        P("fsdp", "tp"),
        P("fsdp", "tp"),
        P("tp", "fsdp"),
        P("tp"),
        P("fsdp", "tp"),
        P("fsdp", "tp"),
    )
    per_device = pick_program(mesh)
    return jax.shard_map(
        per_device, mesh=mesh, in_specs=in_specs, out_specs=out_specs, check_vma=False
    )
```

```python
import functools

import jax
import jax.numpy as jnp
from jax import lax
from jax.experimental import pallas as pl
from jax.experimental.pallas import tpu as pltpu
from jax.sharding import PartitionSpec as P

DH = 64
NB = 32


EPS = 1e-06
TAU_CLIP = 6.0


def rms_norm(values, gain):
    return values * lax.rsqrt(jnp.mean(values * values, axis=-1, keepdims=True) + EPS) * gain


def geglu(gate_pre, up_pre):
    return jax.nn.gelu(gate_pre, approximate=True) * up_pre


def segment_of(positions, lengths_row):
    offsets = jnp.cumsum(lengths_row) - lengths_row
    return jnp.sum((positions[:, None] >= offsets[None, :]).astype(jnp.int32), axis=1) - 1


def bucket_ranges(rel_buckets):
    table_len = rel_buckets.shape[0]
    index_all = jnp.arange(table_len, dtype=jnp.int32)
    bucket_ids = jnp.arange(NB, dtype=jnp.int32)
    matched = rel_buckets[:, None] == bucket_ids[None, :]
    range_first = jnp.min(jnp.where(matched, index_all[:, None], table_len), axis=0)
    range_last = jnp.max(jnp.where(matched, index_all[:, None], -1), axis=0)
    return (range_first, range_last, table_len)


def pair_terms(query_pos, query_seg, key_pos, key_seg, ranges, bias_table):
    range_first, range_last, table_len = ranges
    longest = (table_len + 1) // 2
    offset = jnp.clip(key_pos[None, :] - query_pos[:, None] + longest - 1, 0, 2 * longest - 2)
    inside = (offset[None, :, :] >= range_first[:, None, None]) & (
        offset[None, :, :] <= range_last[:, None, None]
    )
    bucket_hot = inside.astype(jnp.bfloat16)
    pair_bias = jnp.einsum(
        "btk,bh->htk", bucket_hot, bias_table, preferred_element_type=jnp.float32
    )
    same_seq = (query_seg[:, None] == key_seg[None, :])[None]
    return (bucket_hot, pair_bias, same_seq)


def per_device_generic(
    tokens,
    cotangent,
    token_order,
    seq_lengths,
    rel_buckets,
    gain_attn,
    w_query,
    w_key,
    w_value,
    w_out,
    rel_bias,
    gain_ffn,
    w_gate,
    w_up,
    w_down,
):
    local_rows = tokens.shape[0]
    head_count = w_query.shape[1] // DH
    group_rows = local_rows * lax.axis_size("ctx")
    key_block = min(512, group_rows)
    block_count = group_rows // key_block
    ranges = bucket_ranges(rel_buckets)
    gain_a, full_query, full_key, full_value, full_out, bias_local = (
        lax.all_gather(gain_attn, "fsdp", axis=0, tiled=True),
        lax.all_gather(w_query, "fsdp", axis=0, tiled=True),
        lax.all_gather(w_key, "fsdp", axis=0, tiled=True),
        lax.all_gather(w_value, "fsdp", axis=0, tiled=True),
        lax.all_gather(w_out, "fsdp", axis=1, tiled=True),
        lax.all_gather(rel_bias, "fsdp", axis=0, tiled=True),
    )
    tokens_f = tokens.astype(jnp.float32)
    gain_a32 = gain_a.astype(jnp.float32)
    normed = rms_norm(tokens_f, gain_a32).astype(jnp.bfloat16)
    queries = jnp.dot(normed, full_query, preferred_element_type=jnp.float32).astype(jnp.bfloat16)
    keys_here = jnp.dot(normed, full_key, preferred_element_type=jnp.float32).astype(jnp.bfloat16)
    values_here = jnp.dot(normed, full_value, preferred_element_type=jnp.float32).astype(
        jnp.bfloat16
    )
    order_row = token_order[0]
    seq_ids = segment_of(order_row, seq_lengths[0])
    row_start = lax.axis_index("ctx") * local_rows
    query_pos = lax.dynamic_slice_in_dim(order_row, row_start, local_rows)
    query_seg = lax.dynamic_slice_in_dim(seq_ids, row_start, local_rows)
    pos_blocks = order_row.reshape(block_count, key_block)
    seg_blocks = seq_ids.reshape(block_count, key_block)
    query_heads = queries.reshape(local_rows, head_count, DH)
    key_all, value_all = (
        lax.all_gather(keys_here, "ctx", axis=0, tiled=True),
        lax.all_gather(values_here, "ctx", axis=0, tiled=True),
    )

    def blocked(array_in):
        return array_in.reshape(block_count, key_block, head_count, DH)

    def forward_block(running, inputs):
        summed, totals, head_top = running
        key_blk, value_blk, pos_blk, seg_blk = inputs
        raw_scores = jnp.einsum(
            "thd,khd->htk", query_heads, key_blk, preferred_element_type=jnp.float32
        )
        bucket_hot, pair_bias, same_seq = pair_terms(
            query_pos, query_seg, pos_blk, seg_blk, ranges, bias_local
        )
        weights = jnp.where(same_seq, jnp.exp(raw_scores + pair_bias), 0.0)
        totals = totals + jnp.sum(weights, axis=2)
        summed = summed + jnp.einsum(
            "htk,khd->thd",
            weights.astype(jnp.bfloat16),
            value_blk,
            preferred_element_type=jnp.float32,
        )
        head_top = jnp.maximum(
            head_top, jnp.max(jnp.where(same_seq, raw_scores, -1e30), axis=(1, 2))
        )
        return ((summed, totals, head_top), None)

    start_state = (
        jnp.zeros((local_rows, head_count, DH), jnp.float32),
        jnp.zeros((head_count, local_rows), jnp.float32),
        jnp.full((head_count,), -1e30, jnp.float32),
    )
    (summed, totals, head_top), unused = lax.scan(
        forward_block, start_state, (blocked(key_all), blocked(value_all), pos_blocks, seg_blocks)
    )
    row_totals = jnp.transpose(totals)[:, :, None]
    context_exact = summed / row_totals
    context = context_exact.reshape(local_rows, head_count * DH).astype(jnp.bfloat16)
    head_maxima = lax.pmax(head_top, ("fsdp", "ctx"))
    attn_out = lax.psum(
        jnp.dot(context, full_out, preferred_element_type=jnp.float32).astype(jnp.bfloat16), "tp"
    ).astype(jnp.float32)
    hidden_state = tokens_f + attn_out
    gain_f, full_gate, full_up, full_down = (
        lax.all_gather(gain_ffn, "fsdp", axis=0, tiled=True),
        lax.all_gather(w_gate, "fsdp", axis=0, tiled=True),
        lax.all_gather(w_up, "fsdp", axis=0, tiled=True),
        lax.all_gather(w_down, "fsdp", axis=1, tiled=True),
    )
    gain_f32 = gain_f.astype(jnp.float32)
    normed_ffn = rms_norm(hidden_state, gain_f32).astype(jnp.bfloat16)
    gate_pre = jnp.dot(normed_ffn, full_gate, preferred_element_type=jnp.float32)
    up_pre = jnp.dot(normed_ffn, full_up, preferred_element_type=jnp.float32)
    inner_act = geglu(gate_pre, up_pre).astype(jnp.bfloat16)
    ffn_out = lax.psum(
        jnp.dot(inner_act, full_down, preferred_element_type=jnp.float32).astype(jnp.bfloat16), "tp"
    ).astype(jnp.float32)
    output = (hidden_state + ffn_out).astype(jnp.bfloat16)
    grad_down = jnp.einsum("tf,td->fd", inner_act, cotangent, preferred_element_type=jnp.float32)
    inner_grad = jnp.einsum("td,fd->tf", cotangent, full_down, preferred_element_type=jnp.float32)
    unused, geglu_back = jax.vjp(geglu, gate_pre, up_pre)
    gate_grad, up_grad = geglu_back(inner_grad)
    gate_grad = gate_grad.astype(jnp.bfloat16)
    up_grad = up_grad.astype(jnp.bfloat16)
    grad_gate = jnp.einsum("tc,tf->cf", normed_ffn, gate_grad, preferred_element_type=jnp.float32)
    grad_up = jnp.einsum("tc,tf->cf", normed_ffn, up_grad, preferred_element_type=jnp.float32)
    ffn_term = jnp.einsum(
        "tf,cf->tc", gate_grad, full_gate, preferred_element_type=jnp.float32
    ) + jnp.einsum("tf,cf->tc", up_grad, full_up, preferred_element_type=jnp.float32)
    normed_ffn_grad = lax.psum(ffn_term.astype(jnp.bfloat16), "tp").astype(jnp.float32)
    unused, norm_ffn_back = jax.vjp(rms_norm, hidden_state, gain_f32)
    hidden_norm_grad, grad_gain_ffn = norm_ffn_back(normed_ffn_grad)
    hidden_grad = cotangent.astype(jnp.float32) + hidden_norm_grad
    attn_grad = hidden_grad.astype(jnp.bfloat16)
    grad_out = jnp.einsum("tc,td->cd", context, attn_grad, preferred_element_type=jnp.float32)
    context_grad = jnp.einsum(
        "td,cd->tc", attn_grad, full_out, preferred_element_type=jnp.float32
    ).reshape(local_rows, head_count, DH)
    summed_grad = (context_grad / row_totals).astype(jnp.bfloat16)
    total_grad = jnp.transpose(-jnp.sum(context_grad * context_exact, axis=2) / row_totals[:, :, 0])
    key_back, value_back = (key_all, value_all)

    def backward_block(running, inputs):
        query_acc, bias_acc = running
        key_blk, value_blk, pos_blk, seg_blk = inputs
        raw_scores = jnp.einsum(
            "thd,khd->htk", query_heads, key_blk, preferred_element_type=jnp.float32
        )
        bucket_hot, pair_bias, same_seq = pair_terms(
            query_pos, query_seg, pos_blk, seg_blk, ranges, bias_local
        )
        weights = jnp.where(same_seq, jnp.exp(raw_scores + pair_bias), 0.0)
        prob_grad = (
            jnp.einsum("thd,khd->htk", summed_grad, value_blk, preferred_element_type=jnp.float32)
            + total_grad[:, :, None]
        )
        score_grad = (weights * prob_grad).astype(jnp.bfloat16)
        query_acc = query_acc + jnp.einsum(
            "htk,khd->thd", score_grad, key_blk, preferred_element_type=jnp.float32
        )
        key_grad = jnp.einsum(
            "htk,thd->khd", score_grad, query_heads, preferred_element_type=jnp.float32
        )
        value_grad = jnp.einsum(
            "htk,thd->khd",
            weights.astype(jnp.bfloat16),
            summed_grad,
            preferred_element_type=jnp.float32,
        )
        bucket_sums = jnp.einsum(
            "htk,btk->hb", score_grad, bucket_hot, preferred_element_type=jnp.float32
        )
        return ((query_acc, bias_acc + bucket_sums), (key_grad, value_grad))

    zero_state = (
        jnp.zeros((local_rows, head_count, DH), jnp.float32),
        jnp.zeros((head_count, NB), jnp.float32),
    )
    (query_acc, bias_acc), (key_grads, value_grads) = lax.scan(
        backward_block, zero_state, (blocked(key_back), blocked(value_back), pos_blocks, seg_blocks)
    )
    key_grad_all, value_grad_all = (
        lax.psum_scatter(
            key_grads.reshape(group_rows, head_count * DH).astype(jnp.bfloat16),
            "ctx",
            scatter_dimension=0,
            tiled=True,
        ).astype(jnp.float32),
        lax.psum_scatter(
            value_grads.reshape(group_rows, head_count * DH).astype(jnp.bfloat16),
            "ctx",
            scatter_dimension=0,
            tiled=True,
        ).astype(jnp.float32),
    )
    query_grad = query_acc.reshape(local_rows, head_count * DH).astype(jnp.bfloat16)
    key_grad = key_grad_all.astype(jnp.bfloat16)
    value_grad = value_grad_all.astype(jnp.bfloat16)
    attn_term = jnp.einsum("tc,dc->td", query_grad, full_query, preferred_element_type=jnp.float32)
    attn_term = attn_term + jnp.einsum(
        "tc,dc->td", key_grad, full_key, preferred_element_type=jnp.float32
    )
    attn_term = attn_term + jnp.einsum(
        "tc,dc->td", value_grad, full_value, preferred_element_type=jnp.float32
    )
    normed_grad = lax.psum(attn_term.astype(jnp.bfloat16), "tp").astype(jnp.float32)
    unused, norm_attn_back = jax.vjp(rms_norm, tokens_f, gain_a32)
    token_norm_grad, grad_gain_attn = norm_attn_back(normed_grad)
    grad_tokens = hidden_grad + token_norm_grad
    grad_query = jnp.einsum("td,tc->dc", normed, query_grad, preferred_element_type=jnp.float32)
    grad_key = jnp.einsum("td,tc->dc", normed, key_grad, preferred_element_type=jnp.float32)
    grad_value = jnp.einsum("td,tc->dc", normed, value_grad, preferred_element_type=jnp.float32)
    grad_bias = jnp.transpose(bias_acc)
    (
        share_gain_a,
        share_query,
        share_key,
        share_value,
        share_out,
        share_bias,
        share_gain_f,
        share_gate,
        share_up,
        share_down,
    ) = (
        lax.psum_scatter(
            grad_gain_attn.astype(jnp.bfloat16), "fsdp", scatter_dimension=0, tiled=True
        ).astype(jnp.float32),
        lax.psum_scatter(
            grad_query.astype(jnp.bfloat16), "fsdp", scatter_dimension=0, tiled=True
        ).astype(jnp.float32),
        lax.psum_scatter(
            grad_key.astype(jnp.bfloat16), "fsdp", scatter_dimension=0, tiled=True
        ).astype(jnp.float32),
        lax.psum_scatter(
            grad_value.astype(jnp.bfloat16), "fsdp", scatter_dimension=0, tiled=True
        ).astype(jnp.float32),
        lax.psum_scatter(
            grad_out.astype(jnp.bfloat16), "fsdp", scatter_dimension=1, tiled=True
        ).astype(jnp.float32),
        lax.psum_scatter(
            grad_bias.astype(jnp.bfloat16), "fsdp", scatter_dimension=0, tiled=True
        ).astype(jnp.float32),
        lax.psum_scatter(
            grad_gain_ffn.astype(jnp.bfloat16), "fsdp", scatter_dimension=0, tiled=True
        ).astype(jnp.float32),
        lax.psum_scatter(
            grad_gate.astype(jnp.bfloat16), "fsdp", scatter_dimension=0, tiled=True
        ).astype(jnp.float32),
        lax.psum_scatter(
            grad_up.astype(jnp.bfloat16), "fsdp", scatter_dimension=0, tiled=True
        ).astype(jnp.float32),
        lax.psum_scatter(
            grad_down.astype(jnp.bfloat16), "fsdp", scatter_dimension=1, tiled=True
        ).astype(jnp.float32),
    )
    (
        final_gain_a,
        final_query,
        final_key,
        final_value,
        final_out,
        final_bias,
        final_gain_f,
        final_gate,
        final_up,
        final_down,
    ) = (
        lax.psum(share_gain_a.astype(jnp.bfloat16), "ctx").astype(jnp.float32),
        lax.psum(share_query.astype(jnp.bfloat16), "ctx").astype(jnp.float32),
        lax.psum(share_key.astype(jnp.bfloat16), "ctx").astype(jnp.float32),
        lax.psum(share_value.astype(jnp.bfloat16), "ctx").astype(jnp.float32),
        lax.psum(share_out.astype(jnp.bfloat16), "ctx").astype(jnp.float32),
        lax.psum(share_bias.astype(jnp.bfloat16), "ctx").astype(jnp.float32),
        lax.psum(share_gain_f.astype(jnp.bfloat16), "ctx").astype(jnp.float32),
        lax.psum(share_gate.astype(jnp.bfloat16), "ctx").astype(jnp.float32),
        lax.psum(share_up.astype(jnp.bfloat16), "ctx").astype(jnp.float32),
        lax.psum(share_down.astype(jnp.bfloat16), "ctx").astype(jnp.float32),
    )
    clip_scale = TAU_CLIP / jnp.maximum(head_maxima, TAU_CLIP)
    column_scale = jnp.repeat(jnp.sqrt(clip_scale), DH)
    query_clipped = (w_query.astype(jnp.float32) * column_scale[None, :]).astype(jnp.bfloat16)
    key_clipped = (w_key.astype(jnp.float32) * column_scale[None, :]).astype(jnp.bfloat16)
    return (
        output,
        grad_tokens,
        final_gain_a,
        final_query,
        final_key,
        final_value,
        final_out,
        final_bias,
        final_gain_f,
        final_gate,
        final_up,
        final_down,
        head_maxima,
        query_clipped,
        key_clipped,
    )


RING = (0, 2, 4, 6, 7, 5, 3, 1)
F32 = jnp.float32
BF16 = jnp.bfloat16


def look_up(table, index):
    found = jnp.int32(table[0])
    for place in range(1, len(table)):
        found = jnp.where(index == place, table[place], found)
    return found


def swap(array_in, axis_name):
    return lax.ppermute(array_in, axis_name, [(0, 1), (1, 0)])


def dot_f32(left, right):
    return jnp.dot(left, right, preferred_element_type=F32)


def dot_nt(left, right):
    return lax.dot_general(left, right, (((1,), (1,)), ((), ())), preferred_element_type=F32)


def dot_tn(left, right):
    return lax.dot_general(left, right, (((0,), (0,)), ((), ())), preferred_element_type=F32)


BAND = 512


TILE = 256
PAIR = 2 * DH
FAR_OFF = 1e30


def lane_of(rows):
    return lax.broadcasted_iota(jnp.int32, (rows, PAIR), 1)


def head_lanes(lane, head):
    own = lane < DH if head == 0 else lane >= DH
    spare = lane - DH if head == 0 else lane
    return (own, spare)


def sequence_of(offsets, start):
    position = start + lax.broadcasted_iota(jnp.int32, (TILE, PAIR), 0)
    sequence = jnp.zeros((TILE, PAIR), jnp.int32)
    for item in range(1, offsets.shape[0]):
        sequence = sequence + (position >= offsets[item]).astype(jnp.int32)
    return sequence


def tile_rows(index):
    return pl.ds(pl.multiple_of(index * TILE, TILE), TILE)


MOVED = 1024


def moved_rows(index):
    return pl.ds(pl.multiple_of(index * MOVED, MOVED), MOVED)


def put_in_order(order_row, source, target):
    @pl.loop(0, source.shape[0] // MOVED)
    def part(index):
        position = index * MOVED + lax.broadcasted_iota(jnp.int32, (MOVED, source.shape[0]), 0)
        hot = (order_row[...] == position).astype(F32).astype(BF16)
        target[moved_rows(index), :] = dot_f32(hot, source[...]).astype(BF16)


def put_back(order_col, source, target):
    @pl.loop(0, source.shape[0] // MOVED)
    def part(index):
        position = lax.broadcasted_iota(jnp.int32, (MOVED, source.shape[0]), 1)
        hot = (order_col[moved_rows(index), :] == position).astype(F32).astype(BF16)
        target[moved_rows(index), :] = dot_f32(hot, source[...]).astype(BF16)


def tile_pairs(low, high, tiles):
    pairs = (high - low + 1) // 2
    return (jnp.minimum(low, tiles - 2 * pairs), pairs)


def strip_place(distance, reach):
    return tile_rows(jnp.clip(distance + reach, 0, 2 * reach))


def fill_strip(strip, table):
    width = table.shape[1]
    for head in range(2):
        row = jnp.broadcast_to(table[pl.ds(head, 1), :], (TILE, width))
        strip[head] = pltpu.roll(row, 1, 1, stride=1, stride_axis=0)


def score_operands(query, key, sequence, head):
    own, spare = head_lanes(lane_of(TILE), head)
    differs = jnp.where((spare < 8) & (sequence != spare), 1.0, 0.0)
    blocked = jnp.where(sequence == spare, -FAR_OFF, 0.0)
    return (
        jnp.where(own, query, differs).astype(BF16),
        jnp.where(own, key, blocked).astype(BF16),
    )


def attend_kernel(
    low, high, offsets, order_row, order_col, table, mixed,
    ordered, context, exact, inverse, tops,
    query_aug, key_aug, value_aug, strip, total, held,
):
    tiles = mixed.shape[0] // TILE
    reach = strip.shape[2] // TILE // 2
    lane = lane_of(TILE)
    fill_strip(strip, table)
    put_in_order(order_row, mixed, ordered)
    tops[...] = jnp.full(tops.shape, -FAR_OFF, F32)

    @pl.loop(0, tiles)
    def arrange(index):
        rows = tile_rows(index)
        block = ordered[rows, :].astype(F32)
        sequence = sequence_of(offsets, index * TILE)
        for head in range(2):
            own, spare = head_lanes(lane, head)
            query, key = score_operands(
                block[:, :PAIR], block[:, PAIR : 2 * PAIR], sequence, head
            )
            query_aug[head, rows, :] = query
            key_aug[head, rows, :] = key
            value_aug[head, rows, :] = jnp.where(
                own, block[:, 2 * PAIR :], jnp.where(spare == 0, 1.0, 0.0)
            ).astype(BF16)

    @pl.loop(0, tiles)
    def attend(index):
        rows = tile_rows(index)
        total[...] = jnp.zeros(total.shape, F32)

        start, pairs = tile_pairs(low[index], high[index], tiles)

        @pl.loop(0, pairs)
        def keys(pair):
            others = [start + 2 * pair, start + 2 * pair + 1]
            columns = [tile_rows(other) for other in others]
            places = [strip_place(other - index, reach) for other in others]
            cases = [(head, side) for head in range(2) for side in range(2)]
            raws = [
                dot_nt(query_aug[head, rows, :], key_aug[head, columns[side], :])
                for head, side in cases
            ]
            weights = [
                jnp.exp(raw + strip[head, :, places[side]]).astype(BF16)
                for raw, (head, side) in zip(raws, cases)
            ]
            for head in range(2):
                tops[head] = jnp.maximum(
                    tops[head],
                    jnp.max(
                        jnp.maximum(raws[2 * head], raws[2 * head + 1]).reshape(
                            TILE // 8, 8, TILE
                        ),
                        axis=0,
                    ),
                )
                total[head] += dot_f32(
                    weights[2 * head], value_aug[head, columns[0], :]
                ) + dot_f32(weights[2 * head + 1], value_aug[head, columns[1], :])

        parts = []
        for head in range(2):
            summed = total[head]
            spot = DH if head == 0 else 0
            row_total = summed[:, spot : spot + 1]
            parts.append((summed / row_total, jnp.broadcast_to(1.0 / row_total, summed.shape)))
        first = lane < DH
        result = jnp.where(first, parts[0][0], parts[1][0])
        exact[rows, :] = result
        inverse[rows, :] = jnp.where(first, parts[0][1], parts[1][1])
        held[rows, :] = result.astype(BF16)

    put_back(order_col, held, context)


def attend_back_kernel(
    head, low, high, offsets, order_row, order_col, table, ordered, exact, inverse, incoming,
    other_held, *refs,
):
    outgoing, slanted, moved = refs[-17:-14]
    (
        query_aug, key_aug, value_aug, grad_aug, grad_plain, key_turned,
        strip, gathered, query_turned, key_sum, value_sum, held, weights, scores,
    ) = refs[-14:]
    rows_all = ordered.shape[0]
    tiles = rows_all // TILE
    width = gathered.shape[1]
    reach = width // TILE // 2
    own, spare = head_lanes(lane_of(TILE), head)
    strip[...] = pltpu.roll(
        jnp.broadcast_to(table[pl.ds(head, 1), :], (TILE, width)), 1, 1, stride=1, stride_axis=0
    )
    if head == 0:
        put_in_order(order_row, incoming, moved)
    else:
        moved = incoming
    gathered[...] = jnp.zeros(gathered.shape, F32)
    key_sum[...] = jnp.zeros(key_sum.shape, F32)
    value_sum[...] = jnp.zeros(value_sum.shape, F32)

    @pl.loop(0, tiles)
    def arrange(index):
        rows = tile_rows(index)
        block = ordered[rows, :].astype(F32)
        sequence = sequence_of(offsets, index * TILE)
        scaled = moved[rows, :].astype(F32) * inverse[rows, :]
        grad_plain[rows, :] = scaled.astype(BF16)
        key_turned[:, rows] = block[:, PAIR : 2 * PAIR].T.astype(BF16)
        query, key = score_operands(block[:, :PAIR], block[:, PAIR : 2 * PAIR], sequence, head)
        query_aug[rows, :] = query
        key_aug[rows, :] = key
        value_aug[rows, :] = jnp.where(
            own, block[:, 2 * PAIR :], jnp.where(spare < 2, 1.0, 0.0)
        ).astype(BF16)
        product = jnp.where(own, scaled * exact[rows, :], 0.0)
        shift = -jnp.sum(product, axis=1, keepdims=True)
        coarse = shift.astype(BF16).astype(F32)
        fine = shift - coarse
        extra = jnp.where(spare == 0, coarse, jnp.where(spare == 1, fine, 0.0))
        grad_aug[rows, :] = jnp.where(own, scaled, extra).astype(BF16)

    query_turned[...] = jnp.zeros(query_turned.shape, F32)
    turned = pl.ds(head * DH, DH)

    @pl.loop(0, tiles)
    def attend(index):
        rows = tile_rows(index)
        query_turned[turned, :] = jnp.zeros((DH, TILE), F32)
        start, pairs = tile_pairs(low[index], high[index], tiles)

        @pl.loop(0, pairs)
        def keys(pair):
            others = [start + 2 * pair, start + 2 * pair + 1]
            for side, other in enumerate(others):
                columns = tile_rows(other)
                place = strip_place(index - other, reach)
                raw = dot_nt(key_aug[columns, :], query_aug[rows, :])
                weight = jnp.exp(raw + strip[:, place])
                slope = dot_nt(value_aug[columns, :], grad_aug[rows, :])
                score = weight * slope
                gathered[:, place] += score
                both = pl.ds(side * TILE, TILE)
                weights[both, :] = weight.astype(BF16)
                scores[both, :] = score.astype(BF16)
            key_parts = dot_f32(scores[...], ordered[rows, pl.ds(0, PAIR)])
            value_parts = dot_f32(weights[...], grad_plain[rows, :])
            for side, other in enumerate(others):
                columns = tile_rows(other)
                both = pl.ds(side * TILE, TILE)
                query_turned[turned, :] += dot_f32(key_turned[turned, columns], scores[both, :])
                key_sum[columns, :] += key_parts[side * TILE : (side + 1) * TILE]
                value_sum[columns, :] += value_parts[side * TILE : (side + 1) * TILE]

        held[rows, pl.ds(0, PAIR)] = query_turned[...].T.astype(BF16)

    @pl.loop(0, tiles)
    def keep(index):
        rows = tile_rows(index)
        held[rows, pl.ds(PAIR, PAIR)] = jnp.where(own, key_sum[rows, :], 0.0).astype(BF16)
        held[rows, pl.ds(2 * PAIR, PAIR)] = jnp.where(own, value_sum[rows, :], 0.0).astype(BF16)
        if head == 0:
            outgoing[rows, :] = held[rows, :]
        else:
            held[rows, :] += other_held[rows, :]

    if head == 1:
        put_back(order_col, held, outgoing)
    folded = gathered[...]
    size = TILE // 2
    while size >= 8:
        folded = folded[:size] + pltpu.roll(folded[size:], width - size, 1)
        size //= 2
    slanted[...] = folded


def group_attention(low, high, offsets, order_row, order_col, table, mixed):
    rows = mixed.shape[0]
    smem = pl.BlockSpec(memory_space=pltpu.SMEM)
    vmem = pl.BlockSpec(memory_space=pltpu.VMEM)
    width = table.shape[1]
    return pl.pallas_call(
        attend_kernel,
        out_shape=(
            jax.ShapeDtypeStruct((rows, 3 * PAIR), BF16),
            jax.ShapeDtypeStruct((rows, PAIR), BF16),
            jax.ShapeDtypeStruct((rows, PAIR), F32),
            jax.ShapeDtypeStruct((rows, PAIR), F32),
            jax.ShapeDtypeStruct((2, 8, TILE), F32),
        ),
        in_specs=[smem] * 3 + [vmem] * 4,
        out_specs=(vmem,) * 5,
        scratch_shapes=[
            pltpu.VMEM((2, rows, PAIR), BF16),
            pltpu.VMEM((2, rows, PAIR), BF16),
            pltpu.VMEM((2, rows, PAIR), BF16),
            pltpu.VMEM((2, TILE, width), F32),
            pltpu.VMEM((2, TILE, PAIR), F32),
            pltpu.VMEM((rows, PAIR), BF16),
        ],
        name="attend",
        compiler_params=pltpu.CompilerParams(vmem_limit_bytes=40 << 20),
        cost_estimate=pl.CostEstimate(
            flops=37_000_000_000, bytes_accessed=8_000_000, transcendentals=5_000_000
        ),
    )(low, high, offsets, order_row, order_col, table, mixed)


def group_attention_back(
    head, low, high, offsets, order_row, order_col, table, ordered, exact, inverse, incoming,
    other_held, before=()
):
    rows = ordered.shape[0]
    smem = pl.BlockSpec(memory_space=pltpu.SMEM)
    vmem = pl.BlockSpec(memory_space=pltpu.VMEM)
    width = table.shape[1]
    return pl.pallas_call(
        functools.partial(attend_back_kernel, head),
        out_shape=(
            jax.ShapeDtypeStruct((rows, 3 * PAIR), BF16),
            jax.ShapeDtypeStruct((8, width), F32),
            jax.ShapeDtypeStruct((rows if head == 0 else 16, PAIR), BF16),
        ),
        in_specs=[smem] * 3 + [vmem] * 8 + [pl.BlockSpec(memory_space=pl.ANY)] * len(before),
        out_specs=(vmem,) * 3,
        scratch_shapes=[
            pltpu.VMEM((rows, PAIR), BF16),
            pltpu.VMEM((rows, PAIR), BF16),
            pltpu.VMEM((rows, PAIR), BF16),
            pltpu.VMEM((rows, PAIR), BF16),
            pltpu.VMEM((rows, PAIR), BF16),
            pltpu.VMEM((PAIR, rows), BF16),
            pltpu.VMEM((TILE, width), F32),
            pltpu.VMEM((TILE, width), F32),
            pltpu.VMEM((PAIR, TILE), F32),
            pltpu.VMEM((rows, PAIR), F32),
            pltpu.VMEM((rows, PAIR), F32),
            pltpu.VMEM((rows, 3 * PAIR), BF16),
            pltpu.VMEM((2 * TILE, TILE), BF16),
            pltpu.VMEM((2 * TILE, TILE), BF16),
        ],
        name="attend_back",
        compiler_params=pltpu.CompilerParams(vmem_limit_bytes=50 << 20),
        cost_estimate=pl.CostEstimate(
            flops=20_000_000_000, bytes_accessed=8_000_000, transcendentals=2_500_000
        ),
    )(
        low, high, offsets, order_row, order_col, table, ordered, exact, inverse, incoming,
        other_held, *before,
    )


def sequence_plan(lengths, rows):
    offsets = jnp.cumsum(lengths) - lengths
    ends = offsets + lengths
    starts_at = jnp.arange(rows // TILE, dtype=jnp.int32) * TILE
    seq_first = jnp.sum((starts_at[:, None] >= offsets[None, :]).astype(jnp.int32), axis=1) - 1
    seq_last = (
        jnp.sum((starts_at[:, None] + TILE - 1 >= offsets[None, :]).astype(jnp.int32), axis=1) - 1
    )
    picks = jnp.arange(lengths.shape[0], dtype=jnp.int32)[None, :]
    low = jnp.sum(jnp.where(seq_first[:, None] == picks, offsets[None, :], 0), axis=1) // TILE
    high = jnp.sum(jnp.where(seq_last[:, None] == picks, ends[None, :], 0), axis=1)
    return (low, (high + TILE - 1) // TILE, offsets)


def bias_tables(rel_buckets, bias_pair):
    table_len = rel_buckets.shape[0]
    reach = (table_len + 1) // 2 // TILE
    width = (2 * reach + 1) * TILE
    hot = (rel_buckets[None, :] == jnp.arange(NB, dtype=jnp.int32)[:, None]).astype(BF16)
    table = dot_tn(bias_pair, hot)
    pad = ((0, 0), (0, width - table_len))
    return (jnp.pad(table, pad), jnp.pad(table[:, ::-1], pad))


def bucket_sums(rel_buckets, slanted):
    table_len = rel_buckets.shape[0]
    width = slanted.shape[2]
    total = jnp.zeros((2, table_len), F32)
    for row in range(8):
        total = total + slanted[:, row, row + 1 : row + 1 + table_len]
    hot = (rel_buckets[::-1][:, None] == jnp.arange(NB, dtype=jnp.int32)[None, :]).astype(F32)
    return jnp.dot(total, hot, precision=lax.Precision.HIGHEST, preferred_element_type=F32)


def blank_arrays(shapes):
    def leave(*refs):
        pass

    return pl.pallas_call(
        leave,
        out_shape=tuple(jax.ShapeDtypeStruct(shape, F32) for shape in shapes),
        out_specs=tuple(pl.BlockSpec(memory_space=pl.ANY) for shape in shapes),
        name="blank",
    )()


def bands_of(width):
    return [slice(band * BAND, (band + 1) * BAND) for band in range(width // BAND)]


def pick_kernel(plan, outs, chunks, *refs):
    picked = refs[len(refs) - outs :]
    for flow, start, source, count in plan:
        if source is None:
            picked[flow][pl.ds(start, count), :] = jnp.zeros((count, BAND), BF16)
            continue
        part = refs[source]
        rows = part.shape[0]
        for band, columns in enumerate(bands_of(part.shape[1])):
            picked[flow][pl.ds(start + band * rows, rows), :] = part[:, columns]


def spread_kernel(starts, chunks, message, *refs):
    parts = len(starts)
    results, wide, sems = (refs[parts : 2 * parts], refs[2 * parts : 3 * parts], refs[3 * parts])
    copies = []
    for index, start in enumerate(starts):
        rows = wide[index].shape[0]
        place = pl.ds(pl.multiple_of(chunks[index] * rows, rows), rows)
        for band, columns in enumerate(bands_of(wide[index].shape[1])):
            wide[index][:, columns] = message[pl.ds(start + band * rows, rows), :].astype(F32)
            copy = pltpu.make_async_copy(
                wide[index].at[:, columns],
                results[index].at[place, columns],
                sems.at[len(copies)],
            )
            copy.start()
            copies.append(copy)
    for copy in copies:
        copy.wait()


def whole_spec(shape):
    return pl.BlockSpec(shape, lambda step, chunk: (0,) * len(shape))


def row_spec(rows, width, place):
    return pl.BlockSpec((rows, width), lambda step, chunk: (chunk[place], 0))


def pick_chunks(plan, rows, chunks, sources):
    shapes = tuple(jax.ShapeDtypeStruct((count, BAND), BF16) for count in rows)
    return pl.pallas_call(
        functools.partial(pick_kernel, plan, len(rows)),
        grid_spec=pltpu.PrefetchScalarGridSpec(
            num_scalar_prefetch=1,
            grid=(1,),
            in_specs=[
                row_spec(count, array_in.shape[1], place)
                for place, (array_in, count) in enumerate(sources)
            ],
            out_specs=tuple(whole_spec(shape.shape) for shape in shapes),
        ),
        out_shape=shapes,
        name="pick",
        cost_estimate=pl.CostEstimate(
            flops=0, bytes_accessed=4 * sum(rows) * BAND, transcendentals=0
        ),
    )(chunks, *[array_in for array_in, count in sources])


def spread_chunks(starts, chunks, message, counts, results):
    kept = [pl.BlockSpec(memory_space=pl.ANY)] * len(results)
    shapes = [(count, result.shape[1]) for count, result in zip(counts, results)]
    copies = sum(width // BAND for count, width in shapes)
    return pl.pallas_call(
        functools.partial(spread_kernel, starts),
        in_specs=[
            pl.BlockSpec(memory_space=pltpu.SMEM),
            pl.BlockSpec(memory_space=pltpu.VMEM),
        ]
        + kept,
        out_specs=tuple(kept),
        out_shape=tuple(jax.ShapeDtypeStruct(result.shape, F32) for result in results),
        scratch_shapes=[pltpu.VMEM(shape, F32) for shape in shapes]
        + [pltpu.SemaphoreType.DMA((copies,))],
        input_output_aliases={2 + item: item for item in range(len(results))},
        name="spread",
        cost_estimate=pl.CostEstimate(
            flops=0, bytes_accessed=6 * message.size, transcendentals=0
        ),
    )(chunks, message, *results)


def heads_kernel(chunk, message, *refs):
    for item, result in enumerate(refs[-3:]):
        result[...] = message[:, item * PAIR : (item + 1) * PAIR].astype(F32)


def spread_heads(chip, message, results):
    rows, parts = message.shape[0], len(RING)
    shape = jax.ShapeDtypeStruct((rows, parts * PAIR), F32)
    spec = pl.BlockSpec((rows, PAIR), lambda step, chunk: (0, chunk[0]))
    return pl.pallas_call(
        heads_kernel,
        grid_spec=pltpu.PrefetchScalarGridSpec(
            num_scalar_prefetch=1,
            grid=(1,),
            in_specs=[whole_spec(message.shape)]
            + [pl.BlockSpec(memory_space=pl.ANY)] * len(results),
            out_specs=(spec,) * 3,
        ),
        out_shape=(shape,) * 3,
        input_output_aliases={2 + item: item for item in range(len(results))},
        name="spread_heads",
        cost_estimate=pl.CostEstimate(flops=0, bytes_accessed=6 * message.size, transcendentals=0),
    )(chip.reshape(1), message, *results)


def tie(*values):
    return lax.optimization_barrier(values)


def ring_pairs(way):
    count = len(RING)
    return [(RING[i], RING[(i + way) % count]) for i in range(count)]


def ring_place():
    return look_up([RING.index(c) for c in range(len(RING))], lax.axis_index("ctx"))


def ring_chip(place):
    return look_up(RING, jnp.mod(place, len(RING)))


def tiny_gather(values):
    sent = jnp.broadcast_to(values[None], (len(RING),) + values.shape)
    return lax.all_to_all(sent, "ctx", 0, 0, tiled=True)


class RingSum:
    def __init__(self, ahead, back, results, widths):
        self.flows = [(ahead, 1), (back, -1)]
        self.widths = widths
        self.me = ring_place()
        self.round = 0
        self.results = tuple(results)
        self.arrived = [None, None]
        self.ready = [None, None]
        self.arrays = {}
        self.last = 2 * (len(RING) - 1)
        self.rounds = self.last

    @property
    def done(self):
        return self.round == self.rounds

    def part_rows(self, part):
        return part[1] * (self.widths[part[3]] // BAND)

    def layout(self, parts, round_at):
        start, starts = (0, {})
        for index, part in enumerate(parts):
            if 0 <= round_at < self.last and (round_at > 0 or not part[4]):
                starts[index] = start
                start += self.part_rows(part)
        return (starts, start)

    def chunk(self, part, way, hops):
        return jnp.mod(self.me - way * hops, len(RING)) + part[2]

    def pick(self, round_at):
        self.picked = None
        plan, sources, chunks, message_rows = ([], [], [], [])
        for flow, (parts, way) in enumerate(self.flows):
            starts, rows = self.layout(parts, round_at)
            message_rows.append(rows)
            for index, start in starts.items():
                part = parts[index]
                hops = round_at
                if hops < len(RING):
                    plan.append((flow, start, len(sources), self.part_rows(part)))
                    sources.append((self.arrays[part[3]], part[1]))
                    chunks.append(self.chunk(part, way, hops))
                else:
                    plan.append((flow, start, None, self.part_rows(part)))
        if sources:
            self.picked = pick_chunks(tuple(plan), message_rows, jnp.stack(chunks), sources)

    def send_apart(self):
        plan, sources, chunks, message_rows = ([], [], [], [])
        for flow, (parts, way) in enumerate(self.flows):
            rows = 0
            for part in parts:
                if part[4]:
                    plan.append((flow, rows, len(sources), self.part_rows(part)))
                    sources.append((self.arrays[part[3]], part[1]))
                    chunks.append(self.chunk(part, way, 0))
                    rows += self.part_rows(part)
            message_rows.append(rows)
        messages = pick_chunks(tuple(plan), message_rows, jnp.stack(chunks), sources)
        self.apart = [
            lax.ppermute(message, "ctx", ring_pairs(way))
            for message, (parts, way) in zip(messages, self.flows)
        ]

    def make(self):
        self.ready = []
        for flow, (parts, way) in enumerate(self.flows):
            got = self.arrived[flow]
            if self.round == 0:
                self.ready.append(self.picked[flow])
                continue
            starts, rows = self.layout(parts, self.round)
            before, rows_before = self.layout(parts, self.round - 1)
            kept = [index for index in starts if index in before]
            if kept != list(before):
                got = jnp.concatenate(
                    [got[before[index] : before[index] + self.part_rows(parts[index])] for index in kept]
                )
            if self.picked is not None:
                picked = self.picked[flow]
                same = got.shape[0]
                added = (got.astype(F32) + picked[:same].astype(F32)).astype(BF16)
                if same < rows:
                    apart = self.apart[flow].astype(F32) + picked[same:].astype(F32)
                    added = jnp.concatenate([added, apart.astype(BF16)])
                got = added
            self.ready.append(got)

    def send(self):
        if self.done:
            return
        self.arrived = [
            lax.ppermute(held, "ctx", ring_pairs(way))
            for held, (parts, way) in zip(self.ready, self.flows)
        ]

    def absorb(self):
        if self.done:
            return
        self.round += 1
        self.landed = list(self.arrived)
        if not self.done:
            self.make()

    def prepare(self):
        if self.round + 1 < self.rounds:
            self.pick(self.round + 1)

    def place(self):
        results = list(self.results)
        for flow, (parts, way) in enumerate(self.flows):
            sent_starts, rows = self.layout(parts, self.round)
            came_starts, rows = self.layout(parts, self.round - 1)
            for starts, message, ends in (
                (sent_starts, self.ready[flow], False),
                (came_starts, self.landed[flow], True),
            ):
                picked, ids, counts, chunks = ([], [], [], [])
                for index, start in starts.items():
                    part = parts[index]
                    hops = self.round
                    if hops < len(RING) - 1 or ends != (hops == self.last):
                        continue
                    picked.append(start)
                    ids.append(part[3])
                    counts.append(part[1])
                    chunks.append(self.chunk(part, way, hops))
                if picked:
                    written = spread_chunks(
                        tuple(picked),
                        jnp.stack(chunks),
                        message,
                        counts,
                        [results[item] for item in ids],
                    )
                    for item, result in zip(ids, written):
                        results[item] = result
        self.results = tuple(results)


class RingGather:
    def __init__(self, block):
        self.me = ring_place()
        self.step = 0
        self.ready = (block, block)
        self.arrived = None
        self.results = ()
        self.arrays = ()
        self.landed = ()
        self.found = [(lax.axis_index("ctx"), block)]

    def send(self):
        if self.step == len(RING) // 2:
            return
        self.step += 1
        ahead, back = self.ready
        if self.step == len(RING) // 2:
            rows = ahead.shape[0] // 2
            ahead, back = (ahead[:rows], back[rows:])
        self.arrived = (
            lax.ppermute(ahead, "ctx", ring_pairs(1)),
            lax.ppermute(back, "ctx", ring_pairs(-1)),
        )

    def place(self):
        pass

    def prepare(self):
        pass

    def absorb(self):
        if len(self.found) == len(RING):
            return
        self.ready = self.arrived
        ahead, back = self.arrived
        if self.step < len(RING) // 2:
            self.found.append((ring_chip(self.me - self.step), ahead))
            self.found.append((ring_chip(self.me + self.step), back))
        else:
            self.found.append((ring_chip(self.me - self.step), jnp.concatenate([ahead, back])))


class HeadRing(RingGather):
    def __init__(self, block, results):
        super().__init__(block)
        self.results = results
        self.placed = 0

    def place(self):
        for chip, block in self.found[self.placed :]:
            self.results = spread_heads(chip, block, self.results)
        self.placed = len(self.found)


def stage(values, *rings):
    values, arrived = tie(values, [(ring.arrived, ring.results, ring.arrays) for ring in rings])
    for ring, blocks in zip(rings, arrived):
        ring.arrived, ring.results, ring.arrays = blocks
        ring.absorb()
    for ring in rings:
        ring.ready = list(ring.ready)
        for way in range(len(ring.ready)):
            values, ring.ready[way] = tie(values, ring.ready[way])
        ring.send()
        ring.prepare()
        ring.place()
    return values


def per_device_ring(
    tokens,
    cotangent,
    token_order,
    seq_lengths,
    rel_buckets,
    gain_attn,
    w_query,
    w_key,
    w_value,
    w_out,
    rel_bias,
    gain_ffn,
    w_gate,
    w_up,
    w_down,
):
    core = lax.axis_index("fsdp")
    ctx = lax.axis_index("ctx")
    tp = lax.axis_index("tp")
    local_rows = tokens.shape[0]
    half = w_query.shape[0]
    head_count = w_query.shape[1] // DH
    group_rows = local_rows * lax.axis_size("ctx")
    first = core == 0

    def halves(array_in):
        left, right = (array_in[:, :half], array_in[:, half:])
        return (jnp.where(first, left, right), jnp.where(first, right, left))

    def whole(own, other):
        return jnp.concatenate(
            [jnp.where(first, own, other), jnp.where(first, other, own)], axis=1
        )

    small = jnp.concatenate([gain_attn, gain_ffn, rel_bias.reshape(-1)])
    small_far = swap(small, "fsdp")
    wq_far, wk_far, wv_far = (swap(w_query, "fsdp"), swap(w_key, "fsdp"), swap(w_value, "fsdp"))
    wo_far = swap(w_out, "fsdp")
    wg_far, wu_far, wd_far = (swap(w_gate, "fsdp"), swap(w_up, "fsdp"), swap(w_down, "fsdp"))
    ga_own, ga_far = (gain_attn.astype(F32), small_far[:half].astype(F32))
    gf_own, gf_far = (gain_ffn.astype(F32), small_far[half : 2 * half].astype(F32))
    bias_far = small_far[2 * half :].reshape(rel_bias.shape)
    bias_local = jnp.where(
        first,
        jnp.concatenate([rel_bias, bias_far]),
        jnp.concatenate([bias_far, rel_bias]),
    )
    tok_own, tok_far = halves(tokens)
    cot_own, cot_far = halves(cotangent)
    tok_own, tok_far = (tok_own.astype(F32), tok_far.astype(F32))

    def norm_scale(own, far):
        total = jnp.sum(own * own, axis=1, keepdims=True) + jnp.sum(far * far, axis=1, keepdims=True)
        return lax.rsqrt(total / (2 * half) + EPS)

    scale_a = norm_scale(tok_own, tok_far)
    normed_own = (tok_own * scale_a * ga_own).astype(BF16)
    normed_far = (tok_far * scale_a * ga_far).astype(BF16)
    queries = (dot_f32(normed_own, w_query) + dot_f32(normed_far, wq_far)).astype(BF16)
    keys_here = (dot_f32(normed_own, w_key) + dot_f32(normed_far, wk_far)).astype(BF16)
    values_here = (dot_f32(normed_own, w_value) + dot_f32(normed_far, wv_far)).astype(BF16)
    parts = lax.axis_size("ctx")

    def by_heads(items):
        mixed = jnp.concatenate([item.reshape(local_rows, parts, 1, PAIR) for item in items], axis=2)
        mixed = jnp.transpose(mixed.reshape(local_rows, parts, len(items) * PAIR), (1, 0, 2))
        moved = lax.all_to_all(mixed, "ctx", 0, 0, tiled=True)
        return moved.reshape(group_rows, len(items) * PAIR)

    def by_rows(array_in):
        count = array_in.shape[1] // PAIR
        moved = lax.all_to_all(
            array_in.reshape(parts, local_rows, count * PAIR), "ctx", 0, 0, tiled=True
        )
        moved = jnp.transpose(moved.reshape(parts, local_rows, count, PAIR), (2, 1, 0, 3))
        return moved.reshape(count, local_rows, parts * PAIR)

    order_row = token_order
    order_col = token_order.reshape(group_rows, 1)
    low, high, offsets = sequence_plan(seq_lengths[0], group_rows)
    bias_pair = lax.dynamic_slice_in_dim(bias_local, ctx * 2, 2, axis=1)
    table, table_back = bias_tables(rel_buckets, bias_pair)
    mixed = by_heads([queries, keys_here, values_here])
    mixed, normed_block = tie(mixed, jnp.concatenate([normed_own, normed_far], axis=1))
    normed_ring = RingGather(normed_block)
    normed_ring.send()
    ordered, context_heads, exact, inverse, tops = group_attention(
        low, high, offsets, order_row, order_col, table, mixed
    )
    context_heads, normed_ring.arrived = tie(context_heads, normed_ring.arrived)
    normed_ring.absorb()
    context = by_rows(context_heads)[0]
    context, normed_ring.ready = tie(context, normed_ring.ready)
    normed_ring.send()

    def tp_sum(own, far):
        own, far = (own.astype(BF16), far.astype(BF16))
        return (
            own.astype(F32) + swap(own, "tp").astype(F32),
            far.astype(F32) + swap(far, "tp").astype(F32),
        )

    attn_parts = [dot_f32(context, w_out).astype(BF16), dot_f32(context, wo_far).astype(BF16)]
    attn_parts, cot_own, cot_far = tie(attn_parts, cot_own, cot_far)
    attn_own, attn_far = tp_sum(*attn_parts)
    hid_own, hid_far = (tok_own + attn_own, tok_far + attn_far)
    inner_grad = dot_nt(cot_own, w_down) + dot_nt(cot_far, wd_far)
    scale_f = norm_scale(hid_own, hid_far)
    nffn_own = (hid_own * scale_f * gf_own).astype(BF16)
    nffn_far = (hid_far * scale_f * gf_far).astype(BF16)
    nffn_own, nffn_far, normed_ring.arrived = tie(nffn_own, nffn_far, normed_ring.arrived)
    normed_ring.absorb()
    block_rows = local_rows // 2
    near, far = (slice(0, block_rows), slice(block_rows, local_rows))

    def both_ways(rows):
        ahead, back = normed_ring.ready
        return (
            lax.ppermute(ahead[rows], "ctx", ring_pairs(1)),
            lax.ppermute(back[rows], "ctx", ring_pairs(-1)),
        )

    third_near, third_far = (both_ways(near), both_ways(far))
    gate_pre = dot_f32(nffn_own, w_gate) + dot_f32(nffn_far, wg_far)
    up_pre = dot_f32(nffn_own, w_up) + dot_f32(nffn_far, wu_far)
    inner_act = geglu(gate_pre, up_pre).astype(BF16)
    unused, geglu_back = jax.vjp(geglu, gate_pre, up_pre)
    gate_grad, up_grad = geglu_back(inner_grad)
    gate_grad = gate_grad.astype(BF16)
    up_grad = up_grad.astype(BF16)

    gate_grad, up_grad, inner_act, third_near, third_far = tie(
        gate_grad, up_grad, inner_act, third_near, third_far
    )
    last = (
        lax.ppermute(third_near[0], "ctx", ring_pairs(1)),
        lax.ppermute(third_far[1], "ctx", ring_pairs(-1)),
    )

    def pair_rows(own):
        return jnp.concatenate([own, swap(own, "fsdp")])

    def pair_half(own, far):
        return jnp.concatenate([own, swap(far, "fsdp")])

    nffn_pair = pair_half(nffn_own, nffn_far)
    gate_pair, up_pair, act_pair = (pair_rows(gate_grad), pair_rows(up_grad), pair_rows(inner_act))
    cot_pair = pair_half(cot_own, cot_far)
    dnf_parts = [
        (dot_nt(gate_grad, w_gate) + dot_nt(up_grad, w_up)).astype(BF16),
        (dot_nt(gate_grad, wg_far) + dot_nt(up_grad, wu_far)).astype(BF16),
    ]
    dnf_parts, nffn_pair, act_pair = tie(dnf_parts, nffn_pair, act_pair)
    dnf_own, dnf_far = tp_sum(*dnf_parts)
    grad_down = dot_tn(act_pair, cot_pair).astype(BF16)
    grad_gate = dot_tn(nffn_pair, gate_pair).astype(BF16)
    grad_up = dot_tn(nffn_pair, up_pair).astype(BF16)
    parts_round = len(RING)
    grad_rows = grad_gate.shape[0] // parts_round
    down_rows = grad_down.shape[0] // (2 * parts_round)
    out_rows = w_out.shape[0] // (2 * parts_round)
    out_shape = (w_out.shape[0], half)
    blanks = blank_arrays(
        [grad_gate.shape, grad_up.shape, grad_down.shape, out_shape] + [w_query.shape] * 3
    )
    ring = RingSum(
        [
            (None, grad_rows, 0, 0, False),
            (None, down_rows, 0, 2, False),
            (None, out_rows, 0, 3, True),
        ],
        [
            (None, grad_rows, 0, 1, False),
            (None, down_rows, parts_round, 2, False),
            (None, out_rows, parts_round, 3, True),
        ],
        blanks[:4],
        [grad_gate.shape[1], grad_up.shape[1], half, half],
    )
    ring.arrays = {0: grad_gate, 1: grad_up, 2: grad_down}
    ring.pick(0)
    ring.make()
    ring.send()

    def norm_back(own, far, scale, gain_own, gain_far, dy_own, dy_far):
        mean_term = (
            jnp.sum(gain_own * dy_own * own, axis=1, keepdims=True)
            + jnp.sum(gain_far * dy_far * far, axis=1, keepdims=True)
        ) / (2 * half)
        cubed = scale * scale * scale * mean_term
        return (
            scale * (gain_own * dy_own) - own * cubed,
            scale * (gain_far * dy_far) - far * cubed,
            jnp.sum(dy_own * own * scale, axis=0),
            jnp.sum(dy_far * far * scale, axis=0),
        )

    back_own, back_far, dgf_own, dgf_far = norm_back(
        hid_own, hid_far, scale_f, gf_own, gf_far, dnf_own, dnf_far
    )
    hgrad_own = cot_own.astype(F32) + back_own
    hgrad_far = cot_far.astype(F32) + back_far
    ag_own, ag_far = (hgrad_own.astype(BF16), hgrad_far.astype(BF16))
    grad_out = dot_tn(pair_rows(context), pair_half(ag_own, ag_far)).astype(BF16)
    context_grad = dot_nt(ag_own, w_out) + dot_nt(ag_far, wo_far)
    context_grad, ring.ready = tie(context_grad.astype(BF16), ring.ready)
    grad_mixed = by_heads([context_grad])
    ring.arrays[3] = grad_out
    ring.send_apart()
    ring.prepare()
    stage((), ring)
    plan = (low, high, offsets, order_row, order_col, table_back, ordered, exact, inverse)
    first_held, first_slanted, ordered_grad = group_attention_back(
        0, *plan, grad_mixed, jnp.zeros((16, 3 * PAIR), BF16), (*ring.picked, *ring.ready)
    )
    first_held, ordered_grad = stage((first_held, ordered_grad), ring)
    outgoing, second_slanted, unused = group_attention_back(
        1, *plan, ordered_grad, first_held, tuple(ring.ready)
    )
    slanted = jnp.stack([first_slanted, second_slanted])
    outgoing, tops = stage((outgoing, tops), ring)
    found = [(chip * local_rows, block) for chip, block in normed_ring.found]
    for hops, ends in ((-3, (third_near[0], third_far[0])), (3, (third_near[1], third_far[1])), (4, last)):
        start = ring_chip(ring_place() + hops) * local_rows
        found += [(start, ends[0]), (start + block_rows, ends[1])]
    outgoing, blocks = tie(outgoing, [block for start, block in found])
    query_grad, key_grad, value_grad = by_rows(outgoing)
    outgoing_turned = jnp.concatenate(
        [
            lax.dynamic_slice_in_dim(outgoing, start, block.shape[0])
            for start, block in found
        ]
    )
    head_grads = dot_tn(jnp.concatenate(blocks), outgoing_turned)
    head_grads, head_grads_sent = (head_grads[:half], head_grads[half:].astype(BF16))
    head_grads = (head_grads + swap(head_grads_sent, "fsdp").astype(F32)).astype(BF16)
    head_ring = HeadRing(head_grads, blanks[4:])
    head_ring.send()
    head_grads = stage(head_grads, ring)
    head_ring.place()
    dn_parts = (
        dot_nt(query_grad, w_query) + dot_nt(key_grad, w_key) + dot_nt(value_grad, w_value),
        dot_nt(query_grad, wq_far) + dot_nt(key_grad, wk_far) + dot_nt(value_grad, wv_far),
    )
    dn_parts = (dn_parts[0].astype(BF16), dn_parts[1].astype(BF16))
    dn_own, dn_far = tp_sum(*dn_parts)
    dn_own, dn_far, inner_act = stage((dn_own, dn_far, inner_act), ring, head_ring)
    tback_own, tback_far, dga_own, dga_far = norm_back(
        tok_own, tok_far, scale_a, ga_own, ga_far, dn_own, dn_far
    )
    grad_tokens = whole(hgrad_own + tback_own, hgrad_far + tback_far)
    ffn_own, ffn_far = tp_sum(dot_f32(inner_act, w_down), dot_f32(inner_act, wd_far))
    output = whole(hid_own + ffn_own, hid_far + ffn_far).astype(BF16)
    pair_top = jnp.max(tops, axis=(1, 2))
    here = jnp.arange(parts, dtype=jnp.int32)[:, None] == ctx
    pair_bias = bucket_sums(rel_buckets, slanted)
    grad_bias = jnp.transpose(
        jnp.where(here[:, :, None], pair_bias[None], 0.0).reshape(head_count, NB)
    )
    bias_flat = grad_bias.reshape(2, -1)
    small_own = jnp.concatenate(
        [dga_own, dgf_own, jnp.where(first, bias_flat[0], bias_flat[1]), pair_top]
    )
    small_sent = jnp.concatenate(
        [dga_far, dgf_far, jnp.where(first, bias_flat[1], bias_flat[0]), pair_top]
    )
    small_got = swap(small_sent, "fsdp")
    grad_tokens, output, small_own, small_got = stage(
        (grad_tokens, output, small_own, small_got), ring, head_ring
    )
    small_both = jnp.concatenate(
        [small_own[:-2] + small_got[:-2], jnp.maximum(small_own[-2:], small_got[-2:])]
    )
    small_all = tiny_gather(small_both)
    stage((), ring, head_ring)
    head_maxima = small_all[:, -2:].reshape(head_count)
    small_sum = jnp.sum(small_all[:, :-2], axis=0)
    final_gain_a, final_gain_f = (small_sum[:half], small_sum[half : 2 * half])
    final_bias = small_sum[2 * half :].reshape(rel_bias.shape)
    clip_scale = TAU_CLIP / jnp.maximum(head_maxima, TAU_CLIP)
    column_scale = jnp.repeat(jnp.sqrt(clip_scale), DH)
    query_clipped = (w_query.astype(F32) * column_scale[None, :]).astype(BF16)
    key_clipped = (w_key.astype(F32) * column_scale[None, :]).astype(BF16)
    others = (
        grad_tokens,
        output,
        final_gain_a,
        final_gain_f,
        final_bias,
        head_maxima,
        query_clipped,
        key_clipped,
    )
    while not ring.done:
        stage((), ring, head_ring)
        if ring.round == len(RING) + 2:
            others, ring.arrived = tie(others, ring.arrived)
    final_gate, final_up, final_down, final_out = ring.results
    final_query, final_key, final_value = head_ring.results
    (
        grad_tokens,
        output,
        final_gain_a,
        final_gain_f,
        final_bias,
        head_maxima,
        query_clipped,
        key_clipped,
    ) = others
    return (
        output,
        grad_tokens,
        final_gain_a,
        final_query,
        final_key,
        final_value,
        final_out,
        final_bias,
        final_gain_f,
        final_gate,
        final_up,
        final_down,
        head_maxima,
        query_clipped,
        key_clipped,
    )


def pick_program(mesh):
    sizes = dict(mesh.shape)
    if sizes["fsdp"] == 2 and sizes["ctx"] == len(RING) and sizes["tp"] == 2:
        return per_device_ring
    return per_device_generic


def solution(mesh):
    in_specs = (
        P(("fsdp", "ctx"), None),
        P(("fsdp", "ctx"), None),
        P("fsdp", None),
        P("fsdp", None),
        P(),
        P("fsdp"),
        P("fsdp", "tp"),
        P("fsdp", "tp"),
        P("fsdp", "tp"),
        P("tp", "fsdp"),
        P("fsdp", "tp"),
        P("fsdp"),
        P("fsdp", "tp"),
        P("fsdp", "tp"),
        P("tp", "fsdp"),
    )
    out_specs = (
        P(("fsdp", "ctx"), None),
        P(("fsdp", "ctx"), None),
        P("fsdp"),
        P("fsdp", "tp"),
        P("fsdp", "tp"),
        P("fsdp", "tp"),
        P("tp", "fsdp"),
        P("fsdp", "tp"),
        P("fsdp"),
        P("fsdp", "tp"),
        P("fsdp", "tp"),
        P("tp", "fsdp"),
        P("tp"),
        P("fsdp", "tp"),
        P("fsdp", "tp"),
    )
    per_device = pick_program(mesh)
    return jax.shard_map(
        per_device, mesh=mesh, in_specs=in_specs, out_specs=out_specs, check_vma=False
    )
```
